128 devices in a mesh: col: 8 (over z, core), dp: 16 (over x, y).
Axes of the slice: x: 4, y: 4, z: 4, core: 2. Of those that a mesh axis runs over, the one named last changes fastest.
Arguments:
- tokens: bfloat16 [1024, 8192], P('col', 'dp'), may hold values from -6 to 6
- cotangent: bfloat16 [1024, 8192], P('col', 'dp'), may hold values from -0.1796875 to 0.1796875
- gate_weight: bfloat16 [8192, 14336], P('dp', 'col'), may hold values from -0.09375 to 0.09375
- up_weight: bfloat16 [8192, 14336], P('dp', 'col'), may hold values from -0.09375 to 0.09375
- down_weight: bfloat16 [14336, 8192], P('col', 'dp'), may hold values from -0.0625 to 0.0625
- gate_mask: int32 [64, 112], P('dp', 'col'), may hold values 0 or 1
- up_mask: int32 [64, 112], P('dp', 'col'), may hold values 0 or 1
- down_mask: int32 [112, 64], P('col', 'dp'), may hold values 0 or 1
- counts: int32 [8], P('col'), may hold values from 1 to 128, 768 in all
Outputs:
- output: bfloat16 [1024, 8192], P('col', 'dp')
- gate_grad: float32 [8192, 14336], P('dp', 'col')
- up_grad: float32 [8192, 14336], P('dp', 'col')
- down_grad: float32 [14336, 8192], P('col', 'dp')
The draws below stay inside these ranges and needn't reach their ends.
Inputs may be any that keep to these rules, and one draw needn't show every extreme that they name: `counts`: the largest count equals 128.
All inputs are finite; a program needn't handle non-finite values. No bound on the sum of `gate_mask` or of `up_mask` or of `down_mask` or of `counts` on one device may be relied on, other than what follows from the above.
Results may differ from the reference program's by a relative error of at most 0.039.
Values may be sent and summed in bfloat16 or wider, within the bound.
No kernel may reach another device: no remote copies, remote signals or barrier semaphores. Data moves between devices by JAX's collectives and lax.ppermute only.
A program may use at most 128 MiB of HBM per device.

```python
import math
import jax
import jax.numpy as jnp
import numpy as np
from jax import lax

D = 8192
FF = 14336
BLOCK = 128
TOK_DEV = 128
TOKENS = 1024
N_COL = 8
N_DP = 16


def with_ends(values, own_key, least, high):
    dims = values.shape
    spot = [jax.random.randint(jax.random.fold_in(own_key, axis), (), 0, dims[axis]) for axis in range(len(dims))]
    values = values.at[tuple(spot)].set(least)
    longest = dims.index(max(dims))
    spot[longest] = (spot[longest] + 1) % dims[longest]
    return values.at[tuple(spot)].set(high)


def steps_of(rng, dims, pieces, smallest, high):
    def one(axis_at, shards_of):
        steps = jax.random.uniform(jax.random.fold_in(jax.random.fold_in(rng, 6), axis_at), (shards_of,), jnp.float32, smallest / len(pieces), high / len(pieces))
        return jnp.repeat(jnp.exp(steps), dims[axis_at] // shards_of).reshape((-1,) + (1,) * (len(dims) - axis_at - 1))

    gain = one(*pieces[0])
    for cut in pieces[1:]:
        gain = gain * one(*cut)
    return gain


def profile(count, total, most, slope):
    weights = [(1 << 20) // math.isqrt(grade ** slope) + 1 for grade in range(2, count + 1)]
    rest, holding = total - most - (count - 1), [1] * (count - 1)
    while rest > 0:
        movable = [i for i in range(count - 1) if holding[i] < most]
        pool, budget = sum([weights[i] for i in movable]), rest
        for i in movable:
            more = min(most - holding[i], max(1, budget * weights[i] // pool), rest)
            holding[i] = holding[i] + more
            rest = rest - more
    return np.array([most] + holding)


def uneven(stream_key, number_of, total, reach, slope):
    if number_of == 2:
        one = jax.random.randint(stream_key, (), max(1, total - reach), min(reach, total - 1) + 1)
        return jnp.stack([one, total - one])
    tallies = jnp.asarray(profile(number_of, total, reach, slope), jnp.int32)
    couples = (number_of - 1) // 2
    giver, receiver = tallies[1:1 + 2 * couples:2], tallies[2:2 + 2 * couples:2]
    margin = jnp.minimum(giver - 1, reach - receiver)
    passed = jax.random.randint(jax.random.fold_in(stream_key, 1), (couples,), 0, 1 << 20) % (margin + 1)
    tallies = tallies.at[1:1 + 2 * couples:2].set(giver - passed).at[2:2 + 2 * couples:2].set(receiver + passed)
    return tallies[jax.random.permutation(jax.random.fold_in(stream_key, 2), number_of)]


def normal_values(rng, shape, deviation, reach, cuts=(), kind=jnp.bfloat16):
    drawn = jax.random.normal(rng, shape, jnp.float32) * deviation
    if len(cuts) > 0:
        drawn = steps_of(rng, shape, cuts, -0.22, 0.18) * drawn
    return jnp.clip(drawn, min=-reach, max=reach).astype(kind)


def setup_inputs(seed: int = 0) -> dict:
    keys = jax.random.split(jax.random.key(seed), 10)
    return {
        "tokens": normal_values(keys[0], (TOKENS, D), 1.0, 6.0, ((0, 8), (1, 16))),
        "cotangent": normal_values(keys[1], (TOKENS, D), 0.03, 0.1796875, ((0, 8), (1, 16))),
        "gate_weight": normal_values(keys[2], (D, FF), (D // 2) ** -0.5, 0.09375, ((0, 16), (1, 8))),
        "up_weight": normal_values(keys[3], (D, FF), (D // 2) ** -0.5, 0.09375, ((0, 16), (1, 8))),
        "down_weight": normal_values(keys[4], (FF, D), (FF // 2) ** -0.5, 0.0625, ((0, 8), (1, 16))),
        "gate_mask": with_ends((jax.random.randint(keys[5], (D // BLOCK, FF // BLOCK), 0, 2) < 1).astype(jnp.int32), jax.random.fold_in(keys[5], 1), 0, 1),
        "up_mask": with_ends((jax.random.randint(keys[6], (D // BLOCK, FF // BLOCK), 0, 2) < 1).astype(jnp.int32), jax.random.fold_in(keys[6], 1), 0, 1),
        "down_mask": with_ends((jax.random.randint(keys[7], (FF // BLOCK, D // BLOCK), 0, 2) < 1).astype(jnp.int32), jax.random.fold_in(keys[7], 1), 0, 1),
        "counts": uneven(keys[8], N_COL, TOK_DEV * N_COL * 3 // 4, TOK_DEV, 2).astype(jnp.int32),
    }


def expand(mask):
    wide = jnp.repeat(jnp.repeat(mask, BLOCK, axis=0), BLOCK, axis=1)
    return wide


def grouped(left, right, groups):
    width = left.shape[1] // groups
    total = jnp.zeros((left.shape[0], right.shape[1]), jnp.float32)
    for index in range(groups):
        piece = jnp.dot(left[:, index * width:(index + 1) * width], right[index * width:(index + 1) * width], preferred_element_type=jnp.float32)
        rounded = lax.optimization_barrier(piece.astype(jnp.bfloat16))
        total = total + rounded.astype(jnp.float32)
    return total


def reference(tokens, cotangent, gate_weight, up_weight, down_weight, gate_mask, up_mask, down_mask, counts):
    slots = jnp.arange(TOKENS, dtype=jnp.int32)
    live = ((slots % TOK_DEV) < jnp.repeat(counts, TOK_DEV))[:, None]
    keep_gate = expand(gate_mask)
    keep_up = expand(up_mask)
    keep_down = expand(down_mask)
    w_gate = jnp.where(keep_gate > 0, gate_weight, jnp.zeros_like(gate_weight))
    w_up = jnp.where(keep_up > 0, up_weight, jnp.zeros_like(up_weight))
    w_down = jnp.where(keep_down > 0, down_weight, jnp.zeros_like(down_weight))
    g_live = jnp.where(live, cotangent, jnp.zeros_like(cotangent))
    gate = grouped(tokens, w_gate, N_DP)
    upward = grouped(tokens, w_up, N_DP)
    sigma = jax.nn.sigmoid(gate)
    active = gate * sigma
    hidden = (active * upward).astype(jnp.bfloat16)
    mixed = grouped(hidden, w_down, N_COL)
    output = jnp.where(live, mixed, jnp.zeros_like(mixed)).astype(jnp.bfloat16)
    back = grouped(g_live, w_down.T, N_DP)
    d_gate = (back * upward * sigma * (1.0 + gate * (1.0 - sigma))).astype(jnp.bfloat16)
    d_up = (back * active).astype(jnp.bfloat16)
    gate_grad = jnp.dot(tokens.T, d_gate, preferred_element_type=jnp.float32)
    up_grad = jnp.dot(tokens.T, d_up, preferred_element_type=jnp.float32)
    down_grad = jnp.dot(hidden.T, g_live, preferred_element_type=jnp.float32)
    gate_grad = jnp.where(keep_gate > 0, gate_grad, jnp.zeros_like(gate_grad))
    up_grad = jnp.where(keep_up > 0, up_grad, jnp.zeros_like(up_grad))
    down_grad = jnp.where(keep_down > 0, down_grad, jnp.zeros_like(down_grad))
    return (output, gate_grad, up_grad, down_grad)
```

```python
import functools

import jax
import jax.numpy as jnp
from jax import lax
from jax.experimental import pallas as pl
from jax.experimental.pallas import tpu as pltpu
from jax.sharding import PartitionSpec as P

BF = jnp.bfloat16
F32 = jnp.float32
LIVE = 768
PAD = 144
SIDE = 4
BLK = 128
UNITS = 1792
HALF = UNITS // 2
STEPS = HALF // BLK
FEAT = 512
SLOTS = 1024

MASKS = {"xA": (1, 0), "xB": (3, 0), "yA": (0, 1), "yB": (0, 3)}
ROUNDS = {
    (0, 0): (("xA", 0), ("xB", 1), ("yA", 2), ("yB", 3)),
    (0, 1): (("xB", 0), ("xA", 1), ("yB", 2), ("yA", 3)),
    (1, 0): (("yA", 2), ("yB", 3), ("xA", 0), ("xB", 1)),
    (1, 1): (("yB", 2), ("yA", 3), ("xB", 0), ("xA", 1)),
}
GROUPS = tuple(ROUNDS)


def partners(name):
    dx, dy = MASKS[name]
    return [
        (x * SIDE + y, (x ^ dx) * SIDE + (y ^ dy)) for x in range(SIDE) for y in range(SIDE)
    ]


def shift(dz, dc):
    return [
        (z * 2 + c, ((z + dz) % SIDE) * 2 + (c + dc) % 2) for z in range(SIDE) for c in range(2)
    ]


def logical_rows():
    place = lax.axis_index("dp")
    x, y = place // SIDE, place % SIDE

    def sides(v):
        high = v // 2
        return (v % 2) ^ high, high

    xa, xb = sides(x)
    ya, yb = sides(y)
    first = xa * 8 + xb * 4 + ya * 2 + yb
    second = xb * 8 + xa * 4 + yb * 2 + ya
    row = lax.iota(jnp.int32, LIVE)
    half, block, rest = row // 384, (row % 384) // 24, row % 24
    return half * 384 + (block ^ jnp.where(half > 0, second, first)) * 24 + rest


def kept(mask_ref, row, col, value):
    return jnp.where(mask_ref[row, col] > 0, value, jnp.zeros_like(value))


def compact_kernel(offs, cnts, rows_ref, all_ref, x_ref, g_ref, xt_ref):
    rows = rows_ref[...]
    slot = lax.broadcasted_iota(jnp.int32, (LIVE, BLK), 1)
    total = None
    for pair in range(4):
        picks = []
        for c in (2 * pair, 2 * pair + 1):
            hit = (rows - offs[c] == slot) & (slot < cnts[c])
            picks.append(jnp.where(hit, 1.0, 0.0).astype(BF))
        pick = jnp.concatenate(picks, axis=1)
        source = jnp.concatenate(
            [all_ref[2 * pair, :BLK, :], all_ref[2 * pair + 1, :BLK, :]], axis=0
        )
        part = jnp.dot(pick, source, preferred_element_type=F32)
        total = part if total is None else total + part
    x_ref[...] = total[:, :FEAT].astype(BF)
    g_ref[...] = total[:, FEAT:].astype(BF)
    xt_ref[...] = total[:, :FEAT].T.astype(BF)


def compact(offs, cnts, rows, gathered):
    smem = pl.BlockSpec(memory_space=pltpu.SMEM)
    vmem = pl.BlockSpec(memory_space=pltpu.VMEM)
    return pl.pallas_call(
        compact_kernel,
        out_shape=(
            jax.ShapeDtypeStruct((LIVE, FEAT), BF),
            jax.ShapeDtypeStruct((LIVE, FEAT), BF),
            jax.ShapeDtypeStruct((FEAT, LIVE), BF),
        ),
        in_specs=[smem, smem, vmem, vmem],
        out_specs=(vmem, vmem, vmem),
        compiler_params=pltpu.CompilerParams(vmem_limit_bytes=48 << 20),
        cost_estimate=pl.CostEstimate(
            flops=2 * LIVE * SLOTS * SLOTS, bytes_accessed=5 << 20, transcendentals=0
        ),
        name="compact",
    )(offs, cnts, rows, gathered)


def masked_columns(mask_ref, ref, col):
    return jnp.concatenate(
        [kept(mask_ref, r, col, ref[r * BLK : (r + 1) * BLK, :]) for r in range(4)], axis=0
    )


def masked_rows(mask_ref, ref, row):
    return jnp.concatenate(
        [kept(mask_ref, row, c, ref[:, c * BLK : (c + 1) * BLK]) for c in range(4)], axis=1
    )


def partial_kernel(
    gm, um, dm, x_ref, g_ref, wga, wgb, wua, wub, wda, wdb, as0, ak0, as1, ak1, bs0, bk0, bs1, bk1
):
    j = pl.program_id(0)
    w_gate = jnp.concatenate(
        [masked_columns(gm, wga, j), masked_columns(gm, wgb, STEPS + j)], axis=1
    )
    w_up = jnp.concatenate(
        [masked_columns(um, wua, j), masked_columns(um, wub, STEPS + j)], axis=1
    )
    w_down = jnp.concatenate([masked_rows(dm, wda, j), masked_rows(dm, wdb, STEPS + j)], axis=0)
    x, g = x_ref[...], g_ref[...]
    results = (
        jnp.dot(x, w_gate, preferred_element_type=F32),
        jnp.dot(x, w_up, preferred_element_type=F32),
        lax.dot_general(g, w_down, (((1,), (1,)), ((), ())), preferred_element_type=F32),
    )
    for which, result in enumerate(results):
        left, right = result[:, :BLK], result[:, BLK:]
        for q, (send, keep) in enumerate(((as0, ak0), (as1, ak1))):
            keep[which] = left[q * 384 : q * 384 + 192].astype(BF)
            send[which] = left[q * 384 + 192 : q * 384 + 384].astype(BF)
        for q, (send, keep) in enumerate(((bs0, bk0), (bs1, bk1))):
            for t in range(4):
                at = q * 384 + t * 96
                keep[which, t] = right[at : at + 48].astype(BF)
                send[which, t] = right[at + 48 : at + 96].astype(BF)


def weight_specs():
    return [
        pl.BlockSpec((FEAT, BLK), lambda j: (0, j)),
        pl.BlockSpec((FEAT, BLK), lambda j: (0, STEPS + j)),
        pl.BlockSpec((FEAT, BLK), lambda j: (0, j)),
        pl.BlockSpec((FEAT, BLK), lambda j: (0, STEPS + j)),
        pl.BlockSpec((BLK, FEAT), lambda j: (j, 0)),
        pl.BlockSpec((BLK, FEAT), lambda j: (STEPS + j, 0)),
    ]


def partials(gm, um, dm, x, g, wg, wu, wd):
    smem = pl.BlockSpec(memory_space=pltpu.SMEM)
    whole = pl.BlockSpec((LIVE, FEAT), lambda j: (0, 0))
    a_spec = pl.BlockSpec((3, 192, BLK), lambda j: (0, 0, j))
    b_spec = pl.BlockSpec((3, 4, 48, BLK), lambda j: (0, 0, 0, j))
    a_out = jax.ShapeDtypeStruct((3, 192, HALF), BF)
    b_out = jax.ShapeDtypeStruct((3, 4, 48, HALF), BF)
    return pl.pallas_call(
        partial_kernel,
        grid=(STEPS,),
        out_shape=(a_out,) * 4 + (b_out,) * 4,
        in_specs=[smem, smem, smem, whole, whole] + weight_specs(),
        out_specs=(a_spec,) * 4 + (b_spec,) * 4,
        compiler_params=pltpu.CompilerParams(vmem_limit_bytes=48 << 20),
        cost_estimate=pl.CostEstimate(
            flops=2 * LIVE * FEAT * 3 * UNITS, bytes_accessed=16 << 20, transcendentals=0
        ),
        name="partials",
    )(gm, um, dm, x, g, wg, wg, wu, wu, wd, wd)


def rows_a(own, far, which):
    return [own[which], far[which]]


def rows_b(own, far, which):
    return [piece for t in range(4) for piece in (own[which, t], far[which, t])]


def output_kernel(
    offs, cnts, dm, rows_ref, a0, a0f, a1, a1f, b0, b0f, b1, b1f, wda, wdb, out_ref, total
):
    j = pl.program_id(0)
    left = jnp.concatenate(rows_a(a0, a0f, 0) + rows_a(a1, a1f, 0), axis=0)
    right = jnp.concatenate(rows_b(b0, b0f, 0) + rows_b(b1, b1f, 0), axis=0)
    hidden = jnp.concatenate([left, right], axis=1)
    w_down = jnp.concatenate([masked_rows(dm, wda, j), masked_rows(dm, wdb, STEPS + j)], axis=0)
    part = jnp.dot(hidden, w_down, preferred_element_type=F32)

    @pl.when(j == 0)
    def _():
        total[...] = part

    @pl.when(j > 0)
    def _():
        total[...] += part

    @pl.when(j == STEPS - 1)
    def _():
        mixed = total[...].astype(BF)
        rows = rows_ref[...]
        slot = lax.broadcasted_iota(jnp.int32, (BLK, LIVE), 0)
        for k in range(8):
            hit = (rows - offs[k] == slot) & (slot < cnts[k])
            pick = jnp.where(hit, 1.0, 0.0).astype(BF)
            out_ref[k // 4, k % 4] = jnp.dot(pick, mixed, preferred_element_type=F32).astype(BF)


def output_rows(offs, cnts, dm, rows, parts, wd):
    smem = pl.BlockSpec(memory_space=pltpu.SMEM)
    a_spec = pl.BlockSpec((1, 192, BLK), lambda j: (0, 0, j))
    b_spec = pl.BlockSpec((1, 4, 48, BLK), lambda j: (0, 0, 0, j))
    return pl.pallas_call(
        output_kernel,
        grid=(STEPS,),
        out_shape=jax.ShapeDtypeStruct((2, 4, BLK, FEAT), BF),
        in_specs=[smem, smem, smem, pl.BlockSpec((1, LIVE), lambda j: (0, 0))]
        + [a_spec] * 4
        + [b_spec] * 4
        + weight_specs()[4:],
        out_specs=pl.BlockSpec((2, 4, BLK, FEAT), lambda j: (0, 0, 0, 0)),
        scratch_shapes=[pltpu.VMEM((LIVE, FEAT), F32)],
        compiler_params=pltpu.CompilerParams(vmem_limit_bytes=48 << 20),
        cost_estimate=pl.CostEstimate(
            flops=2 * LIVE * FEAT * (UNITS + SLOTS), bytes_accessed=6 << 20, transcendentals=0
        ),
        name="output_rows",
    )(offs, cnts, dm, rows, *parts, wd, wd)


def grad_kernel(
    gm, um, dm, xt_ref, g_ref, a0, a0f, a1, a1f, b0, b0f, b1, b1f, gate_out, up_out, down_out
):
    k = pl.program_id(0)

    def work(rows, first, second):
        hidden, d_gate, d_up = [
            jnp.concatenate(rows(*first, which) + rows(*second, which), axis=0)
            for which in range(3)
        ]
        both = jnp.dot(
            xt_ref[...], jnp.concatenate([d_gate, d_up], axis=1), preferred_element_type=F32
        )
        down = lax.dot_general(
            hidden, g_ref[...], (((0,), (0,)), ((), ())), preferred_element_type=F32
        )
        for r in range(4):
            at = slice(r * BLK, (r + 1) * BLK)
            gate_out[at, :] = kept(gm, r, k, both[at, :BLK])
            up_out[at, :] = kept(um, r, k, both[at, BLK:])
            down_out[:, at] = kept(dm, k, r, down[:, at])

    @pl.when(k < STEPS)
    def _():
        work(rows_a, (a0, a0f), (a1, a1f))

    @pl.when(k >= STEPS)
    def _():
        work(rows_b, (b0, b0f), (b1, b1f))


def gradients(gm, um, dm, xt, g, parts):
    smem = pl.BlockSpec(memory_space=pltpu.SMEM)
    a_spec = pl.BlockSpec((3, 192, BLK), lambda k: (0, 0, jnp.minimum(k, STEPS - 1)))
    b_spec = pl.BlockSpec((3, 4, 48, BLK), lambda k: (0, 0, 0, jnp.maximum(k - STEPS, 0)))
    return pl.pallas_call(
        grad_kernel,
        grid=(2 * STEPS,),
        out_shape=(
            jax.ShapeDtypeStruct((FEAT, UNITS), F32),
            jax.ShapeDtypeStruct((FEAT, UNITS), F32),
            jax.ShapeDtypeStruct((UNITS, FEAT), F32),
        ),
        in_specs=[
            smem,
            smem,
            smem,
            pl.BlockSpec((FEAT, LIVE), lambda k: (0, 0)),
            pl.BlockSpec((LIVE, FEAT), lambda k: (0, 0)),
        ]
        + [a_spec] * 4
        + [b_spec] * 4,
        out_specs=(
            pl.BlockSpec((FEAT, BLK), lambda k: (0, k)),
            pl.BlockSpec((FEAT, BLK), lambda k: (0, k)),
            pl.BlockSpec((BLK, FEAT), lambda k: (k, 0)),
        ),
        compiler_params=pltpu.CompilerParams(vmem_limit_bytes=48 << 20),
        cost_estimate=pl.CostEstimate(
            flops=2 * LIVE * FEAT * 3 * UNITS, bytes_accessed=20 << 20, transcendentals=0
        ),
        name="gradients",
    )(gm, um, dm, xt, g, *parts)


def split(value, axis):
    lower = lax.slice_in_dim(value, 0, 1, axis=axis)
    upper = lax.slice_in_dim(value, 1, 2, axis=axis)
    return lower, upper


def activate(total):
    gate, upward, back = total[0], total[1], total[2]
    sigma = jax.nn.sigmoid(gate)
    active = gate * sigma
    hidden = (active * upward).astype(BF)
    d_gate = (back * upward * sigma * (1.0 + gate * (1.0 - sigma))).astype(BF)
    d_up = (back * active).astype(BF)
    return jnp.stack([hidden, d_gate, d_up])


def on_device(
    tokens, cotangent, gate_weight, up_weight, down_weight, gate_mask, up_mask, down_mask, counts
):
    tok_dev = tokens.shape[0]
    live = (lax.iota(jnp.int32, tok_dev) < counts[0])[:, None]
    tail = jnp.full((PAD - tok_dev, 2 * FEAT), counts[0], F32).astype(BF)
    mine = jnp.concatenate([jnp.concatenate([tokens, cotangent], axis=1), tail], axis=0)
    gathered = lax.all_gather(mine, "col", axis=0, tiled=False)
    cnts = gathered[:, tok_dev, 0].astype(jnp.int32)
    offs = jnp.cumsum(cnts) - cnts
    rows = logical_rows()
    x, g, xt = compact(offs, cnts, rows[:, None], gathered)
    as0, ak0, as1, ak1, bs0, bk0, bs1, bk1 = partials(
        gate_mask, up_mask, down_mask, x, g, gate_weight, up_weight, down_weight
    )

    def spread(value, bit):
        sizes = [1 if b == bit else 2 for b in range(4)]
        return value.reshape((3, *sizes, 24, HALF))

    send = {
        (0, 0): spread(as0, 0),
        (0, 1): spread(as1, 0),
        (1, 0): spread(bs0, 2),
        (1, 1): spread(bs1, 2),
    }
    keep = {
        (0, 0): spread(ak0, 0),
        (0, 1): spread(ak1, 0),
        (1, 0): spread(bk0, 2),
        (1, 1): spread(bk1, 2),
    }
    for number in range(4):
        come = {
            s: lax.ppermute(send[s], "dp", partners(ROUNDS[s][number][0])) for s in GROUPS
        }
        for s in GROUPS:
            total = keep[s].astype(F32) + come[s].astype(F32)
            if number < 3:
                lower, upper = split(total, 1 + ROUNDS[s][number + 1][1])
                keep[s], send[s] = lower.astype(BF), upper.astype(BF)
            else:
                keep[s] = activate(total)
    for number in (3, 2, 1, 0):
        come = {
            s: lax.ppermute(keep[s], "dp", partners(ROUNDS[s][number][0])) for s in GROUPS
        }
        if number > 0:
            for s in GROUPS:
                keep[s] = jnp.concatenate([keep[s], come[s]], axis=1 + ROUNDS[s][number][1])
    parts = []
    for s in GROUPS:
        shape = (3, 192, HALF) if s[0] == 0 else (3, 4, 48, HALF)
        parts += [keep[s].reshape(shape), come[s].reshape(shape)]

    place = lax.axis_index("col")
    order = jnp.arange(8)
    owner = ((place // 2 + order % 4) % SIDE) * 2 + ((place % 2) ^ (order // 4))
    expanded = output_rows(offs[owner], cnts[owner], down_mask, rows[None, :], parts, down_weight)
    other = lax.ppermute(expanded[1], "col", shift(0, 1))
    summed = expanded[0].astype(F32) + other.astype(F32)
    near, up, far, down = [summed[k].astype(BF) for k in range(4)]
    mixed = (
        near.astype(F32)
        + lax.ppermute(up, "col", shift(1, 0)).astype(F32)
        + lax.ppermute(down, "col", shift(-1, 0)).astype(F32)
        + lax.ppermute(far, "col", shift(2, 0)).astype(F32)
    )
    output = jnp.where(live, mixed, jnp.zeros_like(mixed)).astype(BF)
    gate_grad, up_grad, down_grad = gradients(gate_mask, up_mask, down_mask, xt, g, parts)
    return (output, gate_grad, up_grad, down_grad)


def solution(mesh):
    in_specs = (
        P("col", "dp"),
        P("col", "dp"),
        P("dp", "col"),
        P("dp", "col"),
        P("col", "dp"),
        P("dp", "col"),
        P("dp", "col"),
        P("col", "dp"),
        P("col"),
    )
    out_specs = (P("col", "dp"), P("dp", "col"), P("dp", "col"), P("col", "dp"))
    return jax.shard_map(
        on_device, mesh=mesh, in_specs=in_specs, out_specs=out_specs, check_vma=False
    )
```

```python
import functools

import jax
import jax.numpy as jnp
from jax import lax
from jax.experimental import pallas as pl
from jax.experimental.pallas import tpu as pltpu
from jax.sharding import PartitionSpec as P

BF = jnp.bfloat16
F32 = jnp.float32
LIVE = 768
PAD = 144
SIDE = 4
BLK = 128
PAIR = 2 * BLK
UNITS = 1792
HALF = UNITS // 2
STEPS = UNITS // PAIR
FEAT = 512
SLOTS = 1024
CUT = 96
FIRST = 576
LAST = LIVE - FIRST
VMEM = 48 << 20

MASKS = {"xA": (1, 0), "xB": (3, 0), "yA": (0, 1), "yB": (0, 3)}
ROUNDS = {
    (0, 0): (("xA", 0), ("xB", 1), ("yA", 2), ("yB", 3)),
    (0, 1): (("xB", 1), ("xA", 0), ("yB", 3), ("yA", 2)),
    (1, 0): (("yA", 0), ("yB", 1), ("xA", 2), ("xB", 3)),
    (1, 1): (("yB", 1), ("yA", 0), ("xB", 3), ("xA", 2)),
}
GROUPS = tuple(ROUNDS)


def partners(name):
    dx, dy = MASKS[name]
    return [
        (x * SIDE + y, (x ^ dx) * SIDE + (y ^ dy)) for x in range(SIDE) for y in range(SIDE)
    ]


def shift(dz, dc):
    return [
        (z * 2 + c, ((z + dz) % SIDE) * 2 + (c + dc) % 2) for z in range(SIDE) for c in range(2)
    ]


def logical_rows():
    place = lax.axis_index("dp")
    x, y = place // SIDE, place % SIDE

    def sides(v):
        high = v // 2
        return (v % 2) ^ high, high

    xa, xb = sides(x)
    ya, yb = sides(y)
    first = xa * 8 + xb * 4 + ya * 2 + yb
    second = ya * 8 + yb * 4 + xa * 2 + xb
    row = lax.iota(jnp.int32, LIVE)
    early = row < FIRST
    half = jnp.where(early, row // 288, (row - FIRST) // CUT)
    piece = jnp.where(early, (row % 288) // CUT, 3)
    block, rest = piece * 4 + (row % CUT) // 24, row % 24
    return half * 384 + (block ^ jnp.where(half > 0, second, first)) * 24 + rest


def kept(mask_ref, row, col, value):
    return jnp.where(mask_ref[row, col] > 0, value, jnp.zeros_like(value))


def smem():
    return pl.BlockSpec(memory_space=pltpu.SMEM)


def whole(shape):
    return pl.BlockSpec(shape, lambda j: (0,) * len(shape))


def call(kernel, name, flops, moved, **rest):
    return pl.pallas_call(
        kernel,
        compiler_params=pltpu.CompilerParams(vmem_limit_bytes=VMEM),
        cost_estimate=pl.CostEstimate(flops=flops, bytes_accessed=moved, transcendentals=0),
        name=name,
        **rest,
    )


def pack_kernel(tok_ref, cot_ref, count_ref, out_ref):
    out_ref[:BLK, :FEAT] = tok_ref[...]
    out_ref[:BLK, FEAT:] = cot_ref[...]
    count = jnp.full((PAD - BLK, 2 * FEAT), count_ref[0], jnp.int32)
    out_ref[BLK:, :] = count.astype(F32).astype(BF)


def pack(tokens, cotangent, counts):
    vmem = pl.BlockSpec(memory_space=pltpu.VMEM)
    return call(
        pack_kernel,
        "pack",
        0,
        1 << 19,
        out_shape=jax.ShapeDtypeStruct((PAD, 2 * FEAT), BF),
        in_specs=[vmem, vmem, smem()],
        out_specs=vmem,
    )(tokens, cotangent, counts)


def prepare_kernel(gm, um, dm, wg, wu, wd, wx_ref, wdt_ref, wd_ref):
    j = pl.program_id(0)
    for which, (mask, ref) in enumerate(((gm, wg), (um, wu))):
        for r in range(4):
            for b in range(2):
                at = slice(r * BLK, (r + 1) * BLK)
                wx_ref[0, at, which * PAIR + b * BLK : which * PAIR + (b + 1) * BLK] = kept(
                    mask, r, 2 * j + b, ref[at, b * BLK : (b + 1) * BLK]
                )
    down = jnp.concatenate(
        [
            jnp.concatenate(
                [
                    kept(dm, 2 * j + b, c, wd[b * BLK : (b + 1) * BLK, c * BLK : (c + 1) * BLK])
                    for c in range(4)
                ],
                axis=1,
            )
            for b in range(2)
        ],
        axis=0,
    )
    wd_ref[...] = down
    wdt_ref[0] = down.T


def prepare(gm, um, dm, wg, wu, wd):
    return call(
        prepare_kernel,
        "prepare",
        0,
        13 << 20,
        grid=(STEPS,),
        out_shape=(
            jax.ShapeDtypeStruct((STEPS, FEAT, 2 * PAIR), BF),
            jax.ShapeDtypeStruct((STEPS, FEAT, PAIR), BF),
            jax.ShapeDtypeStruct((UNITS, FEAT), BF),
        ),
        in_specs=[
            smem(),
            smem(),
            smem(),
            pl.BlockSpec((FEAT, PAIR), lambda j: (0, j)),
            pl.BlockSpec((FEAT, PAIR), lambda j: (0, j)),
            pl.BlockSpec((PAIR, FEAT), lambda j: (j, 0)),
        ],
        out_specs=(
            pl.BlockSpec((1, FEAT, 2 * PAIR), lambda j: (j, 0, 0)),
            pl.BlockSpec((1, FEAT, PAIR), lambda j: (j, 0, 0)),
            pl.BlockSpec((PAIR, FEAT), lambda j: (j, 0)),
        ),
    )(gm, um, dm, wg, wu, wd)


def compact_kernel(shard, rows_ref, *refs):
    sources, (x_ref, g_ref, xt_first, xt_last, offs_ref, cnts_ref) = refs[:8], refs[8:]
    rows = rows_ref[...]
    slot = lax.broadcasted_iota(jnp.int32, (LIVE, BLK), 1)
    cnts = [ref[BLK : BLK + 1, 0:1].astype(F32).astype(jnp.int32) for ref in sources]
    total = None
    for pair in range(4):
        picks = []
        for k in (2 * pair, 2 * pair + 1):
            offset = jnp.zeros((1, 1), jnp.int32)
            for other in range(8):
                if other != k:
                    offset += jnp.where(shard[other] < shard[k], cnts[other], 0)
            offs_ref[k] = jnp.broadcast_to(offset, (8, BLK))
            cnts_ref[k] = jnp.broadcast_to(cnts[k], (8, BLK))
            hit = (rows - offset == slot) & (slot < cnts[k])
            picks.append(jnp.where(hit, 1.0, 0.0).astype(BF))
        source = jnp.concatenate(
            [sources[2 * pair][:BLK, :], sources[2 * pair + 1][:BLK, :]], axis=0
        )
        part = jnp.dot(jnp.concatenate(picks, axis=1), source, preferred_element_type=F32)
        total = part if total is None else total + part
    x_ref[...] = total[:, :FEAT].astype(BF)
    g_ref[...] = total[:, FEAT:].astype(BF)
    xt_first[...] = total[:FIRST, :FEAT].T.astype(BF)
    xt_last[...] = total[FIRST:, :FEAT].T.astype(BF)


def compact(shard, rows, sources):
    vmem = pl.BlockSpec(memory_space=pltpu.VMEM)
    return call(
        compact_kernel,
        "compact",
        2 * LIVE * SLOTS * SLOTS,
        5 << 20,
        out_shape=(
            jax.ShapeDtypeStruct((LIVE, FEAT), BF),
            jax.ShapeDtypeStruct((LIVE, FEAT), BF),
            jax.ShapeDtypeStruct((FEAT, FIRST), BF),
            jax.ShapeDtypeStruct((FEAT, LAST), BF),
            jax.ShapeDtypeStruct((8, 8, BLK), jnp.int32),
            jax.ShapeDtypeStruct((8, 8, BLK), jnp.int32),
        ),
        in_specs=[smem(), vmem] + [vmem] * 8,
        out_specs=(vmem,) * 6,
    )(shard, rows, *sources)


def partial_kernel(start, pieces, x_ref, g_ref, wx_ref, wdt_ref, *outs):
    count = 2 * pieces * CUT
    x, g = x_ref[start : start + count, :], g_ref[start : start + count, :]
    both = jnp.dot(x, wx_ref[0], preferred_element_type=F32)
    back = jnp.dot(g, wdt_ref[0], preferred_element_type=F32)
    for which, result in enumerate((both[:, :PAIR], both[:, PAIR:], back)):
        result = result.astype(BF)
        for h in range(2):
            for piece in range(pieces):
                at = (h * pieces + piece) * CUT
                for q in range(2):
                    outs[(piece * 2 + h) * 2 + q][which] = result[
                        at : at + CUT, q * BLK : (q + 1) * BLK
                    ]


def partials(start, pieces, x, g, wx, wdt):
    count = 2 * pieces * CUT
    return call(
        functools.partial(partial_kernel, start, pieces),
        "partials",
        2 * count * FEAT * 3 * UNITS,
        7 << 20,
        grid=(STEPS,),
        out_shape=(jax.ShapeDtypeStruct((3, CUT, HALF), BF),) * (4 * pieces),
        in_specs=[
            whole((LIVE, FEAT)),
            whole((LIVE, FEAT)),
            pl.BlockSpec((1, FEAT, 2 * PAIR), lambda j: (j, 0, 0)),
            pl.BlockSpec((1, FEAT, PAIR), lambda j: (j, 0, 0)),
        ],
        out_specs=(pl.BlockSpec((3, CUT, BLK), lambda j: (0, 0, j)),) * (4 * pieces),
    )(x, g, wx, wdt)


def stacked(refs, which, pieces):
    return jnp.concatenate(
        [
            jnp.concatenate([refs[(p * 2 + h) * 2 + q][which] for q in range(2)], axis=1)
            for h in range(2)
            for p in pieces
        ],
        axis=0,
    )


def picked(rows, offs, cnts, k, slot):
    hit = (rows - offs[k, 0:1, 0:1] == slot) & (slot < cnts[k, 0:1, 0:1])
    return jnp.where(hit, 1.0, 0.0).astype(BF)


def first_output_kernel(rows_ref, offs, cnts, wd_ref, *refs):
    parts, (out_ref, total) = refs[:12], refs[12:]
    j = pl.program_id(0)
    part = jnp.dot(stacked(parts, 0, range(3)), wd_ref[...], preferred_element_type=F32)

    @pl.when(j == 0)
    def _():
        total[...] = part

    @pl.when(j > 0)
    def _():
        total[...] += part

    @pl.when(j == STEPS - 1)
    def _():
        mixed = total[...].astype(BF)
        rows = rows_ref[0:1, :]
        slot = lax.broadcasted_iota(jnp.int32, (BLK, FIRST), 0)
        for k in range(8):
            pick = picked(rows, offs, cnts, k, slot)
            out_ref[k] = jnp.dot(pick, mixed, preferred_element_type=F32).astype(BF)


def first_output(rows, offs, cnts, wd, parts):
    return call(
        first_output_kernel,
        "first_output",
        2 * FIRST * FEAT * (UNITS + SLOTS),
        5 << 20,
        grid=(STEPS,),
        out_shape=jax.ShapeDtypeStruct((8, BLK, FEAT), BF),
        in_specs=[whole((1, FIRST)), whole((8, 8, BLK)), whole((8, 8, BLK))]
        + [pl.BlockSpec((PAIR, FEAT), lambda j: (j, 0))]
        + [pl.BlockSpec((1, CUT, BLK), lambda j: (0, 0, j))] * 12,
        out_specs=whole((8, BLK, FEAT)),
        scratch_shapes=[pltpu.VMEM((FIRST, FEAT), F32)],
    )(rows, offs, cnts, wd, *parts)


def last_output_kernel(rows_ref, offs, cnts, early_ref, wd_ref, *refs):
    parts, (near_ref, away_ref) = refs[:4], refs[4:]
    mixed = None
    for j in range(STEPS):
        hidden = jnp.concatenate(
            [
                jnp.concatenate(
                    [parts[h * 2 + q][0, :, j * BLK : (j + 1) * BLK] for q in range(2)], axis=1
                )
                for h in range(2)
            ],
            axis=0,
        )
        part = jnp.dot(
            hidden, wd_ref[j * PAIR : (j + 1) * PAIR, :], preferred_element_type=F32
        )
        mixed = part if mixed is None else mixed + part
    mixed = mixed.astype(BF)
    rows = rows_ref[0:1, :]
    slot = lax.broadcasted_iota(jnp.int32, (BLK, LAST), 0)
    for k in range(8):
        pick = picked(rows, offs, cnts, k, slot)
        late = jnp.dot(pick, mixed, preferred_element_type=F32)
        target = near_ref if k < 4 else away_ref
        target[k % 4] = (early_ref[k].astype(F32) + late).astype(BF)


def last_output(rows, offs, cnts, early, wd, parts):
    return call(
        last_output_kernel,
        "last_output",
        2 * LAST * FEAT * (UNITS + SLOTS),
        5 << 20,
        grid=(1,),
        out_shape=(jax.ShapeDtypeStruct((4, BLK, FEAT), BF),) * 2,
        in_specs=[
            whole((1, LAST)),
            whole((8, 8, BLK)),
            whole((8, 8, BLK)),
            whole((8, BLK, FEAT)),
            whole((UNITS, FEAT)),
        ]
        + [whole((1, CUT, HALF))] * 4,
        out_specs=(whole((4, BLK, FEAT)),) * 2,
    )(rows, offs, cnts, early, wd, *parts)


def grad_kernel(gm, um, dm, xt_first, xt_last, g_ref, *refs):
    parts, (gate_out, up_out, down_out) = refs[:16], refs[16:]
    j = pl.program_id(0)

    def side(which):
        return stacked(parts, which, range(3)), stacked(parts, which, (3,))

    (hidden, hidden_l), (d_gate, d_gate_l), (d_up, d_up_l) = [side(which) for which in range(3)]
    xt, xt_l = xt_first[...], xt_last[...]
    gate = jnp.dot(xt, d_gate, preferred_element_type=F32) + jnp.dot(
        xt_l, d_gate_l, preferred_element_type=F32
    )
    up = jnp.dot(xt, d_up, preferred_element_type=F32) + jnp.dot(
        xt_l, d_up_l, preferred_element_type=F32
    )
    down = lax.dot_general(
        jnp.concatenate([hidden, hidden_l], axis=0),
        g_ref[...],
        (((0,), (0,)), ((), ())),
        preferred_element_type=F32,
    )
    for r in range(4):
        for b in range(2):
            at, by = slice(r * BLK, (r + 1) * BLK), slice(b * BLK, (b + 1) * BLK)
            gate_out[at, by] = kept(gm, r, 2 * j + b, gate[at, by])
            up_out[at, by] = kept(um, r, 2 * j + b, up[at, by])
            down_out[by, at] = kept(dm, 2 * j + b, r, down[by, at])


def gradients(gm, um, dm, xt_first, xt_last, g, parts):
    return call(
        grad_kernel,
        "gradients",
        2 * LIVE * FEAT * 3 * UNITS,
        20 << 20,
        grid=(STEPS,),
        out_shape=(
            jax.ShapeDtypeStruct((FEAT, UNITS), F32),
            jax.ShapeDtypeStruct((FEAT, UNITS), F32),
            jax.ShapeDtypeStruct((UNITS, FEAT), F32),
        ),
        in_specs=[
            smem(),
            smem(),
            smem(),
            whole((FEAT, FIRST)),
            whole((FEAT, LAST)),
            whole((LIVE, FEAT)),
        ]
        + [pl.BlockSpec((3, CUT, BLK), lambda j: (0, 0, j))] * 16,
        out_specs=(
            pl.BlockSpec((FEAT, PAIR), lambda j: (0, j)),
            pl.BlockSpec((FEAT, PAIR), lambda j: (0, j)),
            pl.BlockSpec((PAIR, FEAT), lambda j: (j, 0)),
        ),
    )(gm, um, dm, xt_first, xt_last, g, *parts)


def split(value, axis):
    lower = lax.slice_in_dim(value, 0, 1, axis=axis)
    upper = lax.slice_in_dim(value, 1, 2, axis=axis)
    return lower, upper


def activate(total):
    gate, upward, back = total[0], total[1], total[2]
    sigma = jax.nn.sigmoid(gate)
    active = gate * sigma
    hidden = (active * upward).astype(BF)
    d_gate = (back * upward * sigma * (1.0 + gate * (1.0 - sigma))).astype(BF)
    d_up = (back * active).astype(BF)
    return jnp.stack([hidden, d_gate, d_up])


def exchange(values, number):
    return {
        s: lax.ppermute(values[s], "dp", partners(ROUNDS[s][number][0])) for s in GROUPS
    }


def on_device(
    tokens, cotangent, gate_weight, up_weight, down_weight, gate_mask, up_mask, down_mask, counts
):
    live = (lax.iota(jnp.int32, tokens.shape[0]) < counts[0])[:, None]
    place = lax.axis_index("col")
    order = jnp.arange(8)
    shard = ((place // 2 + order % 4) % SIDE) * 2 + ((place % 2) ^ (order // 4))
    own = pack(tokens, cotangent, counts)
    column = [own] + [lax.ppermute(own, "col", shift(-dz, 0)) for dz in (1, 2, 3)]
    beside = [lax.ppermute(value, "col", shift(0, 1)) for value in column]
    wx, wdt, wd = prepare(gate_mask, up_mask, down_mask, gate_weight, up_weight, down_weight)
    rows = logical_rows()
    x, g, xt_first, xt_last, offs, cnts = compact(shard, rows[:, None], column + beside)

    early = partials(FIRST, 1, x, g, wx, wdt)
    late = partials(0, 3, x, g, wx, wdt)
    piece = {}
    for s in GROUPS:
        at = s[0] * 2 + s[1]
        piece[s] = (late[at], late[4 + at], late[8 + at], early[at])
    other = {s: tuple(2 - ROUNDS[s][n][1] for n in range(2)) for s in GROUPS}

    come = exchange({s: piece[s][3] for s in GROUPS}, 0)
    second = {
        s: (piece[s][other[s][1]].astype(F32) + come[s].astype(F32)).astype(BF) for s in GROUPS
    }
    come_rest = exchange({s: piece[s][other[s][0]] for s in GROUPS}, 0)
    come_second = exchange(second, 1)
    keep, send = {}, {}
    for s in GROUPS:
        total = (
            piece[s][0].astype(F32) + come_rest[s].astype(F32) + come_second[s].astype(F32)
        ).reshape(3, 2, 2, 24, HALF)
        keep[s], upper = split(total, ROUNDS[s][2][1] - 1)
        send[s] = upper.astype(BF)
    come = exchange(send, 2)
    for s in GROUPS:
        total = keep[s] + come[s].astype(F32)
        keep[s], upper = split(total, ROUNDS[s][3][1] - 1)
        send[s] = upper.astype(BF)
    come = exchange(send, 3)
    held = {s: activate(keep[s] + come[s].astype(F32)) for s in GROUPS}
    for number in (3, 2):
        come = exchange(held, number)
        held = {
            s: jnp.concatenate([held[s], come[s]], axis=ROUNDS[s][number][1] - 1)
            for s in GROUPS
        }
    held = {s: held[s].reshape(3, CUT, HALF) for s in GROUPS}
    near = exchange(held, 1)
    far = exchange(held, 0)
    last = exchange(near, 0)
    parts = [[], [], [], []]
    for s in GROUPS:
        given = {0: held[s], other[s][1]: near[s], other[s][0]: far[s], 3: last[s]}
        for p in range(4):
            parts[p].append(given[p])

    early_rows, last_rows = rows[None, :FIRST], rows[None, FIRST:]
    begun = first_output(early_rows, offs, cnts, wd, parts[0] + parts[1] + parts[2])
    mine, away = last_output(last_rows, offs, cnts, begun, wd, parts[3])
    summed = mine.astype(F32) + lax.ppermute(away, "col", shift(0, 1)).astype(F32)
    terms = [summed[k].astype(BF) for k in range(4)]
    mixed = terms[0].astype(F32)
    for dz in (1, 2, 3):
        mixed += lax.ppermute(terms[dz], "col", shift(dz, 0)).astype(F32)
    output = jnp.where(live, mixed, jnp.zeros_like(mixed)).astype(BF)
    gate_grad, up_grad, down_grad = gradients(
        gate_mask,
        up_mask,
        down_mask,
        xt_first,
        xt_last,
        g,
        parts[0] + parts[1] + parts[2] + parts[3],
    )
    return (output, gate_grad, up_grad, down_grad)


def solution(mesh):
    in_specs = (
        P("col", "dp"),
        P("col", "dp"),
        P("dp", "col"),
        P("dp", "col"),
        P("col", "dp"),
        P("dp", "col"),
        P("dp", "col"),
        P("col", "dp"),
        P("col"),
    )
    out_specs = (P("col", "dp"), P("dp", "col"), P("dp", "col"), P("col", "dp"))
    return jax.shard_map(
        on_device, mesh=mesh, in_specs=in_specs, out_specs=out_specs, check_vma=False
    )
```

```python
import functools

import jax
import jax.numpy as jnp
from jax import lax
from jax.experimental import pallas as pl
from jax.experimental.pallas import tpu as pltpu
from jax.sharding import PartitionSpec as P

BF = jnp.bfloat16
F32 = jnp.float32
LIVE = 768
PAD = 144
SIDE = 4
BLK = 128
PAIR = 2 * BLK
UNITS = 1792
HALF = UNITS // 2
STEPS = UNITS // PAIR
FEAT = 512
SLOTS = 1024
CUT = 96
VMEM = 48 << 20

MASKS = {"xA": (1, 0), "xB": (3, 0), "yA": (0, 1), "yB": (0, 3)}
ROUNDS = {
    (0, 0): (("xA", 0), ("xB", 1), ("yA", 2), ("yB", 3)),
    (0, 1): (("xB", 1), ("xA", 0), ("yB", 3), ("yA", 2)),
    (1, 0): (("yA", 0), ("yB", 1), ("xA", 2), ("xB", 3)),
    (1, 1): (("yB", 1), ("yA", 0), ("xB", 3), ("xA", 2)),
}
GROUPS = tuple(ROUNDS)


def partners(name):
    dx, dy = MASKS[name]
    return [
        (x * SIDE + y, (x ^ dx) * SIDE + (y ^ dy)) for x in range(SIDE) for y in range(SIDE)
    ]


def shift(dz, dc):
    return [
        (z * 2 + c, ((z + dz) % SIDE) * 2 + (c + dc) % 2) for z in range(SIDE) for c in range(2)
    ]


def logical_rows():
    place = lax.axis_index("dp")
    x, y = place // SIDE, place % SIDE

    def sides(v):
        high = v // 2
        return (v % 2) ^ high, high

    xa, xb = sides(x)
    ya, yb = sides(y)
    first = xa * 8 + xb * 4 + ya * 2 + yb
    second = ya * 8 + yb * 4 + xa * 2 + xb
    row = lax.iota(jnp.int32, LIVE)
    half, block, rest = row // 384, (row % 384) // 24, row % 24
    return half * 384 + (block ^ jnp.where(half > 0, second, first)) * 24 + rest


def kept(mask_ref, row, col, value):
    return jnp.where(mask_ref[row, col] > 0, value, jnp.zeros_like(value))


def smem():
    return pl.BlockSpec(memory_space=pltpu.SMEM)


def whole(shape):
    return pl.BlockSpec(shape, lambda j: (0,) * len(shape))


def call(kernel, name, flops, moved, **rest):
    return pl.pallas_call(
        kernel,
        compiler_params=pltpu.CompilerParams(vmem_limit_bytes=VMEM),
        cost_estimate=pl.CostEstimate(flops=flops, bytes_accessed=moved, transcendentals=0),
        name=name,
        **rest,
    )


def pack_kernel(tok_ref, cot_ref, count_ref, out_ref):
    out_ref[:BLK, :FEAT] = tok_ref[...]
    out_ref[:BLK, FEAT:] = cot_ref[...]
    count = jnp.full((PAD - BLK, 2 * FEAT), count_ref[0], jnp.int32)
    out_ref[BLK:, :] = count.astype(F32).astype(BF)


def pack(tokens, cotangent, counts):
    vmem = pl.BlockSpec(memory_space=pltpu.VMEM)
    return call(
        pack_kernel,
        "pack",
        0,
        1 << 19,
        out_shape=jax.ShapeDtypeStruct((PAD, 2 * FEAT), BF),
        in_specs=[vmem, vmem, smem()],
        out_specs=vmem,
    )(tokens, cotangent, counts)


def prepare_kernel(gm, um, dm, wg, wu, wd, wx_ref, wdt_ref, wd_ref):
    j = pl.program_id(0)
    for which, (mask, ref) in enumerate(((gm, wg), (um, wu))):
        for r in range(4):
            for b in range(2):
                at = slice(r * BLK, (r + 1) * BLK)
                to = b * PAIR + which * BLK
                wx_ref[0, at, to : to + BLK] = kept(
                    mask, r, 2 * j + b, ref[at, b * BLK : (b + 1) * BLK]
                )
    down = jnp.concatenate(
        [
            jnp.concatenate(
                [
                    kept(dm, 2 * j + b, c, wd[b * BLK : (b + 1) * BLK, c * BLK : (c + 1) * BLK])
                    for c in range(4)
                ],
                axis=1,
            )
            for b in range(2)
        ],
        axis=0,
    )
    wd_ref[...] = down
    wdt_ref[0] = down.T


def prepare(gm, um, dm, wg, wu, wd):
    return call(
        prepare_kernel,
        "prepare",
        0,
        13 << 20,
        grid=(STEPS,),
        out_shape=(
            jax.ShapeDtypeStruct((STEPS, FEAT, 2 * PAIR), BF),
            jax.ShapeDtypeStruct((STEPS, FEAT, PAIR), BF),
            jax.ShapeDtypeStruct((UNITS, FEAT), BF),
        ),
        in_specs=[
            smem(),
            smem(),
            smem(),
            pl.BlockSpec((FEAT, PAIR), lambda j: (0, j)),
            pl.BlockSpec((FEAT, PAIR), lambda j: (0, j)),
            pl.BlockSpec((PAIR, FEAT), lambda j: (j, 0)),
        ],
        out_specs=(
            pl.BlockSpec((1, FEAT, 2 * PAIR), lambda j: (j, 0, 0)),
            pl.BlockSpec((1, FEAT, PAIR), lambda j: (j, 0, 0)),
            pl.BlockSpec((PAIR, FEAT), lambda j: (j, 0)),
        ),
    )(gm, um, dm, wg, wu, wd)


def compact_kernel(shard, rows_ref, *refs):
    sources, (x_ref, g_ref, xt_ref, offs_ref, cnts_ref) = refs[:8], refs[8:]
    rows = rows_ref[...]
    slot = lax.broadcasted_iota(jnp.int32, (LIVE, BLK), 1)
    cnts = [ref[BLK : BLK + 1, 0:1].astype(F32).astype(jnp.int32) for ref in sources]
    total = None
    for pair in range(4):
        picks = []
        for k in (2 * pair, 2 * pair + 1):
            offset = jnp.zeros((1, 1), jnp.int32)
            for other in range(8):
                if other != k:
                    offset += jnp.where(shard[other] < shard[k], cnts[other], 0)
            offs_ref[k] = jnp.broadcast_to(offset, (8, BLK))
            cnts_ref[k] = jnp.broadcast_to(cnts[k], (8, BLK))
            hit = (rows - offset == slot) & (slot < cnts[k])
            picks.append(jnp.where(hit, 1.0, 0.0).astype(BF))
        source = jnp.concatenate(
            [sources[2 * pair][:BLK, :], sources[2 * pair + 1][:BLK, :]], axis=0
        )
        part = jnp.dot(jnp.concatenate(picks, axis=1), source, preferred_element_type=F32)
        total = part if total is None else total + part
    x_ref[...] = total[:, :FEAT].astype(BF)
    g_ref[...] = total[:, FEAT:].astype(BF)
    xt_ref[...] = total[:, :FEAT].T.astype(BF)


def compact(shard, rows, sources):
    vmem = pl.BlockSpec(memory_space=pltpu.VMEM)
    return call(
        compact_kernel,
        "compact",
        2 * LIVE * SLOTS * SLOTS,
        5 << 20,
        out_shape=(
            jax.ShapeDtypeStruct((LIVE, FEAT), BF),
            jax.ShapeDtypeStruct((LIVE, FEAT), BF),
            jax.ShapeDtypeStruct((FEAT, LIVE), BF),
            jax.ShapeDtypeStruct((8, 8, BLK), jnp.int32),
            jax.ShapeDtypeStruct((8, 8, BLK), jnp.int32),
        ),
        in_specs=[smem(), vmem] + [vmem] * 8,
        out_specs=(vmem,) * 5,
    )(shard, rows, *sources)


SENT = {0: (2, 3), 1: (1, 3)}
KEPT = {0: (0, 1), 1: (0, 2)}


def partial_kernel(pieces, x_ref, g_ref, wx_ref, wdt_ref, *refs):
    outs, (xs, gs) = refs[:4], refs[4:]

    @pl.when(pl.program_id(0) == 0)
    def _():
        for q in range(2):
            for h in range(2):
                for i, piece in enumerate(pieces[q]):
                    to, at = (h * 2 + i) * CUT, (h * 4 + piece) * CUT
                    xs[q, to : to + CUT, :] = x_ref[at : at + CUT, :]
                    gs[q, to : to + CUT, :] = g_ref[at : at + CUT, :]

    for q in range(2):
        both = jnp.dot(
            xs[q], wx_ref[0, :, q * PAIR : (q + 1) * PAIR], preferred_element_type=F32
        )
        back = jnp.dot(
            gs[q], wdt_ref[0, :, q * BLK : (q + 1) * BLK], preferred_element_type=F32
        )
        for which, result in enumerate((both[:, :BLK], both[:, BLK:], back)):
            for h in range(2):
                outs[h * 2 + q][which] = result[h * 2 * CUT : (h + 1) * 2 * CUT].astype(BF)


def partials(pieces, x, g, wx, wdt):
    count = 4 * CUT
    return call(
        functools.partial(partial_kernel, pieces),
        "partials",
        2 * count * FEAT * 3 * UNITS,
        7 << 20,
        grid=(STEPS,),
        out_shape=(jax.ShapeDtypeStruct((3, 2 * CUT, HALF), BF),) * 4,
        in_specs=[
            whole((LIVE, FEAT)),
            whole((LIVE, FEAT)),
            pl.BlockSpec((1, FEAT, 2 * PAIR), lambda j: (j, 0, 0)),
            pl.BlockSpec((1, FEAT, PAIR), lambda j: (j, 0, 0)),
        ],
        out_specs=(pl.BlockSpec((3, 2 * CUT, BLK), lambda j: (0, 0, j)),) * 4,
        scratch_shapes=[pltpu.VMEM((2, count, FEAT), BF)] * 2,
    )(x, g, wx, wdt)


def picked(rows, offs, cnts, k, slot):
    hit = (rows - offs[k, 0:1, 0:1] == slot) & (slot < cnts[k, 0:1, 0:1])
    return jnp.where(hit, 1.0, 0.0).astype(BF)


def products(sides, spare, w_down):
    shared = jnp.concatenate(
        [jnp.concatenate([sides[q][h][spare] for q in range(2)], axis=1) for h in range(2)],
        axis=0,
    )
    result = [jnp.dot(shared, w_down, preferred_element_type=F32)]
    for q in range(2):
        single = jnp.concatenate([sides[q][h][1 - spare] for h in range(2)], axis=0)
        result.append(
            jnp.dot(single, w_down[q * BLK : (q + 1) * BLK, :], preferred_element_type=F32)
        )
    return result


def cut(refs, columns):
    return [
        [[refs[h * 2 + q][0, i * CUT : (i + 1) * CUT, columns] for i in range(2)] for h in range(2)]
        for q in range(2)
    ]


def first_output_kernel(wd_ref, *refs):
    parts, total = refs[:4], refs[4]
    j = pl.program_id(0)
    results = products(cut(parts, slice(None)), 0, wd_ref[...])

    @pl.when(j == 0)
    def _():
        for i in range(3):
            total[i] = results[i]

    @pl.when(j > 0)
    def _():
        for i in range(3):
            total[i] += results[i]


def first_output(wd, parts):
    return call(
        first_output_kernel,
        "first_output",
        2 * 4 * CUT * FEAT * UNITS,
        5 << 20,
        grid=(STEPS,),
        out_shape=jax.ShapeDtypeStruct((3, 2 * CUT, FEAT), F32),
        in_specs=[pl.BlockSpec((PAIR, FEAT), lambda j: (j, 0))]
        + [pl.BlockSpec((1, 2 * CUT, BLK), lambda j: (2, 0, j))] * 4,
        out_specs=whole((3, 2 * CUT, FEAT)),
    )(wd, *parts)


def last_output_kernel(rows_ref, offs, cnts, early_ref, wd_ref, *refs):
    parts, (near_ref, away_ref) = refs[:4], refs[4:]
    totals = None
    for j in range(STEPS):
        results = products(
            cut(parts, slice(j * BLK, (j + 1) * BLK)), 1, wd_ref[j * PAIR : (j + 1) * PAIR, :]
        )
        totals = results if j == 0 else [a + b for a, b in zip(totals, results)]
    pieces = (early_ref[0], early_ref[1] + totals[2], early_ref[2] + totals[1], totals[0])
    mixed = jnp.concatenate([piece.astype(BF) for piece in pieces], axis=0)
    rows = rows_ref[0:1, :]
    slot = lax.broadcasted_iota(jnp.int32, (BLK, LIVE), 0)
    for k in range(8):
        pick = picked(rows, offs, cnts, k, slot)
        target = near_ref if k < 4 else away_ref
        target[k % 4] = jnp.dot(pick, mixed, preferred_element_type=F32).astype(BF)


def last_output(rows, offs, cnts, early, wd, parts):
    return call(
        last_output_kernel,
        "last_output",
        2 * LIVE * FEAT * (HALF + SLOTS),
        5 << 20,
        grid=(1,),
        out_shape=(jax.ShapeDtypeStruct((4, BLK, FEAT), BF),) * 2,
        in_specs=[
            whole((1, LIVE)),
            whole((8, 8, BLK)),
            whole((8, 8, BLK)),
            whole((3, 2 * CUT, FEAT)),
            whole((UNITS, FEAT)),
        ]
        + [pl.BlockSpec((1, 2 * CUT, HALF), lambda j: (2, 0, 0))] * 4,
        out_specs=(whole((4, BLK, FEAT)),) * 2,
    )(rows, offs, cnts, early, wd, *parts)


def all_rows(owns, comes, which):
    columns = []
    for q in range(2):
        pieces = []
        for h in range(2):
            own, come = owns[h * 2 + q], comes[h * 2 + q]
            if q == 0:
                pieces += [own[which], come[which]]
            else:
                pieces += [ref[which, i : i + CUT] for i in (0, CUT) for ref in (own, come)]
        columns.append(jnp.concatenate(pieces, axis=0))
    return jnp.concatenate(columns, axis=1)


def down_kernel(dm, g_ref, *refs):
    owns, comes, down_out = refs[:4], refs[4:8], refs[8]
    j = pl.program_id(0)
    down = lax.dot_general(
        all_rows(owns, comes, 0),
        g_ref[...],
        (((0,), (0,)), ((), ())),
        preferred_element_type=F32,
    )
    for r in range(4):
        for b in range(2):
            at, by = slice(r * BLK, (r + 1) * BLK), slice(b * BLK, (b + 1) * BLK)
            down_out[by, at] = kept(dm, 2 * j + b, r, down[by, at])


def down_gradient(dm, g, parts):
    return call(
        down_kernel,
        "down_gradient",
        2 * LIVE * FEAT * UNITS,
        8 << 20,
        grid=(STEPS,),
        out_shape=jax.ShapeDtypeStruct((UNITS, FEAT), F32),
        in_specs=[smem(), whole((LIVE, FEAT))]
        + [pl.BlockSpec((1, 2 * CUT, BLK), lambda j: (2, 0, j))] * 8,
        out_specs=pl.BlockSpec((PAIR, FEAT), lambda j: (j, 0)),
    )(dm, g, *parts)


def grad_kernel(gm, um, xt_ref, *refs):
    owns, comes, (gate_out, up_out) = refs[:4], refs[4:8], refs[8:]
    j = pl.program_id(0)
    xt = xt_ref[...]
    for which, mask, target in ((0, gm, gate_out), (1, um, up_out)):
        grad = jnp.dot(xt, all_rows(owns, comes, which), preferred_element_type=F32)
        for r in range(4):
            for b in range(2):
                at, by = slice(r * BLK, (r + 1) * BLK), slice(b * BLK, (b + 1) * BLK)
                target[at, by] = kept(mask, r, 2 * j + b, grad[at, by])


def gradients(gm, um, xt, parts):
    return call(
        grad_kernel,
        "gradients",
        2 * LIVE * FEAT * 2 * UNITS,
        13 << 20,
        grid=(STEPS,),
        out_shape=(jax.ShapeDtypeStruct((FEAT, UNITS), F32),) * 2,
        in_specs=[smem(), smem(), whole((FEAT, LIVE))]
        + [pl.BlockSpec((2, 2 * CUT, BLK), lambda j: (0, 0, j))] * 8,
        out_specs=(pl.BlockSpec((FEAT, PAIR), lambda j: (0, j)),) * 2,
    )(gm, um, xt, *parts)


def split(value, axis):
    lower = lax.slice_in_dim(value, 0, 1, axis=axis)
    upper = lax.slice_in_dim(value, 1, 2, axis=axis)
    return lower, upper


def activate(total):
    gate, upward, back = total[0], total[1], total[2]
    sigma = jax.nn.sigmoid(gate)
    active = gate * sigma
    hidden = (active * upward).astype(BF)
    d_gate = (back * upward * sigma * (1.0 + gate * (1.0 - sigma))).astype(BF)
    d_up = (back * active).astype(BF)
    return jnp.stack([d_gate, d_up, hidden])


def exchange(values, number):
    return {
        s: lax.ppermute(values[s], "dp", partners(ROUNDS[s][number][0])) for s in GROUPS
    }


def on_device(
    tokens, cotangent, gate_weight, up_weight, down_weight, gate_mask, up_mask, down_mask, counts
):
    live = (lax.iota(jnp.int32, tokens.shape[0]) < counts[0])[:, None]
    place = lax.axis_index("col")
    order = jnp.arange(8)
    shard = ((place // 2 + order % 4) % SIDE) * 2 + ((place % 2) ^ (order // 4))
    own = pack(tokens, cotangent, counts)
    column = [own] + [lax.ppermute(own, "col", shift(-dz, 0)) for dz in (1, 2, 3)]
    beside = [lax.ppermute(own, "col", shift(0, 1))]
    wx, wdt, wd = prepare(gate_mask, up_mask, down_mask, gate_weight, up_weight, down_weight)
    rows = logical_rows()
    place_rows = rows.reshape(2, 4, CUT).transpose(1, 0, 2).reshape(1, LIVE)
    *column, wx, wdt, wd, rows, place_rows, shard = lax.optimization_barrier(
        (*column, wx, wdt, wd, rows[:, None], place_rows, shard)
    )
    beside += [lax.ppermute(value, "col", shift(0, 1)) for value in column[1:]]
    x, g, xt, offs, cnts = compact(shard, rows, column + beside)

    sent = dict(zip(GROUPS, partials(SENT, x, g, wx, wdt)))
    come = exchange(sent, 0)
    x_rest, g_rest, *_ = lax.optimization_barrier((x, g, *sent.values()))
    keep = dict(zip(GROUPS, partials(KEPT, x_rest, g_rest, wx, wdt)))
    send = {}
    for s in GROUPS:
        total = (keep[s].astype(F32) + come[s].astype(F32)).reshape(3, 2, CUT, HALF)
        keep[s], upper = split(total, 1)
        send[s] = upper.astype(BF)
    come = exchange(send, 1)
    for s in GROUPS:
        total = (keep[s] + come[s].astype(F32)).reshape(3, 2, 2, 24, HALF)
        keep[s], upper = split(total, ROUNDS[s][2][1] - 1)
        send[s] = upper.astype(BF)
    come = exchange(send, 2)
    keep = {s: (keep[s] + come[s].astype(F32)).astype(BF) for s in GROUPS}
    come = exchange(keep, 3)
    held = {}
    for s in GROUPS:
        axis = ROUNDS[s][3][1] - 1
        lower, upper = split(come[s], axis)
        arrived = jnp.concatenate([upper, lower], axis=axis)
        held[s] = activate(keep[s].astype(F32) + arrived.astype(F32))
    come = exchange(held, 2)
    held = {
        s: jnp.concatenate([held[s], come[s]], axis=ROUNDS[s][2][1] - 1).reshape(3, CUT, HALF)
        for s in GROUPS
    }
    come = exchange(held, 1)
    held = {s: jnp.concatenate([held[s], come[s]], axis=1) for s in GROUPS}
    come = exchange(held, 0)
    owns, comes = [held[s] for s in GROUPS], [come[s] for s in GROUPS]

    begun = first_output(wd, owns)
    mine, away = last_output(place_rows, offs, cnts, begun, wd, comes)
    other = lax.ppermute(away, "col", shift(0, 1))
    down_grad = down_gradient(down_mask, g, owns + comes)
    other, down_grad = lax.optimization_barrier((other, down_grad))
    summed = mine.astype(F32) + other.astype(F32)
    terms = [summed[k].astype(BF) for k in range(4)]
    mixed = terms[0].astype(F32)
    for dz in (1, 2, 3):
        mixed += lax.ppermute(terms[dz], "col", shift(dz, 0)).astype(F32)
    output = jnp.where(live, mixed, jnp.zeros_like(mixed)).astype(BF)
    gate_grad, up_grad = gradients(gate_mask, up_mask, xt, owns + comes)
    return (output, gate_grad, up_grad, down_grad)


def solution(mesh):
    in_specs = (
        P("col", "dp"),
        P("col", "dp"),
        P("dp", "col"),
        P("dp", "col"),
        P("col", "dp"),
        P("dp", "col"),
        P("dp", "col"),
        P("col", "dp"),
        P("col"),
    )
    out_specs = (P("col", "dp"), P("dp", "col"), P("dp", "col"), P("col", "dp"))
    return jax.shard_map(
        on_device, mesh=mesh, in_specs=in_specs, out_specs=out_specs, check_vma=False
    )
```

```python
import functools

import jax
import jax.numpy as jnp
from jax import lax
from jax.experimental import pallas as pl
from jax.experimental.pallas import tpu as pltpu
from jax.sharding import PartitionSpec as P

BF = jnp.bfloat16
F32 = jnp.float32
LIVE = 768
PAD = 144
SIDE = 4
BLK = 128
PAIR = 2 * BLK
UNITS = 1792
HALF = UNITS // 2
STEPS = UNITS // PAIR
FEAT = 512
SLOTS = 1024
CUT = 192
FIRST = 576
LAST = LIVE - FIRST
VMEM = 32 << 20

MASKS = {"xA": (1, 0), "xB": (3, 0), "yA": (0, 1), "yB": (0, 3)}
ROUNDS = (
    ((0, ("xA", "yA")), (1, ("xB", "yB")), (2, ("yA", "xA")), (3, ("yB", "xB"))),
    ((1, ("xB", "yB")), (0, ("xA", "yA")), (3, ("yB", "xB")), (2, ("yA", "xA"))),
)
SIDES = (0, 1)


def partners(names):
    pairs = []
    for col in range(2 * SIDE):
        dx, dy = MASKS[names[col % 2]]
        for x in range(SIDE):
            for y in range(SIDE):
                start = (col * SIDE + x) * SIDE + y
                pairs.append((start, (col * SIDE + (x ^ dx)) * SIDE + (y ^ dy)))
    return pairs


def shift(dz, dc):
    return [
        (z * 2 + c, ((z + dz) % SIDE) * 2 + (c + dc) % 2) for z in range(SIDE) for c in range(2)
    ]


def logical_rows():
    place = lax.axis_index("dp")
    x, y = place // SIDE, place % SIDE

    def sides(v):
        high = v // 2
        return (v % 2) ^ high, high

    xa, xb = sides(x)
    ya, yb = sides(y)
    first = xa * 8 + xb * 4 + ya * 2 + yb
    second = ya * 8 + yb * 4 + xa * 2 + xb
    mask = jnp.where(lax.axis_index("col") % 2 > 0, second, first)
    row = lax.iota(jnp.int32, LIVE)
    return ((row // 48) ^ mask) * 48 + row % 48


def kept(mask_ref, row, col, value):
    return jnp.where(mask_ref[row, col] > 0, value, jnp.zeros_like(value))


def smem():
    return pl.BlockSpec(memory_space=pltpu.SMEM)


def whole(shape):
    return pl.BlockSpec(shape, lambda j: (0,) * len(shape))


def call(kernel, name, flops, moved, **rest):
    return pl.pallas_call(
        kernel,
        compiler_params=pltpu.CompilerParams(vmem_limit_bytes=VMEM),
        cost_estimate=pl.CostEstimate(flops=flops, bytes_accessed=moved, transcendentals=0),
        name=name,
        **rest,
    )


def pack_kernel(tok_ref, cot_ref, count_ref, out_ref):
    out_ref[:BLK, :FEAT] = tok_ref[...]
    out_ref[:BLK, FEAT:] = cot_ref[...]
    count = jnp.full((PAD - BLK, 2 * FEAT), count_ref[0], jnp.int32)
    out_ref[BLK:, :] = count.astype(F32).astype(BF)


def pack(tokens, cotangent, counts):
    return call(
        pack_kernel,
        "pack",
        0,
        1 << 19,
        out_shape=jax.ShapeDtypeStruct((PAD, 2 * FEAT), BF),
        grid=(1,),
        in_specs=[whole((BLK, FEAT)), whole((BLK, FEAT)), smem()],
        out_specs=whole((PAD, 2 * FEAT)),
    )(tokens, cotangent, counts)


def prepare_kernel(gm, um, dm, wg, wu, wd, wx_ref, wdt_ref, wd_ref):
    j = pl.program_id(0)
    for which, (mask, ref) in enumerate(((gm, wg), (um, wu))):
        for r in range(4):
            for b in range(2):
                at = slice(r * BLK, (r + 1) * BLK)
                wx_ref[0, at, which * PAIR + b * BLK : which * PAIR + (b + 1) * BLK] = kept(
                    mask, r, 2 * j + b, ref[at, b * BLK : (b + 1) * BLK]
                )
    down = jnp.concatenate(
        [
            jnp.concatenate(
                [
                    kept(dm, 2 * j + b, c, wd[b * BLK : (b + 1) * BLK, c * BLK : (c + 1) * BLK])
                    for c in range(4)
                ],
                axis=1,
            )
            for b in range(2)
        ],
        axis=0,
    )
    wd_ref[...] = down
    wdt_ref[0] = down.T


def prepare(gm, um, dm, wg, wu, wd):
    return call(
        prepare_kernel,
        "prepare",
        0,
        13 << 20,
        grid=(STEPS,),
        out_shape=(
            jax.ShapeDtypeStruct((STEPS, FEAT, 2 * PAIR), BF),
            jax.ShapeDtypeStruct((STEPS, FEAT, PAIR), BF),
            jax.ShapeDtypeStruct((UNITS, FEAT), BF),
        ),
        in_specs=[
            smem(),
            smem(),
            smem(),
            pl.BlockSpec((FEAT, PAIR), lambda j: (0, j)),
            pl.BlockSpec((FEAT, PAIR), lambda j: (0, j)),
            pl.BlockSpec((PAIR, FEAT), lambda j: (j, 0)),
        ],
        out_specs=(
            pl.BlockSpec((1, FEAT, 2 * PAIR), lambda j: (j, 0, 0)),
            pl.BlockSpec((1, FEAT, PAIR), lambda j: (j, 0, 0)),
            pl.BlockSpec((PAIR, FEAT), lambda j: (j, 0)),
        ),
    )(gm, um, dm, wg, wu, wd)


def compact_kernel(shard, rows_ref, *refs):
    sources, (x_ref, g_ref, xt_ref, offs_ref, cnts_ref) = refs[:8], refs[8:]
    rows = rows_ref[...]
    slot = lax.broadcasted_iota(jnp.int32, (LIVE, BLK), 1)
    cnts = [ref[BLK : BLK + 1, 0:1].astype(F32).astype(jnp.int32) for ref in sources]
    total = None
    for pair in range(4):
        picks = []
        for k in (2 * pair, 2 * pair + 1):
            offset = jnp.zeros((1, 1), jnp.int32)
            for other in range(8):
                if other != k:
                    offset += jnp.where(shard[other] < shard[k], cnts[other], 0)
            offs_ref[k] = jnp.broadcast_to(offset, (8, BLK))
            cnts_ref[k] = jnp.broadcast_to(cnts[k], (8, BLK))
            hit = (rows - offset == slot) & (slot < cnts[k])
            picks.append(jnp.where(hit, 1.0, 0.0).astype(BF))
        source = jnp.concatenate(
            [sources[2 * pair][:BLK, :], sources[2 * pair + 1][:BLK, :]], axis=0
        )
        part = jnp.dot(jnp.concatenate(picks, axis=1), source, preferred_element_type=F32)
        total = part if total is None else total + part
    x_ref[...] = total[:, :FEAT].astype(BF)
    g_ref[...] = total[:, FEAT:].astype(BF)
    xt_ref[...] = total[:, :FEAT].T.astype(BF)


def compact(shard, rows, sources):
    vmem = pl.BlockSpec(memory_space=pltpu.VMEM)
    return call(
        compact_kernel,
        "compact",
        2 * LIVE * SLOTS * SLOTS,
        5 << 20,
        out_shape=(
            jax.ShapeDtypeStruct((LIVE, FEAT), BF),
            jax.ShapeDtypeStruct((LIVE, FEAT), BF),
            jax.ShapeDtypeStruct((FEAT, LIVE), BF),
            jax.ShapeDtypeStruct((8, 8, BLK), jnp.int32),
            jax.ShapeDtypeStruct((8, 8, BLK), jnp.int32),
        ),
        in_specs=[smem(), vmem] + [vmem] * 8,
        out_specs=(vmem,) * 5,
    )(shard, rows, *sources)


def partial_kernel(start, pieces, x_ref, g_ref, wx_ref, wdt_ref, *outs):
    count = pieces * CUT
    x, g = x_ref[start : start + count, :], g_ref[start : start + count, :]
    both = jnp.dot(x, wx_ref[0], preferred_element_type=F32)
    back = jnp.dot(g, wdt_ref[0], preferred_element_type=F32)
    for which, result in enumerate((both[:, :PAIR], both[:, PAIR:], back)):
        for piece in range(pieces):
            for q in SIDES:
                outs[piece * 2 + q][which] = result[
                    piece * CUT : (piece + 1) * CUT, q * BLK : (q + 1) * BLK
                ].astype(BF)


def partials(start, pieces, x, g, wx, wdt):
    count = pieces * CUT
    return call(
        functools.partial(partial_kernel, start, pieces),
        "partials",
        2 * count * FEAT * 3 * UNITS,
        7 << 20,
        grid=(STEPS,),
        out_shape=(jax.ShapeDtypeStruct((3, CUT, HALF), BF),) * (2 * pieces),
        in_specs=[
            whole((LIVE, FEAT)),
            whole((LIVE, FEAT)),
            pl.BlockSpec((1, FEAT, 2 * PAIR), lambda j: (j, 0, 0)),
            pl.BlockSpec((1, FEAT, PAIR), lambda j: (j, 0, 0)),
        ],
        out_specs=(pl.BlockSpec((3, CUT, BLK), lambda j: (0, 0, j)),) * (2 * pieces),
    )(x, g, wx, wdt)


def stacked(refs, which, pieces):
    return jnp.concatenate(
        [jnp.concatenate([refs[p * 2 + q][which] for q in SIDES], axis=1) for p in pieces],
        axis=0,
    )


def picked(rows, offs, cnts, k, slot):
    hit = (rows - offs[k, 0:1, 0:1] == slot) & (slot < cnts[k, 0:1, 0:1])
    return jnp.where(hit, 1.0, 0.0).astype(BF)


def first_output_kernel(rows_ref, offs, cnts, wd_ref, *refs):
    parts, (out_ref, total) = refs[:6], refs[6:]
    j = pl.program_id(0)
    part = jnp.dot(stacked(parts, 0, range(3)), wd_ref[...], preferred_element_type=F32)

    @pl.when(j == 0)
    def _():
        total[...] = part

    @pl.when(j > 0)
    def _():
        total[...] += part

    @pl.when(j == STEPS - 1)
    def _():
        mixed = total[...].astype(BF)
        rows = rows_ref[0:1, :]
        slot = lax.broadcasted_iota(jnp.int32, (BLK, FIRST), 0)
        for k in range(8):
            pick = picked(rows, offs, cnts, k, slot)
            out_ref[k] = jnp.dot(pick, mixed, preferred_element_type=F32).astype(BF)


def first_output(rows, offs, cnts, wd, parts):
    return call(
        first_output_kernel,
        "first_output",
        1,
        1 << 12,
        grid=(STEPS,),
        out_shape=jax.ShapeDtypeStruct((8, BLK, FEAT), BF),
        in_specs=[whole((1, FIRST)), whole((8, 8, BLK)), whole((8, 8, BLK))]
        + [pl.BlockSpec((PAIR, FEAT), lambda j: (j, 0))]
        + [pl.BlockSpec((1, CUT, BLK), lambda j: (2, 0, j))] * 6,
        out_specs=whole((8, BLK, FEAT)),
        scratch_shapes=[pltpu.VMEM((FIRST, FEAT), F32)],
    )(rows, offs, cnts, wd, *parts)


def last_output_kernel(rows_ref, offs, cnts, early_ref, wd_ref, *refs):
    parts, (near_ref, away_ref) = refs[:2], refs[2:]
    mixed = None
    for j in range(STEPS):
        hidden = jnp.concatenate(
            [parts[q][0, :, j * BLK : (j + 1) * BLK] for q in SIDES], axis=1
        )
        part = jnp.dot(
            hidden, wd_ref[j * PAIR : (j + 1) * PAIR, :], preferred_element_type=F32
        )
        mixed = part if mixed is None else mixed + part
    mixed = mixed.astype(BF)
    rows = rows_ref[0:1, :]
    slot = lax.broadcasted_iota(jnp.int32, (BLK, LAST), 0)
    for k in range(8):
        pick = picked(rows, offs, cnts, k, slot)
        late = jnp.dot(pick, mixed, preferred_element_type=F32)
        target = near_ref if k < 4 else away_ref
        target[k % 4] = (early_ref[k].astype(F32) + late).astype(BF)


def last_output(rows, offs, cnts, early, wd, parts):
    return call(
        last_output_kernel,
        "last_output",
        1,
        1 << 12,
        grid=(1,),
        out_shape=(jax.ShapeDtypeStruct((4, BLK, FEAT), BF),) * 2,
        in_specs=[
            whole((1, LAST)),
            whole((8, 8, BLK)),
            whole((8, 8, BLK)),
            whole((8, BLK, FEAT)),
            whole((UNITS, FEAT)),
        ]
        + [whole((1, CUT, HALF))] * 2,
        out_specs=(whole((4, BLK, FEAT)),) * 2,
    )(rows, offs, cnts, early, wd, *parts)


def grad_kernel(gm, um, dm, xt_ref, g_ref, *refs):
    parts, lasts, last_hidden = refs[:6], refs[6:8], refs[8:10]
    gate_out, up_out, down_out = refs[10:]
    j = pl.program_id(0)

    def rows(which):
        late = stacked(lasts, which, (0,)) if which < 2 else stacked(last_hidden, 0, (0,))
        return jnp.concatenate([stacked(parts, which, range(3)), late], axis=0)

    xt = xt_ref[...]
    gate = jnp.dot(xt, rows(0), preferred_element_type=F32)
    up = jnp.dot(xt, rows(1), preferred_element_type=F32)
    down = lax.dot_general(
        rows(2), g_ref[...], (((0,), (0,)), ((), ())), preferred_element_type=F32
    )
    for r in range(4):
        for b in range(2):
            at, by = slice(r * BLK, (r + 1) * BLK), slice(b * BLK, (b + 1) * BLK)
            gate_out[at, by] = kept(gm, r, 2 * j + b, gate[at, by])
            up_out[at, by] = kept(um, r, 2 * j + b, up[at, by])
            down_out[by, at] = kept(dm, 2 * j + b, r, down[by, at])


def gradients(gm, um, dm, xt, g, parts, lasts, last_hidden):
    return call(
        grad_kernel,
        "gradients",
        2 * LIVE * FEAT * 3 * UNITS,
        20 << 20,
        grid=(STEPS,),
        out_shape=(
            jax.ShapeDtypeStruct((FEAT, UNITS), F32),
            jax.ShapeDtypeStruct((FEAT, UNITS), F32),
            jax.ShapeDtypeStruct((UNITS, FEAT), F32),
        ),
        in_specs=[smem(), smem(), smem(), whole((FEAT, LIVE)), whole((LIVE, FEAT))]
        + [pl.BlockSpec((3, CUT, BLK), lambda j: (0, 0, j))] * 6
        + [pl.BlockSpec((2, CUT, BLK), lambda j: (0, 0, j))] * 2
        + [pl.BlockSpec((1, CUT, BLK), lambda j: (0, 0, j))] * 2,
        out_specs=(
            pl.BlockSpec((FEAT, PAIR), lambda j: (0, j)),
            pl.BlockSpec((FEAT, PAIR), lambda j: (0, j)),
            pl.BlockSpec((PAIR, FEAT), lambda j: (j, 0)),
        ),
    )(gm, um, dm, xt, g, *parts, *lasts, *last_hidden)


def split(value, axis):
    lower = lax.slice_in_dim(value, 0, 1, axis=axis)
    upper = lax.slice_in_dim(value, 1, 2, axis=axis)
    return lower, upper


def activate(total):
    gate, upward, back = total[0], total[1], total[2]
    sigma = jax.nn.sigmoid(gate)
    active = gate * sigma
    hidden = (active * upward).astype(BF)
    d_gate = (back * upward * sigma * (1.0 + gate * (1.0 - sigma))).astype(BF)
    d_up = (back * active).astype(BF)
    return jnp.stack([d_gate, d_up, hidden])


def exchange(values, number):
    return [
        lax.ppermute(values[q], ("col", "dp"), partners(ROUNDS[q][number][1])) for q in SIDES
    ]


def on_device(
    tokens, cotangent, gate_weight, up_weight, down_weight, gate_mask, up_mask, down_mask, counts
):
    live = (lax.iota(jnp.int32, tokens.shape[0]) < counts[0])[:, None]
    place = lax.axis_index("col")
    order = jnp.arange(8)
    shard = ((place // 2 + order % 4) % SIDE) * 2 + ((place % 2) ^ (order // 4))
    own = pack(tokens, cotangent, counts)
    column = [own] + [lax.ppermute(own, "col", shift(-dz, 0)) for dz in (1, 2, 3)]
    beside = [lax.ppermute(own, "col", shift(0, 1))]
    wx, wdt, wd = prepare(gate_mask, up_mask, down_mask, gate_weight, up_weight, down_weight)
    rows = logical_rows()
    *column, wx, wdt, wd, rows_down, rows_along, shard = lax.optimization_barrier(
        (*column, wx, wdt, wd, rows[:, None], rows[None, :], shard)
    )
    beside += [lax.ppermute(value, "col", shift(0, 1)) for value in column[1:]]
    x, g, xt, offs, cnts = compact(shard, rows_down, column + beside)

    early = partials(FIRST, 1, x, g, wx, wdt)
    come_early = exchange(early, 0)
    x_rest, g_rest, *_ = lax.optimization_barrier((x, g, *early))
    late = partials(0, 3, x_rest, g_rest, wx, wdt)
    zero = [late[q] for q in SIDES]
    side = [[late[2 * (2 - ROUNDS[q][n][0]) + q] for q in SIDES] for n in range(2)]
    come_rest = exchange(side[0], 0)
    second = [
        (side[1][q].astype(F32) + come_early[q].astype(F32)).astype(BF) for q in SIDES
    ]
    come_second = exchange(second, 1)
    keep, send = [None] * 2, [None] * 2
    for q in SIDES:
        total = (
            zero[q].astype(F32) + come_rest[q].astype(F32) + come_second[q].astype(F32)
        ).reshape(3, 2, 2, 48, HALF)
        keep[q], upper = split(total, ROUNDS[q][2][0] - 1)
        send[q] = upper.astype(BF)
    come = exchange(send, 2)
    keep = [(keep[q] + come[q].astype(F32)).astype(BF) for q in SIDES]
    come = exchange(keep, 3)
    held = []
    for q in SIDES:
        axis = ROUNDS[q][3][0] - 1
        lower, upper = split(come[q], axis)
        arrived = jnp.concatenate([upper, lower], axis=axis)
        held.append(activate(keep[q].astype(F32) + arrived.astype(F32)))
    come = exchange(held, 2)
    held = [
        jnp.concatenate([held[q], come[q]], axis=ROUNDS[q][2][0] - 1).reshape(3, CUT, HALF)
        for q in SIDES
    ]
    near = exchange(held, 1)
    far = exchange(held, 0)
    last_hidden = exchange([near[q][2:] for q in SIDES], 0)
    lasts = exchange([near[q][:2] for q in SIDES], 0)
    parts = list(held)
    for piece in (1, 2):
        for q in SIDES:
            parts.append(near[q] if 2 - ROUNDS[q][1][0] == piece else far[q])

    begun = first_output(rows_along[:, :FIRST], offs, cnts, wd, parts)
    mine, away = last_output(rows_along[:, FIRST:], offs, cnts, begun, wd, last_hidden)
    other = lax.ppermute(away, "col", shift(0, 1))
    summed = mine.astype(F32) + other.astype(F32)
    terms = [summed[k].astype(BF) for k in range(4)]
    mixed = terms[0].astype(F32)
    for dz in (1, 2, 3):
        mixed += lax.ppermute(terms[dz], "col", shift(dz, 0)).astype(F32)
    output = jnp.where(live, mixed, jnp.zeros_like(mixed)).astype(BF)
    gate_grad, up_grad, down_grad = gradients(
        gate_mask, up_mask, down_mask, xt, g, parts, lasts, last_hidden
    )
    return (output, gate_grad, up_grad, down_grad)


def solution(mesh):
    in_specs = (
        P("col", "dp"),
        P("col", "dp"),
        P("dp", "col"),
        P("dp", "col"),
        P("col", "dp"),
        P("dp", "col"),
        P("dp", "col"),
        P("col", "dp"),
        P("col"),
    )
    out_specs = (P("col", "dp"), P("dp", "col"), P("dp", "col"), P("col", "dp"))
    return jax.shard_map(
        on_device, mesh=mesh, in_specs=in_specs, out_specs=out_specs, check_vma=False
    )
```

```python
import functools

import jax
import jax.numpy as jnp
from jax import lax
from jax.experimental import pallas as pl
from jax.experimental.pallas import tpu as pltpu
from jax.sharding import PartitionSpec as P

BF = jnp.bfloat16
F32 = jnp.float32
LIVE = 768
PAD = 144
SIDE = 4
BLK = 128
PAIR = 2 * BLK
UNITS = 1792
HALF = UNITS // 2
STEPS = UNITS // PAIR
FEAT = 512
SLOTS = 1024
CUT = 192
FIRST = 576
LAST = LIVE - FIRST
VMEM = 32 << 20

MASKS = {"xA": (1, 0), "xB": (3, 0), "yA": (0, 1), "yB": (0, 3)}
ROUNDS = (
    ((0, ("xA", "yA")), (1, ("xB", "yB")), (2, ("yA", "xA")), (3, ("yB", "xB"))),
    ((1, ("xB", "yB")), (0, ("xA", "yA")), (3, ("yB", "xB")), (2, ("yA", "xA"))),
)
SIDES = (0, 1)


def partners(names):
    pairs = []
    for col in range(2 * SIDE):
        dx, dy = MASKS[names[col % 2]]
        for x in range(SIDE):
            for y in range(SIDE):
                start = (col * SIDE + x) * SIDE + y
                pairs.append((start, (col * SIDE + (x ^ dx)) * SIDE + (y ^ dy)))
    return pairs


def shift(dz, dc):
    return [
        (z * 2 + c, ((z + dz) % SIDE) * 2 + (c + dc) % 2) for z in range(SIDE) for c in range(2)
    ]


def logical_rows():
    place = lax.axis_index("dp")
    x, y = place // SIDE, place % SIDE

    def sides(v):
        high = v // 2
        return (v % 2) ^ high, high

    xa, xb = sides(x)
    ya, yb = sides(y)
    first = xa * 8 + xb * 4 + ya * 2 + yb
    second = ya * 8 + yb * 4 + xa * 2 + xb
    mask = jnp.where(lax.axis_index("col") % 2 > 0, second, first)
    row = lax.iota(jnp.int32, LIVE)
    return ((row // 48) ^ mask) * 48 + row % 48


def kept(mask_ref, row, col, value):
    return jnp.where(mask_ref[row, col] > 0, value, jnp.zeros_like(value))


def smem():
    return pl.BlockSpec(memory_space=pltpu.SMEM)


def whole(shape):
    return pl.BlockSpec(shape, lambda j: (0,) * len(shape))


def call(kernel, name, flops, moved, **rest):
    return pl.pallas_call(
        kernel,
        compiler_params=pltpu.CompilerParams(vmem_limit_bytes=VMEM),
        cost_estimate=pl.CostEstimate(flops=flops, bytes_accessed=moved, transcendentals=0),
        name=name,
        **rest,
    )


def pack_kernel(tok_ref, cot_ref, count_ref, out_ref):
    out_ref[:BLK, :FEAT] = tok_ref[...]
    out_ref[:BLK, FEAT:] = cot_ref[...]
    count = jnp.full((PAD - BLK, 2 * FEAT), count_ref[0], jnp.int32)
    out_ref[BLK:, :] = count.astype(F32).astype(BF)


def pack(tokens, cotangent, counts):
    return call(
        pack_kernel,
        "pack",
        0,
        1 << 19,
        out_shape=jax.ShapeDtypeStruct((PAD, 2 * FEAT), BF),
        grid=(1,),
        in_specs=[whole((BLK, FEAT)), whole((BLK, FEAT)), smem()],
        out_specs=whole((PAD, 2 * FEAT)),
    )(tokens, cotangent, counts)


def prepare_kernel(gm, um, dm, wg, wu, wd, wx_ref, wdt_ref, wd_ref):
    j = pl.program_id(0)
    for which, (mask, ref) in enumerate(((gm, wg), (um, wu))):
        for r in range(4):
            for b in range(2):
                at = slice(r * BLK, (r + 1) * BLK)
                wx_ref[0, at, which * PAIR + b * BLK : which * PAIR + (b + 1) * BLK] = kept(
                    mask, r, 2 * j + b, ref[at, b * BLK : (b + 1) * BLK]
                )
    down = jnp.concatenate(
        [
            jnp.concatenate(
                [
                    kept(dm, 2 * j + b, c, wd[b * BLK : (b + 1) * BLK, c * BLK : (c + 1) * BLK])
                    for c in range(4)
                ],
                axis=1,
            )
            for b in range(2)
        ],
        axis=0,
    )
    wd_ref[...] = down
    wdt_ref[0] = down.T


def prepare(gm, um, dm, wg, wu, wd):
    return call(
        prepare_kernel,
        "prepare",
        0,
        13 << 20,
        grid=(STEPS,),
        out_shape=(
            jax.ShapeDtypeStruct((STEPS, FEAT, 2 * PAIR), BF),
            jax.ShapeDtypeStruct((STEPS, FEAT, PAIR), BF),
            jax.ShapeDtypeStruct((UNITS, FEAT), BF),
        ),
        in_specs=[
            smem(),
            smem(),
            smem(),
            pl.BlockSpec((FEAT, PAIR), lambda j: (0, j)),
            pl.BlockSpec((FEAT, PAIR), lambda j: (0, j)),
            pl.BlockSpec((PAIR, FEAT), lambda j: (j, 0)),
        ],
        out_specs=(
            pl.BlockSpec((1, FEAT, 2 * PAIR), lambda j: (j, 0, 0)),
            pl.BlockSpec((1, FEAT, PAIR), lambda j: (j, 0, 0)),
            pl.BlockSpec((PAIR, FEAT), lambda j: (j, 0)),
        ),
    )(gm, um, dm, wg, wu, wd)


def compact_kernel(shard, rows_ref, *refs):
    sources, (x_ref, g_ref, xt_ref, offs_ref, cnts_ref) = refs[:8], refs[8:]
    rows = rows_ref[...]
    slot = lax.broadcasted_iota(jnp.int32, (LIVE, BLK), 1)
    cnts = [ref[BLK : BLK + 1, 0:1].astype(F32).astype(jnp.int32) for ref in sources]
    total = None
    for pair in range(4):
        picks = []
        for k in (2 * pair, 2 * pair + 1):
            offset = jnp.zeros((1, 1), jnp.int32)
            for other in range(8):
                if other != k:
                    offset += jnp.where(shard[other] < shard[k], cnts[other], 0)
            offs_ref[k] = jnp.broadcast_to(offset, (8, BLK))
            cnts_ref[k] = jnp.broadcast_to(cnts[k], (8, BLK))
            hit = (rows - offset == slot) & (slot < cnts[k])
            picks.append(jnp.where(hit, 1.0, 0.0).astype(BF))
        source = jnp.concatenate(
            [sources[2 * pair][:BLK, :], sources[2 * pair + 1][:BLK, :]], axis=0
        )
        part = jnp.dot(jnp.concatenate(picks, axis=1), source, preferred_element_type=F32)
        total = part if total is None else total + part
    x_ref[...] = total[:, :FEAT].astype(BF)
    g_ref[...] = total[:, FEAT:].astype(BF)
    xt_ref[...] = total[:, :FEAT].T.astype(BF)


def compact(shard, rows, sources):
    vmem = pl.BlockSpec(memory_space=pltpu.VMEM)
    return call(
        compact_kernel,
        "compact",
        2 * LIVE * SLOTS * SLOTS,
        5 << 20,
        out_shape=(
            jax.ShapeDtypeStruct((LIVE, FEAT), BF),
            jax.ShapeDtypeStruct((LIVE, FEAT), BF),
            jax.ShapeDtypeStruct((FEAT, LIVE), BF),
            jax.ShapeDtypeStruct((8, 8, BLK), jnp.int32),
            jax.ShapeDtypeStruct((8, 8, BLK), jnp.int32),
        ),
        in_specs=[smem(), vmem] + [vmem] * 8,
        out_specs=(vmem,) * 5,
    )(shard, rows, *sources)


def partial_kernel(start, pieces, x_ref, g_ref, wx_ref, wdt_ref, *outs):
    count = pieces * CUT
    x, g = x_ref[start : start + count, :], g_ref[start : start + count, :]
    both = jnp.dot(x, wx_ref[0], preferred_element_type=F32)
    back = jnp.dot(g, wdt_ref[0], preferred_element_type=F32)
    for which, result in enumerate((both[:, :PAIR], both[:, PAIR:], back)):
        for piece in range(pieces):
            for q in SIDES:
                outs[piece * 2 + q][which] = result[
                    piece * CUT : (piece + 1) * CUT, q * BLK : (q + 1) * BLK
                ].astype(BF)


def partials(start, pieces, x, g, wx, wdt):
    count = pieces * CUT
    return call(
        functools.partial(partial_kernel, start, pieces),
        "partials",
        2 * count * FEAT * 3 * UNITS,
        7 << 20,
        grid=(STEPS,),
        out_shape=(jax.ShapeDtypeStruct((3, CUT, HALF), BF),) * (2 * pieces),
        in_specs=[
            whole((LIVE, FEAT)),
            whole((LIVE, FEAT)),
            pl.BlockSpec((1, FEAT, 2 * PAIR), lambda j: (j, 0, 0)),
            pl.BlockSpec((1, FEAT, PAIR), lambda j: (j, 0, 0)),
        ],
        out_specs=(pl.BlockSpec((3, CUT, BLK), lambda j: (0, 0, j)),) * (2 * pieces),
    )(x, g, wx, wdt)


def picked(rows, offs, cnts, k, slot):
    hit = (rows - offs[k, 0:1, 0:1] == slot) & (slot < cnts[k, 0:1, 0:1])
    return jnp.where(hit, 1.0, 0.0).astype(BF)


def products(lower, upper, shared, w_down):
    both, single = (lower, upper) if shared == 0 else (upper, lower)
    result = [
        jnp.dot(jnp.concatenate(both, axis=1), w_down, preferred_element_type=F32)
    ]
    for q in SIDES:
        result.append(
            jnp.dot(single[q], w_down[q * BLK : (q + 1) * BLK, :], preferred_element_type=F32)
        )
    return result


def first_output_kernel(wd_ref, own0, own1, total):
    j = pl.program_id(0)
    lower = [ref[0, :CUT, :] for ref in (own0, own1)]
    upper = [ref[0, CUT:, :] for ref in (own0, own1)]
    results = products(lower, upper, 0, wd_ref[...])

    @pl.when(j == 0)
    def _():
        for i in range(3):
            total[i] = results[i]

    @pl.when(j > 0)
    def _():
        for i in range(3):
            total[i] += results[i]


def first_output(wd, hidden_own):
    return call(
        first_output_kernel,
        "first_output",
        1,
        1 << 12,
        grid=(STEPS,),
        out_shape=jax.ShapeDtypeStruct((3, CUT, FEAT), F32),
        in_specs=[pl.BlockSpec((PAIR, FEAT), lambda j: (j, 0))]
        + [pl.BlockSpec((1, 2 * CUT, BLK), lambda j: (0, 0, j))] * 2,
        out_specs=whole((3, CUT, FEAT)),
    )(wd, *hidden_own)


def last_output_kernel(rows_ref, offs, cnts, early_ref, wd_ref, come0, come1, near_ref, away_ref):
    totals = None
    for j in range(STEPS):
        by = slice(j * BLK, (j + 1) * BLK)
        lower = [ref[0, :CUT, by] for ref in (come0, come1)]
        upper = [ref[0, CUT:, by] for ref in (come0, come1)]
        results = products(lower, upper, 1, wd_ref[j * PAIR : (j + 1) * PAIR, :])
        totals = results if j == 0 else [a + b for a, b in zip(totals, results)]
    pieces = (early_ref[0], early_ref[1] + totals[2], early_ref[2] + totals[1], totals[0])
    mixed = jnp.concatenate([piece.astype(BF) for piece in pieces], axis=0)
    rows = rows_ref[0:1, :]
    slot = lax.broadcasted_iota(jnp.int32, (BLK, LIVE), 0)
    for k in range(8):
        pick = picked(rows, offs, cnts, k, slot)
        target = near_ref if k < 4 else away_ref
        target[k % 4] = jnp.dot(pick, mixed, preferred_element_type=F32).astype(BF)


def last_output(rows, offs, cnts, early, wd, hidden_come):
    return call(
        last_output_kernel,
        "last_output",
        1,
        1 << 12,
        grid=(1,),
        out_shape=(jax.ShapeDtypeStruct((4, BLK, FEAT), BF),) * 2,
        in_specs=[
            whole((1, LIVE)),
            whole((8, 8, BLK)),
            whole((8, 8, BLK)),
            whole((3, CUT, FEAT)),
            whole((UNITS, FEAT)),
        ]
        + [whole((1, 2 * CUT, HALF))] * 2,
        out_specs=(whole((4, BLK, FEAT)),) * 2,
    )(rows, offs, cnts, early, wd, *hidden_come)


def all_rows(owns, comes, which):
    left = jnp.concatenate([owns[0][which], comes[0][which]], axis=0)
    right = jnp.concatenate(
        [ref[which, i : i + CUT] for i in (0, CUT) for ref in (owns[1], comes[1])], axis=0
    )
    return jnp.concatenate([left, right], axis=1)


def down_kernel(dm, g_ref, own0, own1, come0, come1, down_out):
    j = pl.program_id(0)
    down = lax.dot_general(
        all_rows((own0, own1), (come0, come1), 0),
        g_ref[...],
        (((0,), (0,)), ((), ())),
        preferred_element_type=F32,
    )
    for r in range(4):
        for b in range(2):
            at, by = slice(r * BLK, (r + 1) * BLK), slice(b * BLK, (b + 1) * BLK)
            down_out[by, at] = kept(dm, 2 * j + b, r, down[by, at])


def down_gradient(dm, g, parts):
    return call(
        down_kernel,
        "down_gradient",
        1,
        1 << 12,
        grid=(STEPS,),
        out_shape=jax.ShapeDtypeStruct((UNITS, FEAT), F32),
        in_specs=[smem(), whole((LIVE, FEAT))]
        + [pl.BlockSpec((1, 2 * CUT, BLK), lambda j: (0, 0, j))] * 4,
        out_specs=pl.BlockSpec((PAIR, FEAT), lambda j: (j, 0)),
    )(dm, g, *parts)


def grad_kernel(gm, um, xt_ref, own0, own1, come0, come1, gate_out, up_out):
    j = pl.program_id(0)
    xt = xt_ref[...]
    for which, mask, target in ((0, gm, gate_out), (1, um, up_out)):
        rows = all_rows((own0, own1), (come0, come1), which)
        grad = jnp.dot(xt, rows, preferred_element_type=F32)
        for r in range(4):
            for b in range(2):
                at, by = slice(r * BLK, (r + 1) * BLK), slice(b * BLK, (b + 1) * BLK)
                target[at, by] = kept(mask, r, 2 * j + b, grad[at, by])


def gradients(gm, um, xt, parts):
    return call(
        grad_kernel,
        "gradients",
        2 * LIVE * FEAT * 2 * UNITS,
        13 << 20,
        grid=(STEPS,),
        out_shape=(jax.ShapeDtypeStruct((FEAT, UNITS), F32),) * 2,
        in_specs=[smem(), smem(), whole((FEAT, LIVE))]
        + [pl.BlockSpec((2, 2 * CUT, BLK), lambda j: (0, 0, j))] * 4,
        out_specs=(pl.BlockSpec((FEAT, PAIR), lambda j: (0, j)),) * 2,
    )(gm, um, xt, *parts)


def split(value, axis):
    lower = lax.slice_in_dim(value, 0, 1, axis=axis)
    upper = lax.slice_in_dim(value, 1, 2, axis=axis)
    return lower, upper


def activate(total):
    gate, upward, back = total[0], total[1], total[2]
    sigma = jax.nn.sigmoid(gate)
    active = gate * sigma
    hidden = (active * upward).astype(BF)
    d_gate = (back * upward * sigma * (1.0 + gate * (1.0 - sigma))).astype(BF)
    d_up = (back * active).astype(BF)
    return jnp.stack([d_gate, d_up, hidden])


def exchange(values, number):
    return [
        lax.ppermute(values[q], ("col", "dp"), partners(ROUNDS[q][number][1])) for q in SIDES
    ]


def on_device(
    tokens, cotangent, gate_weight, up_weight, down_weight, gate_mask, up_mask, down_mask, counts
):
    live = (lax.iota(jnp.int32, tokens.shape[0]) < counts[0])[:, None]
    place = lax.axis_index("col")
    order = jnp.arange(8)
    shard = ((place // 2 + order % 4) % SIDE) * 2 + ((place % 2) ^ (order // 4))
    own = pack(tokens, cotangent, counts)
    column = [own] + [lax.ppermute(own, "col", shift(-dz, 0)) for dz in (1, 2, 3)]
    beside = [lax.ppermute(own, "col", shift(0, 1))]
    wx, wdt, wd = prepare(gate_mask, up_mask, down_mask, gate_weight, up_weight, down_weight)
    rows = logical_rows()
    *column, wx, wdt, wd, rows_down, rows_along, shard = lax.optimization_barrier(
        (*column, wx, wdt, wd, rows[:, None], rows[None, :], shard)
    )
    beside += [lax.ppermute(value, "col", shift(0, 1)) for value in column[1:]]
    x, g, xt, offs, cnts = compact(shard, rows_down, column + beside)

    early = partials(FIRST, 1, x, g, wx, wdt)
    come_early = exchange(early, 0)
    x_rest, g_rest, *_ = lax.optimization_barrier((x, g, *early))
    late = partials(0, 3, x_rest, g_rest, wx, wdt)
    zero = [late[q] for q in SIDES]
    side = [[late[2 * (2 - ROUNDS[q][n][0]) + q] for q in SIDES] for n in range(2)]
    come_rest = exchange(side[0], 0)
    come_early = lax.optimization_barrier(come_early)
    second = [
        (side[1][q].astype(F32) + come_early[q].astype(F32)).astype(BF) for q in SIDES
    ]
    come_second = exchange(second, 1)
    *come_rest, last0, last1 = lax.optimization_barrier((*come_rest, *come_second))
    come_second = [last0, last1]
    keep, send = [None] * 2, [None] * 2
    for q in SIDES:
        total = (
            zero[q].astype(F32) + come_rest[q].astype(F32) + come_second[q].astype(F32)
        ).reshape(3, 2, 2, 48, HALF)
        keep[q], upper = split(total, ROUNDS[q][2][0] - 1)
        send[q] = upper.astype(BF)
    come = exchange(send, 2)
    keep = [(keep[q] + come[q].astype(F32)).astype(BF) for q in SIDES]
    come = exchange(keep, 3)
    held = []
    for q in SIDES:
        axis = ROUNDS[q][3][0] - 1
        lower, upper = split(come[q], axis)
        arrived = jnp.concatenate([upper, lower], axis=axis)
        held.append(activate(keep[q].astype(F32) + arrived.astype(F32)))
    come = exchange(held, 2)
    held = [
        jnp.concatenate([held[q], come[q]], axis=ROUNDS[q][2][0] - 1).reshape(3, CUT, HALF)
        for q in SIDES
    ]
    near = exchange(held, 1)
    hidden_own = [jnp.concatenate([held[q][2:], near[q][2:]], axis=1) for q in SIDES]
    derived_own = [jnp.concatenate([held[q][:2], near[q][:2]], axis=1) for q in SIDES]
    hidden_come = exchange(hidden_own, 0)
    derived_come = exchange(derived_own, 0)

    begun = first_output(wd, hidden_own)
    mine, away = last_output(rows_along, offs, cnts, begun, wd, hidden_come)
    other = lax.ppermute(away, "col", shift(0, 1))
    down_grad = down_gradient(down_mask, g, hidden_own + hidden_come)
    other, down_grad = lax.optimization_barrier((other, down_grad))
    summed = mine.astype(F32) + other.astype(F32)
    terms = [summed[k].astype(BF) for k in range(4)]
    arrived = [lax.ppermute(terms[dz], "col", shift(dz, 0)) for dz in (1, 2, 3)]
    gate_grad, up_grad = gradients(gate_mask, up_mask, xt, derived_own + derived_come)
    *arrived, gate_grad, up_grad = lax.optimization_barrier((*arrived, gate_grad, up_grad))
    mixed = sum((term.astype(F32) for term in arrived), terms[0].astype(F32))
    output = jnp.where(live, mixed, jnp.zeros_like(mixed)).astype(BF)
    return (output, gate_grad, up_grad, down_grad)


def solution(mesh):
    in_specs = (
        P("col", "dp"),
        P("col", "dp"),
        P("dp", "col"),
        P("dp", "col"),
        P("col", "dp"),
        P("dp", "col"),
        P("dp", "col"),
        P("col", "dp"),
        P("col"),
    )
    out_specs = (P("col", "dp"), P("dp", "col"), P("dp", "col"), P("col", "dp"))
    return jax.shard_map(
        on_device, mesh=mesh, in_specs=in_specs, out_specs=out_specs, check_vma=False
    )
```

```python
import functools

import jax
import jax.numpy as jnp
from jax import lax
from jax.experimental import pallas as pl
from jax.experimental.pallas import tpu as pltpu
from jax.sharding import PartitionSpec as P

BF = jnp.bfloat16
F32 = jnp.float32
LIVE = 768
PAD = 144
SIDE = 4
BLK = 128
PAIR = 2 * BLK
UNITS = 1792
HALF = UNITS // 2
STEPS = UNITS // PAIR
FEAT = 512
SLOTS = 1024
CUT = 192
FIRST = 576
LAST = LIVE - FIRST
VMEM = 32 << 20

MASKS = {"xA": (1, 0), "xB": (3, 0), "yA": (0, 1), "yB": (0, 3)}
ROUNDS = (
    ((0, ("xA", "yA")), (1, ("xB", "yB")), (2, ("yA", "xA")), (3, ("yB", "xB"))),
    ((1, ("xB", "yB")), (0, ("xA", "yA")), (3, ("yB", "xB")), (2, ("yA", "xA"))),
)
SIDES = (0, 1)


def partners(names):
    pairs = []
    for col in range(2 * SIDE):
        dx, dy = MASKS[names[col % 2]]
        for x in range(SIDE):
            for y in range(SIDE):
                start = (col * SIDE + x) * SIDE + y
                pairs.append((start, (col * SIDE + (x ^ dx)) * SIDE + (y ^ dy)))
    return pairs


def shift(dz, dc):
    return [
        (z * 2 + c, ((z + dz) % SIDE) * 2 + (c + dc) % 2) for z in range(SIDE) for c in range(2)
    ]


def logical_rows():
    place = lax.axis_index("dp")
    x, y = place // SIDE, place % SIDE

    def sides(v):
        high = v // 2
        return (v % 2) ^ high, high

    xa, xb = sides(x)
    ya, yb = sides(y)
    first = xa * 8 + xb * 4 + ya * 2 + yb
    second = ya * 8 + yb * 4 + xa * 2 + xb
    mask = jnp.where(lax.axis_index("col") % 2 > 0, second, first)
    row = lax.iota(jnp.int32, LIVE)
    return ((row // 48) ^ mask) * 48 + row % 48


def kept(mask_ref, row, col, value):
    return jnp.where(mask_ref[row, col] > 0, value, jnp.zeros_like(value))


def smem():
    return pl.BlockSpec(memory_space=pltpu.SMEM)


def whole(shape):
    return pl.BlockSpec(shape, lambda j: (0,) * len(shape))


def call(kernel, name, flops, moved, **rest):
    return pl.pallas_call(
        kernel,
        compiler_params=pltpu.CompilerParams(vmem_limit_bytes=VMEM),
        cost_estimate=pl.CostEstimate(flops=flops, bytes_accessed=moved, transcendentals=0),
        name=name,
        **rest,
    )


def pack_kernel(tok_ref, count_ref, out_ref):
    out_ref[:BLK, :] = tok_ref[...]
    count = jnp.full((PAD - BLK, FEAT), count_ref[0], jnp.int32)
    out_ref[BLK:, :] = count.astype(F32).astype(BF)


def pack(tokens, counts):
    return call(
        pack_kernel,
        "pack",
        0,
        1 << 18,
        out_shape=jax.ShapeDtypeStruct((PAD, FEAT), BF),
        grid=(1,),
        in_specs=[whole((BLK, FEAT)), smem()],
        out_specs=whole((PAD, FEAT)),
    )(tokens, counts)


def prepare_kernel(gm, um, dm, wg, wu, wd, wg_ref, wu_ref, wdt_ref, wd_ref):
    j = pl.program_id(0)
    for mask, ref, target in ((gm, wg, wg_ref), (um, wu, wu_ref)):
        for r in range(4):
            for b in range(2):
                at = slice(r * BLK, (r + 1) * BLK)
                by = slice(b * BLK, (b + 1) * BLK)
                target[0, at, by] = kept(mask, r, 2 * j + b, ref[at, by])
    down = jnp.concatenate(
        [
            jnp.concatenate(
                [
                    kept(dm, 2 * j + b, c, wd[b * BLK : (b + 1) * BLK, c * BLK : (c + 1) * BLK])
                    for c in range(4)
                ],
                axis=1,
            )
            for b in range(2)
        ],
        axis=0,
    )
    wd_ref[...] = down
    wdt_ref[0] = down.T


def prepare(gm, um, dm, wg, wu, wd):
    return call(
        prepare_kernel,
        "prepare",
        0,
        13 << 20,
        grid=(STEPS,),
        out_shape=(
            jax.ShapeDtypeStruct((STEPS, FEAT, PAIR), BF),
            jax.ShapeDtypeStruct((STEPS, FEAT, PAIR), BF),
            jax.ShapeDtypeStruct((STEPS, FEAT, PAIR), BF),
            jax.ShapeDtypeStruct((UNITS, FEAT), BF),
        ),
        in_specs=[
            smem(),
            smem(),
            smem(),
            pl.BlockSpec((FEAT, PAIR), lambda j: (0, j)),
            pl.BlockSpec((FEAT, PAIR), lambda j: (0, j)),
            pl.BlockSpec((PAIR, FEAT), lambda j: (j, 0)),
        ],
        out_specs=(
            pl.BlockSpec((1, FEAT, PAIR), lambda j: (j, 0, 0)),
            pl.BlockSpec((1, FEAT, PAIR), lambda j: (j, 0, 0)),
            pl.BlockSpec((1, FEAT, PAIR), lambda j: (j, 0, 0)),
            pl.BlockSpec((PAIR, FEAT), lambda j: (j, 0)),
        ),
    )(gm, um, dm, wg, wu, wd)


def picked(rows, offset, count, slot):
    hit = (rows - offset == slot) & (slot < count)
    return jnp.where(hit, 1.0, 0.0).astype(BF)


def gathered_rows(rows, offs, cnts, sources):
    slot = lax.broadcasted_iota(jnp.int32, (LIVE, BLK), 1)
    total = None
    for k in range(0, 8, 2):
        pick = jnp.concatenate(
            [picked(rows, offs[i], cnts[i], slot) for i in (k, k + 1)], axis=1
        )
        source = jnp.concatenate([sources[i][:BLK, :] for i in (k, k + 1)], axis=0)
        part = jnp.dot(pick, source, preferred_element_type=F32)
        total = part if total is None else total + part
    return total


def compact_tokens_kernel(shard, rows_ref, *refs):
    sources, (x_ref, xt_ref, offs_ref, cnts_ref) = refs[:8], refs[8:]
    cnts = [ref[BLK : BLK + 1, 0:1].astype(F32).astype(jnp.int32) for ref in sources]
    offs = []
    for k in range(8):
        offset = jnp.zeros((1, 1), jnp.int32)
        for other in range(8):
            if other != k:
                offset += jnp.where(shard[other] < shard[k], cnts[other], 0)
        offs.append(offset)
        offs_ref[k] = jnp.broadcast_to(offset, (8, BLK))
        cnts_ref[k] = jnp.broadcast_to(cnts[k], (8, BLK))
    total = gathered_rows(rows_ref[...], offs, cnts, sources)
    x_ref[...] = total.astype(BF)
    xt_ref[...] = total.T.astype(BF)


def compact_tokens(shard, rows, sources):
    vmem = pl.BlockSpec(memory_space=pltpu.VMEM)
    return call(
        compact_tokens_kernel,
        "compact_tokens",
        2 * LIVE * SLOTS * FEAT,
        3 << 20,
        out_shape=(
            jax.ShapeDtypeStruct((LIVE, FEAT), BF),
            jax.ShapeDtypeStruct((FEAT, LIVE), BF),
            jax.ShapeDtypeStruct((8, 8, BLK), jnp.int32),
            jax.ShapeDtypeStruct((8, 8, BLK), jnp.int32),
        ),
        in_specs=[smem(), vmem] + [vmem] * 8,
        out_specs=(vmem,) * 4,
    )(shard, rows, *sources)


def compact_kernel(rows_ref, offs, cnts, *refs):
    sources, g_ref = refs[:8], refs[8]
    starts = [offs[k, 0:1, 0:1] for k in range(8)]
    sizes = [cnts[k, 0:1, 0:1] for k in range(8)]
    g_ref[...] = gathered_rows(rows_ref[...], starts, sizes, sources).astype(BF)


def compact_cotangent(rows, offs, cnts, sources):
    vmem = pl.BlockSpec(memory_space=pltpu.VMEM)
    return call(
        compact_kernel,
        "compact_cotangent",
        1,
        1 << 12,
        out_shape=jax.ShapeDtypeStruct((LIVE, FEAT), BF),
        in_specs=[vmem] * 11,
        out_specs=vmem,
    )(rows, offs, cnts, *sources)


SENT = ((2, 3), (1, 3))
KEPT = ((0, 1), (0, 2))


def partial_kernel(pieces, planes, *refs):
    operands, weights = refs[:planes], refs[planes : 2 * planes]
    outs, rows = refs[2 * planes : 2 * planes + 2], refs[2 * planes + 2]

    @pl.when(pl.program_id(0) == 0)
    def _():
        for which, ref in enumerate(operands):
            for q in SIDES:
                for i, piece in enumerate(pieces[q]):
                    to, at = slice(i * CUT, (i + 1) * CUT), slice(piece * CUT, (piece + 1) * CUT)
                    rows[2 * which + q, to, :] = ref[at, :]

    for which, w_ref in enumerate(weights):
        for q, out in enumerate(outs):
            out[which] = jnp.dot(
                rows[2 * which + q],
                w_ref[0, :, q * BLK : (q + 1) * BLK],
                preferred_element_type=F32,
            ).astype(BF)


def partials(pieces, operands, weights):
    planes = len(operands)
    return call(
        functools.partial(partial_kernel, pieces, planes),
        "partials",
        1,
        1 << 12,
        grid=(STEPS,),
        out_shape=(jax.ShapeDtypeStruct((planes, 2 * CUT, HALF), BF),) * 2,
        in_specs=[whole((LIVE, FEAT))] * planes
        + [pl.BlockSpec((1, FEAT, PAIR), lambda j: (j, 0, 0))] * planes,
        out_specs=(pl.BlockSpec((planes, 2 * CUT, BLK), lambda j: (0, 0, j)),) * 2,
        scratch_shapes=[pltpu.VMEM((2 * planes, 2 * CUT, FEAT), BF)],
    )(*operands, *weights)


def products(lower, upper, shared, w_down):
    both, single = (lower, upper) if shared == 0 else (upper, lower)
    result = [
        jnp.dot(jnp.concatenate(both, axis=1), w_down, preferred_element_type=F32)
    ]
    for q in SIDES:
        result.append(
            jnp.dot(single[q], w_down[q * BLK : (q + 1) * BLK, :], preferred_element_type=F32)
        )
    return result


def first_output_kernel(wd_ref, own0, own1, total):
    j = pl.program_id(0)
    lower = [ref[0, :CUT, :] for ref in (own0, own1)]
    upper = [ref[0, CUT:, :] for ref in (own0, own1)]
    results = products(lower, upper, 0, wd_ref[...])

    @pl.when(j == 0)
    def _():
        for i in range(3):
            total[i] = results[i]

    @pl.when(j > 0)
    def _():
        for i in range(3):
            total[i] += results[i]


def first_output(wd, hidden_own):
    return call(
        first_output_kernel,
        "first_output",
        1,
        1 << 12,
        grid=(STEPS,),
        out_shape=jax.ShapeDtypeStruct((3, CUT, FEAT), F32),
        in_specs=[pl.BlockSpec((PAIR, FEAT), lambda j: (j, 0))]
        + [pl.BlockSpec((1, 2 * CUT, BLK), lambda j: (0, 0, j))] * 2,
        out_specs=whole((3, CUT, FEAT)),
    )(wd, *hidden_own)


def last_output_kernel(rows_ref, offs, cnts, early_ref, wd_ref, come0, come1, near_ref, away_ref):
    totals = None
    for j in range(STEPS):
        by = slice(j * BLK, (j + 1) * BLK)
        lower = [ref[0, :CUT, by] for ref in (come0, come1)]
        upper = [ref[0, CUT:, by] for ref in (come0, come1)]
        results = products(lower, upper, 1, wd_ref[j * PAIR : (j + 1) * PAIR, :])
        totals = results if j == 0 else [a + b for a, b in zip(totals, results)]
    pieces = (early_ref[0], early_ref[1] + totals[2], early_ref[2] + totals[1], totals[0])
    mixed = jnp.concatenate([piece.astype(BF) for piece in pieces], axis=0)
    rows = rows_ref[0:1, :]
    slot = lax.broadcasted_iota(jnp.int32, (BLK, LIVE), 0)
    for k in range(8):
        pick = picked(rows, offs[k, 0:1, 0:1], cnts[k, 0:1, 0:1], slot)
        target = near_ref if k < 4 else away_ref
        target[k % 4] = jnp.dot(pick, mixed, preferred_element_type=F32).astype(BF)


def last_output(rows, offs, cnts, early, wd, hidden_come):
    return call(
        last_output_kernel,
        "last_output",
        1,
        1 << 12,
        grid=(1,),
        out_shape=(jax.ShapeDtypeStruct((4, BLK, FEAT), BF),) * 2,
        in_specs=[
            whole((1, LIVE)),
            whole((8, 8, BLK)),
            whole((8, 8, BLK)),
            whole((3, CUT, FEAT)),
            whole((UNITS, FEAT)),
        ]
        + [whole((1, 2 * CUT, HALF))] * 2,
        out_specs=(whole((4, BLK, FEAT)),) * 2,
    )(rows, offs, cnts, early, wd, *hidden_come)


def all_rows(owns, comes, which):
    left = jnp.concatenate([owns[0][which], comes[0][which]], axis=0)
    right = jnp.concatenate(
        [ref[which, i : i + CUT] for i in (0, CUT) for ref in (owns[1], comes[1])], axis=0
    )
    return jnp.concatenate([left, right], axis=1)


def down_kernel(dm, g_ref, own0, own1, come0, come1, down_out):
    j = pl.program_id(0)
    down = lax.dot_general(
        all_rows((own0, own1), (come0, come1), 0),
        g_ref[...],
        (((0,), (0,)), ((), ())),
        preferred_element_type=F32,
    )
    for r in range(4):
        for b in range(2):
            at, by = slice(r * BLK, (r + 1) * BLK), slice(b * BLK, (b + 1) * BLK)
            down_out[by, at] = kept(dm, 2 * j + b, r, down[by, at])


def down_gradient(dm, g, parts):
    return call(
        down_kernel,
        "down_gradient",
        1,
        1 << 12,
        grid=(STEPS,),
        out_shape=jax.ShapeDtypeStruct((UNITS, FEAT), F32),
        in_specs=[smem(), whole((LIVE, FEAT))]
        + [pl.BlockSpec((1, 2 * CUT, BLK), lambda j: (0, 0, j))] * 4,
        out_specs=pl.BlockSpec((PAIR, FEAT), lambda j: (j, 0)),
    )(dm, g, *parts)


def grad_kernel(gm, um, xt_ref, own0, own1, come0, come1, gate_out, up_out):
    j = pl.program_id(0)
    xt = xt_ref[...]
    for which, mask, target in ((0, gm, gate_out), (1, um, up_out)):
        rows = all_rows((own0, own1), (come0, come1), which)
        grad = jnp.dot(xt, rows, preferred_element_type=F32)
        for r in range(4):
            for b in range(2):
                at, by = slice(r * BLK, (r + 1) * BLK), slice(b * BLK, (b + 1) * BLK)
                target[at, by] = kept(mask, r, 2 * j + b, grad[at, by])


def gradients(gm, um, xt, parts):
    return call(
        grad_kernel,
        "gradients",
        2 * LIVE * FEAT * 2 * UNITS,
        13 << 20,
        grid=(STEPS,),
        out_shape=(jax.ShapeDtypeStruct((FEAT, UNITS), F32),) * 2,
        in_specs=[smem(), smem(), whole((FEAT, LIVE))]
        + [pl.BlockSpec((2, 2 * CUT, BLK), lambda j: (0, 0, j))] * 4,
        out_specs=(pl.BlockSpec((FEAT, PAIR), lambda j: (0, j)),) * 2,
    )(gm, um, xt, *parts)


def split(value, axis):
    lower = lax.slice_in_dim(value, 0, 1, axis=axis)
    upper = lax.slice_in_dim(value, 1, 2, axis=axis)
    return lower, upper


def activate(gate, upward, back):
    sigma = jax.nn.sigmoid(gate)
    active = gate * sigma
    d_gate = (back * upward * sigma * (1.0 + gate * (1.0 - sigma))).astype(BF)
    d_up = (back * active).astype(BF)
    hidden = (active * upward).astype(BF)
    return hidden[None], jnp.stack([d_gate, d_up])


def exchange(values, number):
    come = [
        lax.ppermute(values[q], ("col", "dp"), partners(ROUNDS[q][number][1])) for q in SIDES
    ]
    return lax.optimization_barrier(come)


def tie(*lists):
    flat = iter(lax.optimization_barrier([value for values in lists for value in values]))
    return [[next(flat) for _ in values] for values in lists]


def widened(value):
    return value.astype(F32)


def halve(keep, come, planes, number):
    kept_rows, send = [], []
    for q in SIDES:
        total = widened(keep[q]) + widened(come[q])
        if number == 1:
            total, axis = total.reshape(planes, 2, CUT, HALF), 1
        else:
            total, axis = total.reshape(planes, 2, 2, 48, HALF), ROUNDS[q][2][0] - 1
        lower, upper = split(total, axis)
        kept_rows.append(lower)
        send.append(upper.astype(BF))
    return kept_rows, send


def met(keep, come):
    totals = []
    for q in SIDES:
        axis = ROUNDS[q][3][0] - 1
        lower, upper = split(come[q], axis)
        arrived = jnp.concatenate([upper, lower], axis=axis)
        totals.append(widened(keep[q]) + widened(arrived))
    return totals


def on_device(
    tokens, cotangent, gate_weight, up_weight, down_weight, gate_mask, up_mask, down_mask, counts
):
    live = (lax.iota(jnp.int32, tokens.shape[0]) < counts[0])[:, None]
    place = lax.axis_index("col")
    order = jnp.arange(8)
    shard = ((place // 2 + order % 4) % SIDE) * 2 + ((place % 2) ^ (order // 4))
    own = pack(tokens, counts)
    column = [own] + [lax.ppermute(own, "col", shift(-dz, 0)) for dz in (1, 2, 3)]
    beside = [lax.ppermute(own, "col", shift(0, 1))]
    wg, wu, wdt, wd = prepare(gate_mask, up_mask, down_mask, gate_weight, up_weight, down_weight)
    rows = logical_rows()
    *column, wg, wu, wdt, wd, rows_down, rows_along, shard, cotangent = lax.optimization_barrier(
        (*column, wg, wu, wdt, wd, rows[:, None], rows[None, :], shard, cotangent)
    )
    beside += [lax.ppermute(value, "col", shift(0, 1)) for value in column[1:]]
    cot_column = [cotangent]
    cot_column += [lax.ppermute(cotangent, "col", shift(-dz, 0)) for dz in (1, 2, 3)]
    x, xt, offs, cnts = compact_tokens(shard, rows_down, column + beside)
    lead_send = partials(SENT, [x], [wg])
    lead_come = exchange(lead_send, 0)
    cot_column, _ = tie(cot_column, lead_send)
    cot_beside = [lax.ppermute(value, "col", shift(0, 1)) for value in cot_column]
    g = compact_cotangent(rows_down, offs, cnts, cot_column + cot_beside)
    next_send = partials(SENT, [x, g], [wu, wdt])
    next_come = exchange(next_send, 0)
    x_rest, g_rest, *_ = lax.optimization_barrier((x, g, *lead_send, *next_send))
    lead_keep = partials(KEPT, [x_rest], [wg])
    next_keep = partials(KEPT, [x_rest, g_rest], [wu, wdt])

    for number in (1, 2):
        lead_keep, lead_send = halve(lead_keep, lead_come, 1, number)
        lead_come = exchange(lead_send, number)
        next_keep, next_send = halve(next_keep, next_come, 2, number)
        next_come = exchange(next_send, number)
    lead_keep = [(lead_keep[q] + widened(lead_come[q])).astype(BF) for q in SIDES]
    lead_come = exchange(lead_keep, 3)
    next_keep = [(next_keep[q] + widened(next_come[q])).astype(BF) for q in SIDES]
    next_come = exchange(next_keep, 3)
    gate = met(lead_keep, lead_come)
    rest = met(next_keep, next_come)
    hidden, derived = [], []
    for q in SIDES:
        first, second = activate(gate[q][0], rest[q][0], rest[q][1])
        hidden.append(first)
        derived.append(second)
    hidden_come = exchange(hidden, 2)
    derived_come = exchange(derived, 2)

    def joined(own_rows, come_rows, planes):
        return [
            jnp.concatenate(
                [own_rows[q], come_rows[q]], axis=ROUNDS[q][2][0] - 1
            ).reshape(planes, CUT, HALF)
            for q in SIDES
        ]

    hidden = joined(hidden, hidden_come, 1)
    near = exchange(hidden, 1)
    derived = joined(derived, derived_come, 2)
    derived_near = exchange(derived, 1)
    hidden_own = [jnp.concatenate([hidden[q], near[q]], axis=1) for q in SIDES]
    hidden_come = exchange(hidden_own, 0)
    derived_own = [jnp.concatenate([derived[q], derived_near[q]], axis=1) for q in SIDES]
    derived_come = exchange(derived_own, 0)

    begun = first_output(wd, hidden_own)
    mine, away = last_output(rows_along, offs, cnts, begun, wd, hidden_come)
    other = lax.ppermute(away, "col", shift(0, 1))
    down_grad = down_gradient(down_mask, g, hidden_own + hidden_come)
    other, down_grad = lax.optimization_barrier((other, down_grad))
    summed = mine.astype(F32) + other.astype(F32)
    terms = [summed[k].astype(BF) for k in range(4)]
    arrived = [lax.ppermute(terms[dz], "col", shift(dz, 0)) for dz in (1, 2, 3)]
    gate_grad, up_grad = gradients(gate_mask, up_mask, xt, derived_own + derived_come)
    *arrived, gate_grad, up_grad = lax.optimization_barrier((*arrived, gate_grad, up_grad))
    mixed = sum((term.astype(F32) for term in arrived), terms[0].astype(F32))
    output = jnp.where(live, mixed, jnp.zeros_like(mixed)).astype(BF)
    return (output, gate_grad, up_grad, down_grad)


def solution(mesh):
    in_specs = (
        P("col", "dp"),
        P("col", "dp"),
        P("dp", "col"),
        P("dp", "col"),
        P("col", "dp"),
        P("dp", "col"),
        P("dp", "col"),
        P("col", "dp"),
        P("col"),
    )
    out_specs = (P("col", "dp"), P("dp", "col"), P("dp", "col"), P("col", "dp"))
    return jax.shard_map(
        on_device, mesh=mesh, in_specs=in_specs, out_specs=out_specs, check_vma=False
    )
```

```python
import functools

import jax
import jax.numpy as jnp
from jax import lax
from jax.experimental import pallas as pl
from jax.experimental.pallas import tpu as pltpu
from jax.sharding import PartitionSpec as P

BF = jnp.bfloat16
F32 = jnp.float32
LIVE = 768
PAD = 144
SIDE = 4
BLK = 128
PAIR = 2 * BLK
UNITS = 1792
HALF = UNITS // 2
STEPS = UNITS // PAIR
FEAT = 512
SLOTS = 1024
CUT = 192
FIRST = 576
LAST = LIVE - FIRST
VMEM = 32 << 20

MASKS = {"xA": (1, 0), "xB": (3, 0), "yA": (0, 1), "yB": (0, 3)}
ROUNDS = (
    ((0, ("xA", "yA")), (1, ("xB", "yB")), (2, ("yA", "xA")), (3, ("yB", "xB"))),
    ((1, ("xB", "yB")), (0, ("xA", "yA")), (3, ("yB", "xB")), (2, ("yA", "xA"))),
)
SIDES = (0, 1)


def partners(names):
    pairs = []
    for col in range(2 * SIDE):
        dx, dy = MASKS[names[col % 2]]
        for x in range(SIDE):
            for y in range(SIDE):
                start = (col * SIDE + x) * SIDE + y
                pairs.append((start, (col * SIDE + (x ^ dx)) * SIDE + (y ^ dy)))
    return pairs


def shift(dz, dc):
    return [
        (z * 2 + c, ((z + dz) % SIDE) * 2 + (c + dc) % 2) for z in range(SIDE) for c in range(2)
    ]


def logical_rows():
    place = lax.axis_index("dp")
    x, y = place // SIDE, place % SIDE

    def sides(v):
        high = v // 2
        return (v % 2) ^ high, high

    xa, xb = sides(x)
    ya, yb = sides(y)
    first = xa * 8 + xb * 4 + ya * 2 + yb
    second = ya * 8 + yb * 4 + xa * 2 + xb
    mask = jnp.where(lax.axis_index("col") % 2 > 0, second, first)
    row = lax.iota(jnp.int32, LIVE)
    return ((row // 48) ^ mask) * 48 + row % 48


def kept(mask_ref, row, col, value):
    return jnp.where(mask_ref[row, col] > 0, value, jnp.zeros_like(value))


def smem():
    return pl.BlockSpec(memory_space=pltpu.SMEM)


def whole(shape):
    return pl.BlockSpec(shape, lambda j: (0,) * len(shape))


def call(kernel, name, flops, moved, **rest):
    return pl.pallas_call(
        kernel,
        compiler_params=pltpu.CompilerParams(vmem_limit_bytes=VMEM),
        cost_estimate=pl.CostEstimate(flops=flops, bytes_accessed=moved, transcendentals=0),
        name=name,
        **rest,
    )


def pack_kernel(tok_ref, cot_ref, count_ref, out_ref, sems):
    copies = [
        pltpu.make_async_copy(
            ref, out_ref.at[pl.ds(0, BLK), pl.ds(i * FEAT, FEAT)], sems.at[i]
        )
        for i, ref in enumerate((tok_ref, cot_ref))
    ]
    for copy in copies:
        copy.start()
    count = jnp.full((PAD - BLK, 2 * FEAT), count_ref[0], jnp.int32)
    out_ref[BLK:, :] = count.astype(F32).astype(BF)
    for copy in copies:
        copy.wait()


def pack(tokens, cotangent, counts):
    return call(
        pack_kernel,
        "pack",
        0,
        1 << 19,
        out_shape=jax.ShapeDtypeStruct((PAD, 2 * FEAT), BF),
        in_specs=[pl.BlockSpec(memory_space=pl.ANY)] * 2 + [smem()],
        out_specs=pl.BlockSpec(memory_space=pltpu.VMEM),
        scratch_shapes=[pltpu.SemaphoreType.DMA((2,))],
    )(tokens, cotangent, counts)


def prepare_kernel(gm, um, dm, wg, wu, wd, wx_ref, wdt_ref, wd_ref):
    j = pl.program_id(0)
    for which, (mask, ref) in enumerate(((gm, wg), (um, wu))):
        for r in range(4):
            for b in range(2):
                at = slice(r * BLK, (r + 1) * BLK)
                wx_ref[0, at, which * PAIR + b * BLK : which * PAIR + (b + 1) * BLK] = kept(
                    mask, r, 2 * j + b, ref[at, b * BLK : (b + 1) * BLK]
                )
    down = jnp.concatenate(
        [
            jnp.concatenate(
                [
                    kept(dm, 2 * j + b, c, wd[b * BLK : (b + 1) * BLK, c * BLK : (c + 1) * BLK])
                    for c in range(4)
                ],
                axis=1,
            )
            for b in range(2)
        ],
        axis=0,
    )
    wd_ref[...] = down
    wdt_ref[0] = down.T


def prepare(gm, um, dm, wg, wu, wd):
    return call(
        prepare_kernel,
        "prepare",
        0,
        13 << 20,
        grid=(STEPS,),
        out_shape=(
            jax.ShapeDtypeStruct((STEPS, FEAT, 2 * PAIR), BF),
            jax.ShapeDtypeStruct((STEPS, FEAT, PAIR), BF),
            jax.ShapeDtypeStruct((UNITS, FEAT), BF),
        ),
        in_specs=[
            smem(),
            smem(),
            smem(),
            pl.BlockSpec((FEAT, PAIR), lambda j: (0, j)),
            pl.BlockSpec((FEAT, PAIR), lambda j: (0, j)),
            pl.BlockSpec((PAIR, FEAT), lambda j: (j, 0)),
        ],
        out_specs=(
            pl.BlockSpec((1, FEAT, 2 * PAIR), lambda j: (j, 0, 0)),
            pl.BlockSpec((1, FEAT, PAIR), lambda j: (j, 0, 0)),
            pl.BlockSpec((PAIR, FEAT), lambda j: (j, 0)),
        ),
    )(gm, um, dm, wg, wu, wd)


def compact_kernel(shard, rows_ref, *refs):
    sources, (x_ref, g_ref, offs_ref, cnts_ref) = refs[:8], refs[8:]
    rows = rows_ref[...]
    slot = lax.broadcasted_iota(jnp.int32, (LIVE, BLK), 1)
    cnts = [ref[BLK : BLK + 1, 0:1].astype(F32).astype(jnp.int32) for ref in sources]
    total = None
    for pair in range(4):
        picks = []
        for k in (2 * pair, 2 * pair + 1):
            offset = jnp.zeros((1, 1), jnp.int32)
            for other in range(8):
                if other != k:
                    offset += jnp.where(shard[other] < shard[k], cnts[other], 0)
            offs_ref[k] = jnp.broadcast_to(offset, (8, BLK))
            cnts_ref[k] = jnp.broadcast_to(cnts[k], (8, BLK))
            hit = (rows - offset == slot) & (slot < cnts[k])
            picks.append(jnp.where(hit, 1.0, 0.0).astype(BF))
        source = jnp.concatenate(
            [sources[2 * pair][:BLK, :], sources[2 * pair + 1][:BLK, :]], axis=0
        )
        part = jnp.dot(jnp.concatenate(picks, axis=1), source, preferred_element_type=F32)
        total = part if total is None else total + part
    x_ref[...] = total[:, :FEAT].astype(BF)
    g_ref[...] = total[:, FEAT:].astype(BF)


def compact(shard, rows, sources):
    vmem = pl.BlockSpec(memory_space=pltpu.VMEM)
    return call(
        compact_kernel,
        "compact",
        2 * LIVE * SLOTS * SLOTS,
        5 << 20,
        out_shape=(
            jax.ShapeDtypeStruct((LIVE, FEAT), BF),
            jax.ShapeDtypeStruct((LIVE, FEAT), BF),
            jax.ShapeDtypeStruct((8, 8, BLK), jnp.int32),
            jax.ShapeDtypeStruct((8, 8, BLK), jnp.int32),
        ),
        in_specs=[smem(), vmem] + [vmem] * 8,
        out_specs=(vmem,) * 4,
    )(shard, rows, *sources)


ORDERS = ((0, 1, 2, 3), (0, 2, 1, 3))


def turn_kernel(x_ref, *outs):
    for order, out in zip(ORDERS, outs):
        rows = [x_ref[p * CUT : (p + 1) * CUT, :] for p in order]
        out[...] = jnp.concatenate(rows, axis=0).astype(F32).T.astype(BF)


def turned(x):
    vmem = pl.BlockSpec(memory_space=pltpu.VMEM)
    return call(
        turn_kernel,
        "turned",
        1,
        1 << 12,
        out_shape=(jax.ShapeDtypeStruct((FEAT, LIVE), BF),) * 2,
        in_specs=[vmem],
        out_specs=(vmem,) * 2,
    )(x)


def partial_kernel(start, pieces, x_ref, g_ref, wx_ref, wdt_ref, *outs):
    count = pieces * CUT
    x, g = x_ref[start : start + count, :], g_ref[start : start + count, :]
    both = jnp.dot(x, wx_ref[0], preferred_element_type=F32)
    back = jnp.dot(g, wdt_ref[0], preferred_element_type=F32)
    for which, result in enumerate((both[:, :PAIR], both[:, PAIR:], back)):
        for piece in range(pieces):
            for q in SIDES:
                outs[piece * 2 + q][which] = result[
                    piece * CUT : (piece + 1) * CUT, q * BLK : (q + 1) * BLK
                ].astype(BF)


def partials(start, pieces, x, g, wx, wdt):
    count = pieces * CUT
    return call(
        functools.partial(partial_kernel, start, pieces),
        "partials",
        2 * count * FEAT * 3 * UNITS,
        7 << 20,
        grid=(STEPS,),
        out_shape=(jax.ShapeDtypeStruct((3, CUT, HALF), BF),) * (2 * pieces),
        in_specs=[
            whole((LIVE, FEAT)),
            whole((LIVE, FEAT)),
            pl.BlockSpec((1, FEAT, 2 * PAIR), lambda j: (j, 0, 0)),
            pl.BlockSpec((1, FEAT, PAIR), lambda j: (j, 0, 0)),
        ],
        out_specs=(pl.BlockSpec((3, CUT, BLK), lambda j: (0, 0, j)),) * (2 * pieces),
    )(x, g, wx, wdt)


def picked(rows, offs, cnts, k, slot):
    hit = (rows - offs[k, 0:1, 0:1] == slot) & (slot < cnts[k, 0:1, 0:1])
    return jnp.where(hit, 1.0, 0.0).astype(BF)


def products(lower, upper, shared, w_down):
    both, single = (lower, upper) if shared == 0 else (upper, lower)
    result = [
        jnp.dot(jnp.concatenate(both, axis=1), w_down, preferred_element_type=F32)
    ]
    for q in SIDES:
        result.append(
            jnp.dot(single[q], w_down[q * BLK : (q + 1) * BLK, :], preferred_element_type=F32)
        )
    return result


def first_output_kernel(wd_ref, own0, own1, total):
    j = pl.program_id(0)
    lower = [ref[0, :CUT, :] for ref in (own0, own1)]
    upper = [ref[0, CUT:, :] for ref in (own0, own1)]
    results = products(lower, upper, 0, wd_ref[...])

    @pl.when(j == 0)
    def _():
        for i in range(3):
            total[i] = results[i]

    @pl.when(j > 0)
    def _():
        for i in range(3):
            total[i] += results[i]


def first_output(wd, hidden_own):
    return call(
        first_output_kernel,
        "first_output",
        1,
        1 << 12,
        grid=(STEPS,),
        out_shape=jax.ShapeDtypeStruct((3, CUT, FEAT), F32),
        in_specs=[pl.BlockSpec((PAIR, FEAT), lambda j: (j, 0))]
        + [pl.BlockSpec((1, 2 * CUT, BLK), lambda j: (0, 0, j))] * 2,
        out_specs=whole((3, CUT, FEAT)),
    )(wd, *hidden_own)


def last_output_kernel(rows_ref, offs, cnts, early_ref, wd_ref, come0, come1, near_ref, away_ref):
    totals = None
    for j in range(STEPS):
        by = slice(j * BLK, (j + 1) * BLK)
        lower = [ref[0, :CUT, by] for ref in (come0, come1)]
        upper = [ref[0, CUT:, by] for ref in (come0, come1)]
        results = products(lower, upper, 1, wd_ref[j * PAIR : (j + 1) * PAIR, :])
        totals = results if j == 0 else [a + b for a, b in zip(totals, results)]
    pieces = (early_ref[0], early_ref[1] + totals[2], early_ref[2] + totals[1], totals[0])
    mixed = jnp.concatenate([piece.astype(BF) for piece in pieces], axis=0)
    rows = rows_ref[0:1, :]
    slot = lax.broadcasted_iota(jnp.int32, (BLK, LIVE), 0)
    for k in range(8):
        pick = picked(rows, offs, cnts, k, slot)
        target = near_ref if k < 4 else away_ref
        target[k % 4] = jnp.dot(pick, mixed, preferred_element_type=F32).astype(BF)


def last_output(rows, offs, cnts, early, wd, hidden_come):
    return call(
        last_output_kernel,
        "last_output",
        1,
        1 << 12,
        grid=(1,),
        out_shape=(jax.ShapeDtypeStruct((4, BLK, FEAT), BF),) * 2,
        in_specs=[
            whole((1, LIVE)),
            whole((8, 8, BLK)),
            whole((8, 8, BLK)),
            whole((3, CUT, FEAT)),
            whole((UNITS, FEAT)),
        ]
        + [whole((1, 2 * CUT, HALF))] * 2,
        out_specs=(whole((4, BLK, FEAT)),) * 2,
    )(rows, offs, cnts, early, wd, *hidden_come)


def all_rows(owns, comes, which):
    left = jnp.concatenate([owns[0][which], comes[0][which]], axis=0)
    right = jnp.concatenate(
        [ref[which, i : i + CUT] for i in (0, CUT) for ref in (owns[1], comes[1])], axis=0
    )
    return jnp.concatenate([left, right], axis=1)


def down_kernel(dm, g_ref, own0, own1, come0, come1, down_out):
    j = pl.program_id(0)
    down = lax.dot_general(
        all_rows((own0, own1), (come0, come1), 0),
        g_ref[...],
        (((0,), (0,)), ((), ())),
        preferred_element_type=F32,
    )
    for r in range(4):
        for b in range(2):
            at, by = slice(r * BLK, (r + 1) * BLK), slice(b * BLK, (b + 1) * BLK)
            down_out[by, at] = kept(dm, 2 * j + b, r, down[by, at])


def down_gradient(dm, g, parts):
    return call(
        down_kernel,
        "down_gradient",
        1,
        1 << 12,
        grid=(STEPS,),
        out_shape=jax.ShapeDtypeStruct((UNITS, FEAT), F32),
        in_specs=[smem(), whole((LIVE, FEAT))]
        + [pl.BlockSpec((1, 2 * CUT, BLK), lambda j: (0, 0, j))] * 4,
        out_specs=pl.BlockSpec((PAIR, FEAT), lambda j: (j, 0)),
    )(dm, g, *parts)


def plane_products(turns, parts, at):
    return [
        jnp.dot(
            turn[:, at : at + 2 * CUT],
            jnp.concatenate([part[0], part[1]], axis=1),
            preferred_element_type=F32,
        )
        for turn, part in zip(turns, parts)
    ]


def first_grad_kernel(xt0, xt1, own0, own1, gate_out, up_out):
    for q, both in enumerate(plane_products((xt0, xt1), (own0, own1), 0)):
        gate_out[:, q * BLK : (q + 1) * BLK] = both[:, :BLK]
        up_out[:, q * BLK : (q + 1) * BLK] = both[:, BLK:]


def last_grad_kernel(gm, um, xt0, xt1, gate_in, up_in, come0, come1, gate_out, up_out):
    j = pl.program_id(0)
    for q, both in enumerate(plane_products((xt0, xt1), (come0, come1), 2 * CUT)):
        by = slice(q * BLK, (q + 1) * BLK)
        for r in range(4):
            at = slice(r * BLK, (r + 1) * BLK)
            gate_out[at, by] = kept(gm, r, 2 * j + q, gate_in[at, by] + both[at, :BLK])
            up_out[at, by] = kept(um, r, 2 * j + q, up_in[at, by] + both[at, BLK:])


def grad_call(kernel, name, first_specs, middle_specs):
    columns = pl.BlockSpec((FEAT, PAIR), lambda j: (0, j))
    return call(
        kernel,
        name,
        2 * LIVE * FEAT * UNITS,
        13 << 20,
        grid=(STEPS,),
        out_shape=(jax.ShapeDtypeStruct((FEAT, UNITS), F32),) * 2,
        in_specs=[smem()] * first_specs
        + [whole((FEAT, LIVE))] * 2
        + [columns] * middle_specs
        + [pl.BlockSpec((2, 2 * CUT, BLK), lambda j: (0, 0, j))] * 2,
        out_specs=(columns,) * 2,
    )


def split(value, axis):
    lower = lax.slice_in_dim(value, 0, 1, axis=axis)
    upper = lax.slice_in_dim(value, 1, 2, axis=axis)
    return lower, upper


def activate(total):
    gate, upward, back = total[0], total[1], total[2]
    sigma = jax.nn.sigmoid(gate)
    active = gate * sigma
    hidden = (active * upward).astype(BF)
    d_gate = (back * upward * sigma * (1.0 + gate * (1.0 - sigma))).astype(BF)
    d_up = (back * active).astype(BF)
    return jnp.stack([d_gate, d_up, hidden])


def exchange(values, number):
    return [
        lax.ppermute(values[q], ("col", "dp"), partners(ROUNDS[q][number][1])) for q in SIDES
    ]


def on_device(
    tokens, cotangent, gate_weight, up_weight, down_weight, gate_mask, up_mask, down_mask, counts
):
    live = (lax.iota(jnp.int32, tokens.shape[0]) < counts[0])[:, None]
    place = lax.axis_index("col")
    order = jnp.arange(8)
    shard = ((place // 2 + order % 4) % SIDE) * 2 + ((place % 2) ^ (order // 4))
    own = pack(tokens, cotangent, counts)
    column = [own] + [lax.ppermute(own, "col", shift(-dz, 0)) for dz in (1, 2, 3)]
    beside = [lax.ppermute(own, "col", shift(0, 1))]
    wx, wdt, wd = prepare(gate_mask, up_mask, down_mask, gate_weight, up_weight, down_weight)
    rows = logical_rows()
    column[1], column[3], wx, wdt, wd, rows_down, rows_along, shard = lax.optimization_barrier(
        (column[1], column[3], wx, wdt, wd, rows[:, None], rows[None, :], shard)
    )
    beside += [lax.ppermute(value, "col", shift(0, 1)) for value in column[1:]]
    x, g, offs, cnts = compact(shard, rows_down, column + beside)

    early = partials(FIRST, 1, x, g, wx, wdt)
    come_early = exchange(early, 0)
    x_rest, g_rest, *_ = lax.optimization_barrier((x, g, *early))
    late = partials(0, 3, x_rest, g_rest, wx, wdt)
    zero = [late[q] for q in SIDES]
    side = [[late[2 * (2 - ROUNDS[q][n][0]) + q] for q in SIDES] for n in range(2)]
    come_rest = exchange(side[0], 0)
    turns = turned(x_rest)
    *come_early, turn0, turn1 = lax.optimization_barrier((*come_early, *turns))
    second = [
        (side[1][q].astype(F32) + come_early[q].astype(F32)).astype(BF) for q in SIDES
    ]
    come_second = exchange(second, 1)
    *come_rest, last0, last1 = lax.optimization_barrier((*come_rest, *come_second))
    come_second = [last0, last1]
    keep, send = [None] * 2, [None] * 2
    for q in SIDES:
        total = (
            zero[q].astype(F32) + come_rest[q].astype(F32) + come_second[q].astype(F32)
        ).reshape(3, 2, 2, 48, HALF)
        keep[q], upper = split(total, ROUNDS[q][2][0] - 1)
        send[q] = upper.astype(BF)
    come = exchange(send, 2)
    keep = [(keep[q] + come[q].astype(F32)).astype(BF) for q in SIDES]
    come = exchange(keep, 3)
    held = []
    for q in SIDES:
        axis = ROUNDS[q][3][0] - 1
        lower, upper = split(come[q], axis)
        arrived = jnp.concatenate([upper, lower], axis=axis)
        held.append(activate(keep[q].astype(F32) + arrived.astype(F32)))
    come = exchange(held, 2)
    held = [
        jnp.concatenate([held[q], come[q]], axis=ROUNDS[q][2][0] - 1).reshape(3, CUT, HALF)
        for q in SIDES
    ]
    near = exchange(held, 1)
    hidden_own = [jnp.concatenate([held[q][2:], near[q][2:]], axis=1) for q in SIDES]
    derived_own = [jnp.concatenate([held[q][:2], near[q][:2]], axis=1) for q in SIDES]
    hidden_come = exchange(hidden_own, 0)
    derived_come = exchange(derived_own, 0)

    begun = first_output(wd, hidden_own)
    grads_begun = grad_call(first_grad_kernel, "first_grad", 0, 0)(turn0, turn1, *derived_own)
    begun, *grads_begun = lax.optimization_barrier((begun, *grads_begun))
    mine, away = last_output(rows_along, offs, cnts, begun, wd, hidden_come)
    other = lax.ppermute(away, "col", shift(0, 1))
    down_grad = down_gradient(down_mask, g, hidden_own + hidden_come)
    other, down_grad = lax.optimization_barrier((other, down_grad))
    summed = mine.astype(F32) + other.astype(F32)
    terms = [summed[k].astype(BF) for k in range(4)]
    arrived = [lax.ppermute(terms[dz], "col", shift(dz, 0)) for dz in (1, 2, 3)]
    gate_grad, up_grad = grad_call(last_grad_kernel, "last_grad", 2, 2)(
        gate_mask, up_mask, turn0, turn1, *grads_begun, *derived_come
    )
    *arrived, gate_grad, up_grad = lax.optimization_barrier((*arrived, gate_grad, up_grad))
    mixed = sum((term.astype(F32) for term in arrived), terms[0].astype(F32))
    output = jnp.where(live, mixed, jnp.zeros_like(mixed)).astype(BF)
    return (output, gate_grad, up_grad, down_grad)


def solution(mesh):
    in_specs = (
        P("col", "dp"),
        P("col", "dp"),
        P("dp", "col"),
        P("dp", "col"),
        P("col", "dp"),
        P("dp", "col"),
        P("dp", "col"),
        P("col", "dp"),
        P("col"),
    )
    out_specs = (P("col", "dp"), P("dp", "col"), P("dp", "col"), P("col", "dp"))
    return jax.shard_map(
        on_device, mesh=mesh, in_specs=in_specs, out_specs=out_specs, check_vma=False
    )
```

```python
import functools

import jax
import jax.numpy as jnp
from jax import lax
from jax.experimental import pallas as pl
from jax.experimental.pallas import tpu as pltpu
from jax.sharding import PartitionSpec as P

BF = jnp.bfloat16
F32 = jnp.float32
LIVE = 768
PAD = 144
SIDE = 4
BLK = 128
PAIR = 2 * BLK
UNITS = 1792
HALF = UNITS // 2
STEPS = UNITS // PAIR
FEAT = 512
SLOTS = 1024
CUT = 192
FIRST = 576
LAST = LIVE - FIRST
VMEM = 32 << 20

MASKS = {"xA": (1, 0), "xB": (3, 0), "yA": (0, 1), "yB": (0, 3)}
ROUNDS = (
    ((0, ("xA", "yA")), (1, ("xB", "yB")), (2, ("yA", "xA")), (3, ("yB", "xB"))),
    ((1, ("xB", "yB")), (0, ("xA", "yA")), (3, ("yB", "xB")), (2, ("yA", "xA"))),
)
SIDES = (0, 1)


def partners(names):
    pairs = []
    for col in range(2 * SIDE):
        dx, dy = MASKS[names[col % 2]]
        for x in range(SIDE):
            for y in range(SIDE):
                start = (col * SIDE + x) * SIDE + y
                pairs.append((start, (col * SIDE + (x ^ dx)) * SIDE + (y ^ dy)))
    return pairs


def shift(dz, dc):
    return [
        (z * 2 + c, ((z + dz) % SIDE) * 2 + (c + dc) % 2) for z in range(SIDE) for c in range(2)
    ]


def logical_rows():
    place = lax.axis_index("dp")
    x, y = place // SIDE, place % SIDE

    def sides(v):
        high = v // 2
        return (v % 2) ^ high, high

    xa, xb = sides(x)
    ya, yb = sides(y)
    first = xa * 8 + xb * 4 + ya * 2 + yb
    second = ya * 8 + yb * 4 + xa * 2 + xb
    mask = jnp.where(lax.axis_index("col") % 2 > 0, second, first)
    row = lax.iota(jnp.int32, LIVE)
    return ((row // 48) ^ mask) * 48 + row % 48


def kept(mask_ref, row, col, value):
    return jnp.where(mask_ref[row, col] > 0, value, jnp.zeros_like(value))


def smem():
    return pl.BlockSpec(memory_space=pltpu.SMEM)


def whole(shape):
    return pl.BlockSpec(shape, lambda j: (0,) * len(shape))


def call(kernel, name, flops, moved, **rest):
    return pl.pallas_call(
        kernel,
        compiler_params=pltpu.CompilerParams(vmem_limit_bytes=VMEM),
        cost_estimate=pl.CostEstimate(flops=flops, bytes_accessed=moved, transcendentals=0),
        name=name,
        **rest,
    )


def pack_kernel(tok_ref, cot_ref, count_ref, out_ref, sems):
    copies = [
        pltpu.make_async_copy(
            ref, out_ref.at[pl.ds(0, BLK), pl.ds(i * FEAT, FEAT)], sems.at[i]
        )
        for i, ref in enumerate((tok_ref, cot_ref))
    ]
    for copy in copies:
        copy.start()
    count = jnp.full((PAD - BLK, 2 * FEAT), count_ref[0], jnp.int32)
    out_ref[BLK:, :] = count.astype(F32).astype(BF)
    for copy in copies:
        copy.wait()


def pack(tokens, cotangent, counts):
    return call(
        pack_kernel,
        "pack",
        0,
        1 << 19,
        out_shape=jax.ShapeDtypeStruct((PAD, 2 * FEAT), BF),
        in_specs=[pl.BlockSpec(memory_space=pl.ANY)] * 2 + [smem()],
        out_specs=pl.BlockSpec(memory_space=pltpu.VMEM),
        scratch_shapes=[pltpu.SemaphoreType.DMA((2,))],
    )(tokens, cotangent, counts)


def prepare_kernel(gm, um, dm, wg, wu, wd, wx_ref, wdt_ref, wd_ref):
    j = pl.program_id(0)
    for which, (mask, ref) in enumerate(((gm, wg), (um, wu))):
        for r in range(4):
            for b in range(2):
                at = slice(r * BLK, (r + 1) * BLK)
                wx_ref[0, at, which * PAIR + b * BLK : which * PAIR + (b + 1) * BLK] = kept(
                    mask, r, 2 * j + b, ref[at, b * BLK : (b + 1) * BLK]
                )
    down = jnp.concatenate(
        [
            jnp.concatenate(
                [
                    kept(dm, 2 * j + b, c, wd[b * BLK : (b + 1) * BLK, c * BLK : (c + 1) * BLK])
                    for c in range(4)
                ],
                axis=1,
            )
            for b in range(2)
        ],
        axis=0,
    )
    wd_ref[...] = down
    wdt_ref[0] = down.T


def prepare(gm, um, dm, wg, wu, wd):
    return call(
        prepare_kernel,
        "prepare",
        0,
        13 << 20,
        grid=(STEPS,),
        out_shape=(
            jax.ShapeDtypeStruct((STEPS, FEAT, 2 * PAIR), BF),
            jax.ShapeDtypeStruct((STEPS, FEAT, PAIR), BF),
            jax.ShapeDtypeStruct((UNITS, FEAT), BF),
        ),
        in_specs=[
            smem(),
            smem(),
            smem(),
            pl.BlockSpec((FEAT, PAIR), lambda j: (0, j)),
            pl.BlockSpec((FEAT, PAIR), lambda j: (0, j)),
            pl.BlockSpec((PAIR, FEAT), lambda j: (j, 0)),
        ],
        out_specs=(
            pl.BlockSpec((1, FEAT, 2 * PAIR), lambda j: (j, 0, 0)),
            pl.BlockSpec((1, FEAT, PAIR), lambda j: (j, 0, 0)),
            pl.BlockSpec((PAIR, FEAT), lambda j: (j, 0)),
        ),
    )(gm, um, dm, wg, wu, wd)


def compact_kernel(shard, rows_ref, *refs):
    sources, (x_ref, g_ref, offs_ref, cnts_ref) = refs[:8], refs[8:]
    rows = rows_ref[...]
    slot = lax.broadcasted_iota(jnp.int32, (LIVE, BLK), 1)
    cnts = [ref[BLK : BLK + 1, 0:1].astype(F32).astype(jnp.int32) for ref in sources]
    total = None
    for pair in range(4):
        picks = []
        for k in (2 * pair, 2 * pair + 1):
            offset = jnp.zeros((1, 1), jnp.int32)
            for other in range(8):
                if other != k:
                    offset += jnp.where(shard[other] < shard[k], cnts[other], 0)
            offs_ref[k] = jnp.broadcast_to(offset, (8, BLK))
            cnts_ref[k] = jnp.broadcast_to(cnts[k], (8, BLK))
            hit = (rows - offset == slot) & (slot < cnts[k])
            picks.append(jnp.where(hit, 1.0, 0.0).astype(BF))
        source = jnp.concatenate(
            [sources[2 * pair][:BLK, :], sources[2 * pair + 1][:BLK, :]], axis=0
        )
        part = jnp.dot(jnp.concatenate(picks, axis=1), source, preferred_element_type=F32)
        total = part if total is None else total + part
    x_ref[...] = total[:, :FEAT].astype(BF)
    g_ref[...] = total[:, FEAT:].astype(BF)


def compact(shard, rows, sources):
    vmem = pl.BlockSpec(memory_space=pltpu.VMEM)
    return call(
        compact_kernel,
        "compact",
        2 * LIVE * SLOTS * SLOTS,
        5 << 20,
        out_shape=(
            jax.ShapeDtypeStruct((LIVE, FEAT), BF),
            jax.ShapeDtypeStruct((LIVE, FEAT), BF),
            jax.ShapeDtypeStruct((8, 8, BLK), jnp.int32),
            jax.ShapeDtypeStruct((8, 8, BLK), jnp.int32),
        ),
        in_specs=[smem(), vmem] + [vmem] * 8,
        out_specs=(vmem,) * 4,
    )(shard, rows, *sources)


ORDERS = ((0, 1, 2, 3), (0, 2, 1, 3))


def turn_kernel(x_ref, *outs):
    for order, out in zip(ORDERS, outs):
        rows = [x_ref[p * CUT : (p + 1) * CUT, :] for p in order]
        out[...] = jnp.concatenate(rows, axis=0).astype(F32).T.astype(BF)


def turned(x):
    vmem = pl.BlockSpec(memory_space=pltpu.VMEM)
    return call(
        turn_kernel,
        "turned",
        1,
        1 << 12,
        out_shape=(jax.ShapeDtypeStruct((FEAT, LIVE), BF),) * 2,
        in_specs=[vmem],
        out_specs=(vmem,) * 2,
    )(x)


def partial_kernel(start, pieces, x_ref, g_ref, wx_ref, wdt_ref, *outs):
    count = pieces * CUT
    x, g = x_ref[start : start + count, :], g_ref[start : start + count, :]
    both = jnp.dot(x, wx_ref[0], preferred_element_type=F32)
    back = jnp.dot(g, wdt_ref[0], preferred_element_type=F32)
    for which, result in enumerate((both[:, :PAIR], both[:, PAIR:], back)):
        for piece in range(pieces):
            for q in SIDES:
                outs[piece * 2 + q][which] = result[
                    piece * CUT : (piece + 1) * CUT, q * BLK : (q + 1) * BLK
                ].astype(BF)


def partials(start, pieces, x, g, wx, wdt):
    count = pieces * CUT
    return call(
        functools.partial(partial_kernel, start, pieces),
        "partials",
        2 * count * FEAT * 3 * UNITS,
        7 << 20,
        grid=(STEPS,),
        out_shape=(jax.ShapeDtypeStruct((3, CUT, HALF), BF),) * (2 * pieces),
        in_specs=[
            whole((LIVE, FEAT)),
            whole((LIVE, FEAT)),
            pl.BlockSpec((1, FEAT, 2 * PAIR), lambda j: (j, 0, 0)),
            pl.BlockSpec((1, FEAT, PAIR), lambda j: (j, 0, 0)),
        ],
        out_specs=(pl.BlockSpec((3, CUT, BLK), lambda j: (0, 0, j)),) * (2 * pieces),
    )(x, g, wx, wdt)


def picked(rows, offs, cnts, k, slot):
    hit = (rows - offs[k, 0:1, 0:1] == slot) & (slot < cnts[k, 0:1, 0:1])
    return jnp.where(hit, 1.0, 0.0).astype(BF)


def products(lower, upper, shared, w_down):
    both, single = (lower, upper) if shared == 0 else (upper, lower)
    result = [
        jnp.dot(jnp.concatenate(both, axis=1), w_down, preferred_element_type=F32)
    ]
    for q in SIDES:
        result.append(
            jnp.dot(single[q], w_down[q * BLK : (q + 1) * BLK, :], preferred_element_type=F32)
        )
    return result


def first_output_kernel(wd_ref, own0, own1, total):
    j = pl.program_id(0)
    lower = [ref[0, :CUT, :] for ref in (own0, own1)]
    upper = [ref[0, CUT:, :] for ref in (own0, own1)]
    results = products(lower, upper, 0, wd_ref[...])

    @pl.when(j == 0)
    def _():
        for i in range(3):
            total[i] = results[i]

    @pl.when(j > 0)
    def _():
        for i in range(3):
            total[i] += results[i]


def first_output(wd, hidden_own):
    return call(
        first_output_kernel,
        "first_output",
        1,
        1 << 12,
        grid=(STEPS,),
        out_shape=jax.ShapeDtypeStruct((3, CUT, FEAT), F32),
        in_specs=[pl.BlockSpec((PAIR, FEAT), lambda j: (j, 0))]
        + [pl.BlockSpec((1, 2 * CUT, BLK), lambda j: (0, 0, j))] * 2,
        out_specs=whole((3, CUT, FEAT)),
    )(wd, *hidden_own)


def last_output_kernel(rows_ref, offs, cnts, early_ref, wd_ref, come0, come1, near_ref, away_ref):
    totals = None
    for j in range(STEPS):
        by = slice(j * BLK, (j + 1) * BLK)
        lower = [ref[0, :CUT, by] for ref in (come0, come1)]
        upper = [ref[0, CUT:, by] for ref in (come0, come1)]
        results = products(lower, upper, 1, wd_ref[j * PAIR : (j + 1) * PAIR, :])
        totals = results if j == 0 else [a + b for a, b in zip(totals, results)]
    pieces = (early_ref[0], early_ref[1] + totals[2], early_ref[2] + totals[1], totals[0])
    mixed = jnp.concatenate([piece.astype(BF) for piece in pieces], axis=0)
    rows = rows_ref[0:1, :]
    slot = lax.broadcasted_iota(jnp.int32, (BLK, LIVE), 0)
    for k in range(8):
        pick = picked(rows, offs, cnts, k, slot)
        target = near_ref if k < 4 else away_ref
        target[k % 4] = jnp.dot(pick, mixed, preferred_element_type=F32).astype(BF)


def last_output(rows, offs, cnts, early, wd, hidden_come):
    return call(
        last_output_kernel,
        "last_output",
        1,
        1 << 12,
        grid=(1,),
        out_shape=(jax.ShapeDtypeStruct((4, BLK, FEAT), BF),) * 2,
        in_specs=[
            whole((1, LIVE)),
            whole((8, 8, BLK)),
            whole((8, 8, BLK)),
            whole((3, CUT, FEAT)),
            whole((UNITS, FEAT)),
        ]
        + [whole((1, 2 * CUT, HALF))] * 2,
        out_specs=(whole((4, BLK, FEAT)),) * 2,
    )(rows, offs, cnts, early, wd, *hidden_come)


def all_rows(owns, comes, which):
    left = jnp.concatenate([owns[0][which], comes[0][which]], axis=0)
    right = jnp.concatenate(
        [ref[which, i : i + CUT] for i in (0, CUT) for ref in (owns[1], comes[1])], axis=0
    )
    return jnp.concatenate([left, right], axis=1)


def down_kernel(dm, g_ref, own0, own1, come0, come1, down_out):
    j = pl.program_id(0)
    down = lax.dot_general(
        all_rows((own0, own1), (come0, come1), 0),
        g_ref[...],
        (((0,), (0,)), ((), ())),
        preferred_element_type=F32,
    )
    for r in range(4):
        for b in range(2):
            at, by = slice(r * BLK, (r + 1) * BLK), slice(b * BLK, (b + 1) * BLK)
            down_out[by, at] = kept(dm, 2 * j + b, r, down[by, at])


def down_gradient(dm, g, parts):
    return call(
        down_kernel,
        "down_gradient",
        1,
        1 << 12,
        grid=(STEPS,),
        out_shape=jax.ShapeDtypeStruct((UNITS, FEAT), F32),
        in_specs=[smem(), whole((LIVE, FEAT))]
        + [pl.BlockSpec((1, 2 * CUT, BLK), lambda j: (0, 0, j))] * 4,
        out_specs=pl.BlockSpec((PAIR, FEAT), lambda j: (j, 0)),
    )(dm, g, *parts)


def plane_products(turns, parts, at):
    return [
        jnp.dot(
            turn[:, at : at + 2 * CUT],
            jnp.concatenate([part[0], part[1]], axis=1),
            preferred_element_type=F32,
        )
        for turn, part in zip(turns, parts)
    ]


def first_grad_kernel(xt0, xt1, own0, own1, gate_out, up_out):
    for q, both in enumerate(plane_products((xt0, xt1), (own0, own1), 0)):
        gate_out[:, q * BLK : (q + 1) * BLK] = both[:, :BLK]
        up_out[:, q * BLK : (q + 1) * BLK] = both[:, BLK:]


def last_grad_kernel(mask, xt0, xt1, early, low0, high0, low1, high1, out):
    j = pl.program_id(0)
    for q, (turn, low, high) in enumerate(((xt0, low0, high0), (xt1, low1, high1))):
        by = slice(q * BLK, (q + 1) * BLK)
        grad = jnp.dot(
            turn[:, 2 * CUT :],
            jnp.concatenate([low[0], high[0]], axis=0),
            preferred_element_type=F32,
        )
        for r in range(4):
            at = slice(r * BLK, (r + 1) * BLK)
            out[at, by] = kept(mask, r, 2 * j + q, early[at, by] + grad[at, :])


COLUMNS = pl.BlockSpec((FEAT, PAIR), lambda j: (0, j))


def first_grad(turns, derived_own):
    return call(
        first_grad_kernel,
        "first_grad",
        2 * LIVE * FEAT * UNITS,
        13 << 20,
        grid=(STEPS,),
        out_shape=(jax.ShapeDtypeStruct((FEAT, UNITS), F32),) * 2,
        in_specs=[whole((FEAT, LIVE))] * 2
        + [pl.BlockSpec((2, 2 * CUT, BLK), lambda j: (0, 0, j))] * 2,
        out_specs=(COLUMNS,) * 2,
    )(*turns, *derived_own)


def last_grad(mask, turns, early, low, high):
    specs, arrays = [], []
    for q in SIDES:
        for values, plane in (low, high):
            arrays.append(values[q])
            specs.append(pl.BlockSpec((1, CUT, BLK), lambda j, plane=plane: (plane, 0, j)))
    return call(
        last_grad_kernel,
        "last_grad",
        LIVE * FEAT * UNITS,
        6 << 20,
        grid=(STEPS,),
        out_shape=jax.ShapeDtypeStruct((FEAT, UNITS), F32),
        in_specs=[smem()] + [whole((FEAT, LIVE))] * 2 + [COLUMNS] + specs,
        out_specs=COLUMNS,
    )(mask, *turns, early, *arrays)


def split(value, axis):
    lower = lax.slice_in_dim(value, 0, 1, axis=axis)
    upper = lax.slice_in_dim(value, 1, 2, axis=axis)
    return lower, upper


def activate(total):
    gate, upward, back = total[0], total[1], total[2]
    sigma = jax.nn.sigmoid(gate)
    active = gate * sigma
    hidden = (active * upward).astype(BF)
    d_gate = (back * upward * sigma * (1.0 + gate * (1.0 - sigma))).astype(BF)
    d_up = (back * active).astype(BF)
    return jnp.stack([d_gate, d_up, hidden])


def exchange(values, number):
    return [
        lax.ppermute(values[q], ("col", "dp"), partners(ROUNDS[q][number][1])) for q in SIDES
    ]


def on_device(
    tokens, cotangent, gate_weight, up_weight, down_weight, gate_mask, up_mask, down_mask, counts
):
    live = (lax.iota(jnp.int32, tokens.shape[0]) < counts[0])[:, None]
    place = lax.axis_index("col")
    order = jnp.arange(8)
    shard = ((place // 2 + order % 4) % SIDE) * 2 + ((place % 2) ^ (order // 4))
    own = pack(tokens, cotangent, counts)
    column = [own] + [lax.ppermute(own, "col", shift(-dz, 0)) for dz in (1, 2, 3)]
    beside = [lax.ppermute(own, "col", shift(0, 1))]
    wx, wdt, wd = prepare(gate_mask, up_mask, down_mask, gate_weight, up_weight, down_weight)
    rows = logical_rows()
    column[1], column[3], wx, wdt, wd, rows_down, rows_along, shard = lax.optimization_barrier(
        (column[1], column[3], wx, wdt, wd, rows[:, None], rows[None, :], shard)
    )
    beside += [lax.ppermute(value, "col", shift(0, 1)) for value in column[1:]]
    x, g, offs, cnts = compact(shard, rows_down, column + beside)

    early = partials(FIRST, 1, x, g, wx, wdt)
    come_early = exchange(early, 0)
    x_rest, g_rest, *_ = lax.optimization_barrier((x, g, *early))
    late = partials(0, 3, x_rest, g_rest, wx, wdt)
    zero = [late[q] for q in SIDES]
    side = [[late[2 * (2 - ROUNDS[q][n][0]) + q] for q in SIDES] for n in range(2)]
    come_rest = exchange(side[0], 0)
    turns = turned(x_rest)
    *come_early, turn0, turn1 = lax.optimization_barrier((*come_early, *turns))
    second = [
        (side[1][q].astype(F32) + come_early[q].astype(F32)).astype(BF) for q in SIDES
    ]
    come_second = exchange(second, 1)
    *come_rest, last0, last1 = lax.optimization_barrier((*come_rest, *come_second))
    come_second = [last0, last1]
    keep, send = [None] * 2, [None] * 2
    for q in SIDES:
        total = (
            zero[q].astype(F32) + come_rest[q].astype(F32) + come_second[q].astype(F32)
        ).reshape(3, 2, 2, 48, HALF)
        keep[q], upper = split(total, ROUNDS[q][2][0] - 1)
        send[q] = upper.astype(BF)
    come = exchange(send, 2)
    keep = [(keep[q] + come[q].astype(F32)).astype(BF) for q in SIDES]
    come = exchange(keep, 3)
    held = []
    for q in SIDES:
        axis = ROUNDS[q][3][0] - 1
        lower, upper = split(come[q], axis)
        arrived = jnp.concatenate([upper, lower], axis=axis)
        held.append(activate(keep[q].astype(F32) + arrived.astype(F32)))
    come = exchange(held, 2)
    held = [
        jnp.concatenate([held[q], come[q]], axis=ROUNDS[q][2][0] - 1).reshape(3, CUT, HALF)
        for q in SIDES
    ]
    near = exchange(held, 1)
    hidden_own = [jnp.concatenate([held[q][2:], near[q][2:]], axis=1) for q in SIDES]
    derived_own = [jnp.concatenate([held[q][:2], near[q][:2]], axis=1) for q in SIDES]
    hidden_come = exchange(hidden_own, 0)
    quarters = [value.reshape(4, CUT, HALF) for value in derived_own]
    most_come = exchange([value[:3] for value in quarters], 0)

    begun = first_output(wd, hidden_own)
    turns = (turn0, turn1)
    gate_begun, up_begun = first_grad(turns, derived_own)
    ends = [value[3:] for value in quarters]
    *ends, begun, gate_begun, up_begun = lax.optimization_barrier(
        (*ends, begun, gate_begun, up_begun)
    )
    end_come = exchange(ends, 0)
    mine, away = last_output(rows_along, offs, cnts, begun, wd, hidden_come)
    other = lax.ppermute(away, "col", shift(0, 1))
    down_grad = down_gradient(down_mask, g, hidden_own + hidden_come)
    other, down_grad = lax.optimization_barrier((other, down_grad))
    summed = mine.astype(F32) + other.astype(F32)
    terms = [summed[k].astype(BF) for k in range(4)]
    arrived = [lax.ppermute(terms[dz], "col", shift(dz, 0)) for dz in (1, 2, 3)]
    gate_grad = last_grad(gate_mask, turns, gate_begun, (most_come, 0), (most_come, 1))
    *end_come, gate_grad = lax.optimization_barrier((*end_come, gate_grad))
    up_grad = last_grad(up_mask, turns, up_begun, (most_come, 2), (end_come, 0))
    *arrived, gate_grad, up_grad = lax.optimization_barrier((*arrived, gate_grad, up_grad))
    mixed = sum((term.astype(F32) for term in arrived), terms[0].astype(F32))
    output = jnp.where(live, mixed, jnp.zeros_like(mixed)).astype(BF)
    return (output, gate_grad, up_grad, down_grad)


def solution(mesh):
    in_specs = (
        P("col", "dp"),
        P("col", "dp"),
        P("dp", "col"),
        P("dp", "col"),
        P("col", "dp"),
        P("dp", "col"),
        P("dp", "col"),
        P("col", "dp"),
        P("col"),
    )
    out_specs = (P("col", "dp"), P("dp", "col"), P("dp", "col"), P("col", "dp"))
    return jax.shard_map(
        on_device, mesh=mesh, in_specs=in_specs, out_specs=out_specs, check_vma=False
    )
```

```python
import functools

import jax
import jax.numpy as jnp
from jax import lax
from jax.experimental import pallas as pl
from jax.experimental.pallas import tpu as pltpu
from jax.sharding import PartitionSpec as P

BF = jnp.bfloat16
F32 = jnp.float32
LIVE = 768
PAD = 144
SIDE = 4
BLK = 128
PAIR = 2 * BLK
UNITS = 1792
HALF = UNITS // 2
STEPS = UNITS // PAIR
FEAT = 512
SLOTS = 1024
CUT = 192
FIRST = 576
LAST = LIVE - FIRST
VMEM = 32 << 20

MASKS = {"xA": (1, 0), "xB": (3, 0), "yA": (0, 1), "yB": (0, 3)}
ROUNDS = (
    ((0, ("xA", "yA")), (1, ("xB", "yB")), (2, ("yA", "xA")), (3, ("yB", "xB"))),
    ((1, ("xB", "yB")), (0, ("xA", "yA")), (3, ("yB", "xB")), (2, ("yA", "xA"))),
)
SIDES = (0, 1)


def partners(names):
    pairs = []
    for col in range(2 * SIDE):
        dx, dy = MASKS[names[col % 2]]
        for x in range(SIDE):
            for y in range(SIDE):
                start = (col * SIDE + x) * SIDE + y
                pairs.append((start, (col * SIDE + (x ^ dx)) * SIDE + (y ^ dy)))
    return pairs


def shift(dz, dc):
    return [
        (z * 2 + c, ((z + dz) % SIDE) * 2 + (c + dc) % 2) for z in range(SIDE) for c in range(2)
    ]


def logical_rows():
    place = lax.axis_index("dp")
    x, y = place // SIDE, place % SIDE

    def sides(v):
        high = v // 2
        return (v % 2) ^ high, high

    xa, xb = sides(x)
    ya, yb = sides(y)
    first = xa * 8 + xb * 4 + ya * 2 + yb
    second = ya * 8 + yb * 4 + xa * 2 + xb
    mask = jnp.where(lax.axis_index("col") % 2 > 0, second, first)
    row = lax.iota(jnp.int32, LIVE)
    return ((row // 48) ^ mask) * 48 + row % 48


def kept(mask_ref, row, col, value):
    return jnp.where(mask_ref[row, col] > 0, value, jnp.zeros_like(value))


def smem():
    return pl.BlockSpec(memory_space=pltpu.SMEM)


def whole(shape):
    return pl.BlockSpec(shape, lambda j: (0,) * len(shape))


def vmem():
    return pl.BlockSpec(memory_space=pltpu.VMEM)


def block(j, size):
    return slice(j * size, (j + 1) * size)


def call(kernel, name, flops, moved, **rest):
    return pl.pallas_call(
        kernel,
        compiler_params=pltpu.CompilerParams(vmem_limit_bytes=VMEM),
        cost_estimate=pl.CostEstimate(flops=flops, bytes_accessed=moved, transcendentals=0),
        name=name,
        **rest,
    )


def pack_kernel(tok_ref, cot_ref, count_ref, out_ref, sems):
    copies = [
        pltpu.make_async_copy(
            ref, out_ref.at[pl.ds(0, BLK), pl.ds(i * FEAT, FEAT)], sems.at[i]
        )
        for i, ref in enumerate((tok_ref, cot_ref))
    ]
    for copy in copies:
        copy.start()
    count = jnp.full((PAD - BLK, 2 * FEAT), count_ref[0], jnp.int32)
    out_ref[BLK:, :] = count.astype(F32).astype(BF)
    for copy in copies:
        copy.wait()


def pack(tokens, cotangent, counts):
    return call(
        pack_kernel,
        "pack",
        0,
        1 << 19,
        out_shape=jax.ShapeDtypeStruct((PAD, 2 * FEAT), BF),
        in_specs=[pl.BlockSpec(memory_space=pl.ANY)] * 2 + [smem()],
        out_specs=pl.BlockSpec(memory_space=pltpu.VMEM),
        scratch_shapes=[pltpu.SemaphoreType.DMA((2,))],
    )(tokens, cotangent, counts)


def prepare_kernel(gm, um, dm, wg, wu, wd, wx_ref, wdt_ref, wd_ref):
    j = pl.program_id(0)
    for which, (mask, ref) in enumerate(((gm, wg), (um, wu))):
        for r in range(4):
            for b in range(2):
                at = slice(r * BLK, (r + 1) * BLK)
                wx_ref[0, at, which * PAIR + b * BLK : which * PAIR + (b + 1) * BLK] = kept(
                    mask, r, 2 * j + b, ref[at, b * BLK : (b + 1) * BLK]
                )
    down = jnp.concatenate(
        [
            jnp.concatenate(
                [
                    kept(dm, 2 * j + b, c, wd[b * BLK : (b + 1) * BLK, c * BLK : (c + 1) * BLK])
                    for c in range(4)
                ],
                axis=1,
            )
            for b in range(2)
        ],
        axis=0,
    )
    wd_ref[...] = down
    wdt_ref[0] = down.T


def prepare(gm, um, dm, wg, wu, wd):
    return call(
        prepare_kernel,
        "prepare",
        0,
        13 << 20,
        grid=(STEPS,),
        out_shape=(
            jax.ShapeDtypeStruct((STEPS, FEAT, 2 * PAIR), BF),
            jax.ShapeDtypeStruct((STEPS, FEAT, PAIR), BF),
            jax.ShapeDtypeStruct((UNITS, FEAT), BF),
        ),
        in_specs=[
            smem(),
            smem(),
            smem(),
            pl.BlockSpec((FEAT, PAIR), lambda j: (0, j)),
            pl.BlockSpec((FEAT, PAIR), lambda j: (0, j)),
            pl.BlockSpec((PAIR, FEAT), lambda j: (j, 0)),
        ],
        out_specs=(
            pl.BlockSpec((1, FEAT, 2 * PAIR), lambda j: (j, 0, 0)),
            pl.BlockSpec((1, FEAT, PAIR), lambda j: (j, 0, 0)),
            pl.BlockSpec((PAIR, FEAT), lambda j: (j, 0)),
        ),
    )(gm, um, dm, wg, wu, wd)


def compact_kernel(shard, rows_ref, *refs):
    sources, (x_ref, g_ref, offs_ref, cnts_ref) = refs[:8], refs[8:]
    rows = rows_ref[...]
    slot = lax.broadcasted_iota(jnp.int32, (LIVE, BLK), 1)
    cnts = [ref[BLK : BLK + 1, 0:1].astype(F32).astype(jnp.int32) for ref in sources]
    total = None
    for pair in range(4):
        picks = []
        for k in (2 * pair, 2 * pair + 1):
            offset = jnp.zeros((1, 1), jnp.int32)
            for other in range(8):
                if other != k:
                    offset += jnp.where(shard[other] < shard[k], cnts[other], 0)
            offs_ref[k] = jnp.broadcast_to(offset, (8, BLK))
            cnts_ref[k] = jnp.broadcast_to(cnts[k], (8, BLK))
            hit = (rows - offset == slot) & (slot < cnts[k])
            picks.append(jnp.where(hit, 1.0, 0.0).astype(BF))
        source = jnp.concatenate(
            [sources[2 * pair][:BLK, :], sources[2 * pair + 1][:BLK, :]], axis=0
        )
        part = jnp.dot(jnp.concatenate(picks, axis=1), source, preferred_element_type=F32)
        total = part if total is None else total + part
    x_ref[...] = total[:, :FEAT].astype(BF)
    g_ref[...] = total[:, FEAT:].astype(BF)


def compact(shard, rows, sources):
    vmem = pl.BlockSpec(memory_space=pltpu.VMEM)
    return call(
        compact_kernel,
        "compact",
        2 * LIVE * SLOTS * SLOTS,
        5 << 20,
        out_shape=(
            jax.ShapeDtypeStruct((LIVE, FEAT), BF),
            jax.ShapeDtypeStruct((LIVE, FEAT), BF),
            jax.ShapeDtypeStruct((8, 8, BLK), jnp.int32),
            jax.ShapeDtypeStruct((8, 8, BLK), jnp.int32),
        ),
        in_specs=[smem(), vmem] + [vmem] * 8,
        out_specs=(vmem,) * 4,
    )(shard, rows, *sources)


ORDERS = ((0, 1, 2, 3), (0, 2, 1, 3))


def turn_kernel(x_ref, *outs):
    for order, out in zip(ORDERS, outs):
        rows = [x_ref[p * CUT : (p + 1) * CUT, :] for p in order]
        out[...] = jnp.concatenate(rows, axis=0).astype(F32).T.astype(BF)


def turned(x):
    return call(
        turn_kernel,
        "turned",
        1,
        1 << 12,
        out_shape=(jax.ShapeDtypeStruct((FEAT, LIVE), BF),) * 2,
        in_specs=[vmem()],
        out_specs=(vmem(),) * 2,
    )(x)


def partial_kernel(start, pieces, x_ref, g_ref, wx_ref, wdt_ref, *outs):
    count = pieces * CUT
    x, g = x_ref[start : start + count, :], g_ref[start : start + count, :]
    for j in range(STEPS):
        both = jnp.dot(x, wx_ref[j], preferred_element_type=F32)
        back = jnp.dot(g, wdt_ref[j], preferred_element_type=F32)
        for which, result in enumerate((both[:, :PAIR], both[:, PAIR:], back)):
            for piece in range(pieces):
                for q in SIDES:
                    outs[piece * 2 + q][which, :, block(j, BLK)] = result[
                        block(piece, CUT), block(q, BLK)
                    ].astype(BF)


def partials(start, pieces, x, g, wx, wdt):
    count = pieces * CUT
    return call(
        functools.partial(partial_kernel, start, pieces),
        "partials",
        2 * count * FEAT * 3 * UNITS,
        7 << 20,
        out_shape=(jax.ShapeDtypeStruct((3, CUT, HALF), BF),) * (2 * pieces),
        in_specs=[vmem()] * 4,
        out_specs=(vmem(),) * (2 * pieces),
    )(x, g, wx, wdt)


def picked(rows, offs, cnts, k, slot):
    hit = (rows - offs[k, 0:1, 0:1] == slot) & (slot < cnts[k, 0:1, 0:1])
    return jnp.where(hit, 1.0, 0.0).astype(BF)


def products(lower, upper, shared, w_down):
    both, single = (lower, upper) if shared == 0 else (upper, lower)
    result = [
        jnp.dot(jnp.concatenate(both, axis=1), w_down, preferred_element_type=F32)
    ]
    for q in SIDES:
        result.append(
            jnp.dot(single[q], w_down[q * BLK : (q + 1) * BLK, :], preferred_element_type=F32)
        )
    return result


def first_output_kernel(wd_ref, own0, own1, total):
    for j in range(STEPS):
        by = block(j, BLK)
        lower = [ref[0, :CUT, by] for ref in (own0, own1)]
        upper = [ref[0, CUT:, by] for ref in (own0, own1)]
        results = products(lower, upper, 0, wd_ref[block(j, PAIR), :])
        for i in range(3):
            if j == 0:
                total[i] = results[i]
            else:
                total[i] += results[i]


def first_output(wd, hidden_own):
    return call(
        first_output_kernel,
        "first_output",
        1,
        1 << 12,
        out_shape=jax.ShapeDtypeStruct((3, CUT, FEAT), F32),
        in_specs=[vmem()] * 3,
        out_specs=vmem(),
    )(wd, *hidden_own)


def last_output_kernel(rows_ref, offs, cnts, early_ref, wd_ref, come0, come1, near_ref, away_ref):
    totals = None
    for j in range(STEPS):
        by = slice(j * BLK, (j + 1) * BLK)
        lower = [ref[0, :CUT, by] for ref in (come0, come1)]
        upper = [ref[0, CUT:, by] for ref in (come0, come1)]
        results = products(lower, upper, 1, wd_ref[j * PAIR : (j + 1) * PAIR, :])
        totals = results if j == 0 else [a + b for a, b in zip(totals, results)]
    pieces = (early_ref[0], early_ref[1] + totals[2], early_ref[2] + totals[1], totals[0])
    mixed = jnp.concatenate([piece.astype(BF) for piece in pieces], axis=0)
    rows = rows_ref[0:1, :]
    slot = lax.broadcasted_iota(jnp.int32, (BLK, LIVE), 0)
    for k in range(8):
        pick = picked(rows, offs, cnts, k, slot)
        target = near_ref if k < 4 else away_ref
        target[k % 4] = jnp.dot(pick, mixed, preferred_element_type=F32).astype(BF)


def last_output(rows, offs, cnts, early, wd, hidden_come):
    return call(
        last_output_kernel,
        "last_output",
        1,
        1 << 12,
        grid=(1,),
        out_shape=(jax.ShapeDtypeStruct((4, BLK, FEAT), BF),) * 2,
        in_specs=[
            whole((1, LIVE)),
            whole((8, 8, BLK)),
            whole((8, 8, BLK)),
            whole((3, CUT, FEAT)),
            whole((UNITS, FEAT)),
        ]
        + [whole((1, 2 * CUT, HALF))] * 2,
        out_specs=(whole((4, BLK, FEAT)),) * 2,
    )(rows, offs, cnts, early, wd, *hidden_come)


def store(block_of, scratch, outs, sems):
    copies = [None, None]
    for j in range(STEPS):
        slot = j % 2
        if copies[slot] is not None:
            for copy in copies[slot]:
                copy.wait()
        places = block_of(j, [ref.at[slot] for ref in scratch])
        copies[slot] = [
            pltpu.make_async_copy(ref.at[slot], out.at[place], sems.at[i, slot])
            for i, (ref, out, place) in enumerate(zip(scratch, outs, places))
        ]
        for copy in copies[slot]:
            copy.start()
    for pair in copies:
        for copy in pair:
            copy.wait()


def down_kernel(dm, g_ref, own0, own1, come0, come1, out, scratch, sems):
    def block_of(j, targets):
        by = block(j, BLK)
        left = jnp.concatenate([own0[0, :, by], come0[0, :, by]], axis=0)
        right = jnp.concatenate(
            [ref[0, block(i, CUT), by] for i in range(2) for ref in (own1, come1)], axis=0
        )
        down = lax.dot_general(
            jnp.concatenate([left, right], axis=1),
            g_ref[...],
            (((0,), (0,)), ((), ())),
            preferred_element_type=F32,
        )
        for r in range(4):
            for b in range(2):
                at, to = block(r, BLK), block(b, BLK)
                targets[0][to, at] = kept(dm, 2 * j + b, r, down[to, at])
        return [(pl.ds(j * PAIR, PAIR), pl.ds(0, FEAT))]

    store(block_of, [scratch], [out], sems)


def down_gradient(dm, g, parts):
    return call(
        down_kernel,
        "down_gradient",
        1,
        1 << 12,
        out_shape=jax.ShapeDtypeStruct((UNITS, FEAT), F32),
        in_specs=[smem()] + [vmem()] * 5,
        out_specs=pl.BlockSpec(memory_space=pl.ANY),
        scratch_shapes=[
            pltpu.VMEM((2, PAIR, FEAT), F32),
            pltpu.SemaphoreType.DMA((1, 2)),
        ],
    )(dm, g, *parts)


def plane_products(turns, parts, at, by):
    return [
        jnp.dot(
            turn[:, at : at + 2 * CUT],
            jnp.concatenate([part[0, :, by], part[1, :, by]], axis=1),
            preferred_element_type=F32,
        )
        for turn, part in zip(turns, parts)
    ]


def first_grad_kernel(xt0, xt1, own0, own1, gate_out, up_out):
    for j in range(STEPS):
        sums = plane_products((xt0, xt1), (own0, own1), 0, block(j, BLK))
        for q, both in enumerate(sums):
            to = block(2 * j + q, BLK)
            gate_out[:, to] = both[:, :BLK]
            up_out[:, to] = both[:, BLK:]


def first_grad(turns, derived_own):
    return call(
        first_grad_kernel,
        "first_grad",
        2 * LIVE * FEAT * UNITS,
        13 << 20,
        out_shape=(jax.ShapeDtypeStruct((FEAT, UNITS), F32),) * 2,
        in_specs=[vmem()] * 4,
        out_specs=(vmem(),) * 2,
    )(*turns, *derived_own)


def last_grad_kernel(
    gm, um, xt0, xt1, gate_in, up_in, come0, come1, gate_out, up_out, gate_part, up_part, sems
):
    def block_of(j, targets):
        sums = plane_products((xt0, xt1), (come0, come1), 2 * CUT, block(j, BLK))
        for q, both in enumerate(sums):
            of, to = block(2 * j + q, BLK), block(q, BLK)
            for r in range(4):
                at = block(r, BLK)
                targets[0][at, to] = kept(gm, r, 2 * j + q, gate_in[at, of] + both[at, :BLK])
                targets[1][at, to] = kept(um, r, 2 * j + q, up_in[at, of] + both[at, BLK:])
        return [(pl.ds(0, FEAT), pl.ds(j * PAIR, PAIR))] * 2

    store(block_of, [gate_part, up_part], [gate_out, up_out], sems)


def last_grad(gm, um, turns, begun, derived_come):
    return call(
        last_grad_kernel,
        "last_grad",
        2 * LIVE * FEAT * UNITS,
        13 << 20,
        out_shape=(jax.ShapeDtypeStruct((FEAT, UNITS), F32),) * 2,
        in_specs=[smem()] * 2 + [vmem()] * 6,
        out_specs=(pl.BlockSpec(memory_space=pl.ANY),) * 2,
        scratch_shapes=[pltpu.VMEM((2, FEAT, PAIR), F32)] * 2
        + [pltpu.SemaphoreType.DMA((2, 2))],
    )(gm, um, *turns, *begun, *derived_come)


def split(value, axis):
    lower = lax.slice_in_dim(value, 0, 1, axis=axis)
    upper = lax.slice_in_dim(value, 1, 2, axis=axis)
    return lower, upper


def activate(total):
    gate, upward, back = total[0], total[1], total[2]
    sigma = jax.nn.sigmoid(gate)
    active = gate * sigma
    hidden = (active * upward).astype(BF)
    d_gate = (back * upward * sigma * (1.0 + gate * (1.0 - sigma))).astype(BF)
    d_up = (back * active).astype(BF)
    return jnp.stack([d_gate, d_up, hidden])


def exchange(values, number):
    return [
        lax.ppermute(values[q], ("col", "dp"), partners(ROUNDS[q][number][1])) for q in SIDES
    ]


def on_device(
    tokens, cotangent, gate_weight, up_weight, down_weight, gate_mask, up_mask, down_mask, counts
):
    live = (lax.iota(jnp.int32, tokens.shape[0]) < counts[0])[:, None]
    place = lax.axis_index("col")
    order = jnp.arange(8)
    shard = ((place // 2 + order % 4) % SIDE) * 2 + ((place % 2) ^ (order // 4))
    own = pack(tokens, cotangent, counts)
    column = [own] + [lax.ppermute(own, "col", shift(-dz, 0)) for dz in (1, 2, 3)]
    beside = [lax.ppermute(own, "col", shift(0, 1))]
    wx, wdt, wd = prepare(gate_mask, up_mask, down_mask, gate_weight, up_weight, down_weight)
    rows = logical_rows()
    column[1], column[3], wx, wdt, wd, rows_down, rows_along, shard = lax.optimization_barrier(
        (column[1], column[3], wx, wdt, wd, rows[:, None], rows[None, :], shard)
    )
    beside += [lax.ppermute(value, "col", shift(0, 1)) for value in column[1:]]
    x, g, offs, cnts = compact(shard, rows_down, column + beside)

    early = partials(FIRST, 1, x, g, wx, wdt)
    come_early = exchange(early, 0)
    x_rest, g_rest, *_ = lax.optimization_barrier((x, g, *early))
    late = partials(0, 3, x_rest, g_rest, wx, wdt)
    zero = [late[q] for q in SIDES]
    side = [[late[2 * (2 - ROUNDS[q][n][0]) + q] for q in SIDES] for n in range(2)]
    come_rest = exchange(side[0], 0)
    turns = turned(x_rest)
    *come_early, turn0, turn1 = lax.optimization_barrier((*come_early, *turns))
    second = [
        (side[1][q].astype(F32) + come_early[q].astype(F32)).astype(BF) for q in SIDES
    ]
    come_second = exchange(second, 1)
    *come_rest, last0, last1 = lax.optimization_barrier((*come_rest, *come_second))
    come_second = [last0, last1]
    keep, send = [None] * 2, [None] * 2
    for q in SIDES:
        total = (
            zero[q].astype(F32) + come_rest[q].astype(F32) + come_second[q].astype(F32)
        ).reshape(3, 2, 2, 48, HALF)
        keep[q], upper = split(total, ROUNDS[q][2][0] - 1)
        send[q] = upper.astype(BF)
    come = exchange(send, 2)
    keep = [(keep[q] + come[q].astype(F32)).astype(BF) for q in SIDES]
    come = exchange(keep, 3)
    held = []
    for q in SIDES:
        axis = ROUNDS[q][3][0] - 1
        lower, upper = split(come[q], axis)
        arrived = jnp.concatenate([upper, lower], axis=axis)
        held.append(activate(keep[q].astype(F32) + arrived.astype(F32)))
    come = exchange(held, 2)
    held = [
        jnp.concatenate([held[q], come[q]], axis=ROUNDS[q][2][0] - 1).reshape(3, CUT, HALF)
        for q in SIDES
    ]
    near = exchange(held, 1)
    hidden_own = [jnp.concatenate([held[q][2:], near[q][2:]], axis=1) for q in SIDES]
    derived_own = [jnp.concatenate([held[q][:2], near[q][:2]], axis=1) for q in SIDES]
    hidden_come = exchange(hidden_own, 0)
    derived_come = exchange(derived_own, 0)

    begun = first_output(wd, hidden_own)
    grads_begun = first_grad((turn0, turn1), derived_own)
    begun, *grads_begun = lax.optimization_barrier((begun, *grads_begun))
    mine, away = last_output(rows_along, offs, cnts, begun, wd, hidden_come)
    other = lax.ppermute(away, "col", shift(0, 1))
    down_grad = down_gradient(down_mask, g, hidden_own + hidden_come)
    other, down_grad = lax.optimization_barrier((other, down_grad))
    summed = mine.astype(F32) + other.astype(F32)
    terms = [summed[k].astype(BF) for k in range(4)]
    arrived = [lax.ppermute(terms[dz], "col", shift(dz, 0)) for dz in (1, 2, 3)]
    gate_grad, up_grad = last_grad(
        gate_mask, up_mask, (turn0, turn1), grads_begun, derived_come
    )
    *arrived, gate_grad, up_grad = lax.optimization_barrier((*arrived, gate_grad, up_grad))
    mixed = sum((term.astype(F32) for term in arrived), terms[0].astype(F32))
    output = jnp.where(live, mixed, jnp.zeros_like(mixed)).astype(BF)
    return (output, gate_grad, up_grad, down_grad)


def solution(mesh):
    in_specs = (
        P("col", "dp"),
        P("col", "dp"),
        P("dp", "col"),
        P("dp", "col"),
        P("col", "dp"),
        P("dp", "col"),
        P("dp", "col"),
        P("col", "dp"),
        P("col"),
    )
    out_specs = (P("col", "dp"), P("dp", "col"), P("dp", "col"), P("col", "dp"))
    return jax.shard_map(
        on_device, mesh=mesh, in_specs=in_specs, out_specs=out_specs, check_vma=False
    )
```

```python
import functools

import jax
import jax.numpy as jnp
from jax import lax
from jax.experimental import pallas as pl
from jax.experimental.pallas import tpu as pltpu
from jax.sharding import PartitionSpec as P

BF = jnp.bfloat16
F32 = jnp.float32
LIVE = 768
PAD = 144
SIDE = 4
BLK = 128
PAIR = 2 * BLK
UNITS = 1792
HALF = UNITS // 2
STEPS = UNITS // PAIR
FEAT = 512
SLOTS = 1024
CUT = 192
FIRST = 576
LAST = LIVE - FIRST
VMEM = 32 << 20

MASKS = {"xA": (1, 0), "xB": (3, 0), "yA": (0, 1), "yB": (0, 3)}
ROUNDS = (
    ((0, ("xA", "yA")), (1, ("xB", "yB")), (2, ("yA", "xA")), (3, ("yB", "xB"))),
    ((1, ("xB", "yB")), (0, ("xA", "yA")), (3, ("yB", "xB")), (2, ("yA", "xA"))),
)
SIDES = (0, 1)


def partners(names):
    pairs = []
    for col in range(2 * SIDE):
        dx, dy = MASKS[names[col % 2]]
        for x in range(SIDE):
            for y in range(SIDE):
                start = (col * SIDE + x) * SIDE + y
                pairs.append((start, (col * SIDE + (x ^ dx)) * SIDE + (y ^ dy)))
    return pairs


def shift(dz, dc):
    return [
        (z * 2 + c, ((z + dz) % SIDE) * 2 + (c + dc) % 2) for z in range(SIDE) for c in range(2)
    ]


def logical_rows():
    place = lax.axis_index("dp")
    x, y = place // SIDE, place % SIDE

    def sides(v):
        high = v // 2
        return (v % 2) ^ high, high

    xa, xb = sides(x)
    ya, yb = sides(y)
    first = xa * 8 + xb * 4 + ya * 2 + yb
    second = ya * 8 + yb * 4 + xa * 2 + xb
    mask = jnp.where(lax.axis_index("col") % 2 > 0, second, first)
    row = lax.iota(jnp.int32, LIVE)
    return ((row // 48) ^ mask) * 48 + row % 48


def kept(mask_ref, row, col, value):
    return jnp.where(mask_ref[row, col] > 0, value, jnp.zeros_like(value))


def smem():
    return pl.BlockSpec(memory_space=pltpu.SMEM)


def whole(shape):
    return pl.BlockSpec(shape, lambda j: (0,) * len(shape))


def vmem():
    return pl.BlockSpec(memory_space=pltpu.VMEM)


def block(j, size):
    return slice(j * size, (j + 1) * size)


def call(kernel, name, flops, moved, **rest):
    return pl.pallas_call(
        kernel,
        compiler_params=pltpu.CompilerParams(vmem_limit_bytes=VMEM),
        cost_estimate=pl.CostEstimate(flops=flops, bytes_accessed=moved, transcendentals=0),
        name=name,
        **rest,
    )


def pack_kernel(tok_ref, cot_ref, count_ref, out_ref, sems):
    copies = [
        pltpu.make_async_copy(
            ref, out_ref.at[pl.ds(0, BLK), pl.ds(i * FEAT, FEAT)], sems.at[i]
        )
        for i, ref in enumerate((tok_ref, cot_ref))
    ]
    for copy in copies:
        copy.start()
    count = jnp.full((PAD - BLK, 2 * FEAT), count_ref[0], jnp.int32)
    out_ref[BLK:, :] = count.astype(F32).astype(BF)
    for copy in copies:
        copy.wait()


def pack(tokens, cotangent, counts):
    return call(
        pack_kernel,
        "pack",
        0,
        1 << 19,
        out_shape=jax.ShapeDtypeStruct((PAD, 2 * FEAT), BF),
        in_specs=[pl.BlockSpec(memory_space=pl.ANY)] * 2 + [smem()],
        out_specs=pl.BlockSpec(memory_space=pltpu.VMEM),
        scratch_shapes=[pltpu.SemaphoreType.DMA((2,))],
    )(tokens, cotangent, counts)


def prepare_kernel(gm, um, dm, wg, wu, wd, wx_ref, wdt_ref, wd_ref):
    j = pl.program_id(0)
    for which, (mask, ref) in enumerate(((gm, wg), (um, wu))):
        for r in range(4):
            for b in range(2):
                at = slice(r * BLK, (r + 1) * BLK)
                wx_ref[0, at, which * PAIR + b * BLK : which * PAIR + (b + 1) * BLK] = kept(
                    mask, r, 2 * j + b, ref[at, b * BLK : (b + 1) * BLK]
                )
    down = jnp.concatenate(
        [
            jnp.concatenate(
                [
                    kept(dm, 2 * j + b, c, wd[b * BLK : (b + 1) * BLK, c * BLK : (c + 1) * BLK])
                    for c in range(4)
                ],
                axis=1,
            )
            for b in range(2)
        ],
        axis=0,
    )
    wd_ref[...] = down
    wdt_ref[0] = down.T


def prepare(gm, um, dm, wg, wu, wd):
    return call(
        prepare_kernel,
        "prepare",
        0,
        13 << 20,
        grid=(STEPS,),
        out_shape=(
            jax.ShapeDtypeStruct((STEPS, FEAT, 2 * PAIR), BF),
            jax.ShapeDtypeStruct((STEPS, FEAT, PAIR), BF),
            jax.ShapeDtypeStruct((UNITS, FEAT), BF),
        ),
        in_specs=[
            smem(),
            smem(),
            smem(),
            pl.BlockSpec((FEAT, PAIR), lambda j: (0, j)),
            pl.BlockSpec((FEAT, PAIR), lambda j: (0, j)),
            pl.BlockSpec((PAIR, FEAT), lambda j: (j, 0)),
        ],
        out_specs=(
            pl.BlockSpec((1, FEAT, 2 * PAIR), lambda j: (j, 0, 0)),
            pl.BlockSpec((1, FEAT, PAIR), lambda j: (j, 0, 0)),
            pl.BlockSpec((PAIR, FEAT), lambda j: (j, 0)),
        ),
    )(gm, um, dm, wg, wu, wd)


def compact_kernel(shard, rows_ref, *refs):
    sources, (x_ref, g_ref, offs_ref, cnts_ref) = refs[:8], refs[8:]
    rows = rows_ref[...]
    slot = lax.broadcasted_iota(jnp.int32, (LIVE, BLK), 1)
    cnts = [ref[BLK : BLK + 1, 0:1].astype(F32).astype(jnp.int32) for ref in sources]
    total = None
    for pair in range(4):
        picks = []
        for k in (2 * pair, 2 * pair + 1):
            offset = jnp.zeros((1, 1), jnp.int32)
            for other in range(8):
                if other != k:
                    offset += jnp.where(shard[other] < shard[k], cnts[other], 0)
            offs_ref[k] = jnp.broadcast_to(offset, (8, BLK))
            cnts_ref[k] = jnp.broadcast_to(cnts[k], (8, BLK))
            hit = (rows - offset == slot) & (slot < cnts[k])
            picks.append(jnp.where(hit, 1.0, 0.0).astype(BF))
        source = jnp.concatenate(
            [sources[2 * pair][:BLK, :], sources[2 * pair + 1][:BLK, :]], axis=0
        )
        part = jnp.dot(jnp.concatenate(picks, axis=1), source, preferred_element_type=F32)
        total = part if total is None else total + part
    x_ref[...] = total[:, :FEAT].astype(BF)
    g_ref[...] = total[:, FEAT:].astype(BF)


def compact(shard, rows, sources):
    vmem = pl.BlockSpec(memory_space=pltpu.VMEM)
    return call(
        compact_kernel,
        "compact",
        2 * LIVE * SLOTS * SLOTS,
        5 << 20,
        out_shape=(
            jax.ShapeDtypeStruct((LIVE, FEAT), BF),
            jax.ShapeDtypeStruct((LIVE, FEAT), BF),
            jax.ShapeDtypeStruct((8, 8, BLK), jnp.int32),
            jax.ShapeDtypeStruct((8, 8, BLK), jnp.int32),
        ),
        in_specs=[smem(), vmem] + [vmem] * 8,
        out_specs=(vmem,) * 4,
    )(shard, rows, *sources)


ORDERS = ((0, 1, 2, 3), (0, 2, 1, 3))


def turn_kernel(x_ref, *outs):
    for order, out in zip(ORDERS, outs):
        rows = [x_ref[p * CUT : (p + 1) * CUT, :] for p in order]
        out[...] = jnp.concatenate(rows, axis=0).astype(F32).T.astype(BF)


def turned(x):
    return call(
        turn_kernel,
        "turned",
        1,
        1 << 12,
        out_shape=(jax.ShapeDtypeStruct((FEAT, LIVE), BF),) * 2,
        in_specs=[vmem()],
        out_specs=(vmem(),) * 2,
    )(x)


def partial_kernel(start, pieces, x_ref, g_ref, wx_ref, wdt_ref, *outs):
    count = pieces * CUT
    x, g = x_ref[start : start + count, :], g_ref[start : start + count, :]
    for j in range(STEPS):
        both = jnp.dot(x, wx_ref[j], preferred_element_type=F32)
        back = jnp.dot(g, wdt_ref[j], preferred_element_type=F32)
        for which, result in enumerate((both[:, :PAIR], both[:, PAIR:], back)):
            for piece in range(pieces):
                for q in SIDES:
                    outs[piece * 2 + q][which, :, block(j, BLK)] = result[
                        block(piece, CUT), block(q, BLK)
                    ].astype(BF)


def partials(start, pieces, x, g, wx, wdt):
    count = pieces * CUT
    return call(
        functools.partial(partial_kernel, start, pieces),
        "partials",
        2 * count * FEAT * 3 * UNITS,
        7 << 20,
        out_shape=(jax.ShapeDtypeStruct((3, CUT, HALF), BF),) * (2 * pieces),
        in_specs=[vmem()] * 4,
        out_specs=(vmem(),) * (2 * pieces),
    )(x, g, wx, wdt)


def picked(rows, offs, cnts, k, slot):
    hit = (rows - offs[k, 0:1, 0:1] == slot) & (slot < cnts[k, 0:1, 0:1])
    return jnp.where(hit, 1.0, 0.0).astype(BF)


def products(lower, upper, shared, w_down):
    both, single = (lower, upper) if shared == 0 else (upper, lower)
    result = [
        jnp.dot(jnp.concatenate(both, axis=1), w_down, preferred_element_type=F32)
    ]
    for q in SIDES:
        result.append(
            jnp.dot(single[q], w_down[q * BLK : (q + 1) * BLK, :], preferred_element_type=F32)
        )
    return result


def first_output_kernel(wd_ref, own0, own1, total):
    for j in range(STEPS):
        by = block(j, BLK)
        lower = [ref[0, :CUT, by] for ref in (own0, own1)]
        upper = [ref[0, CUT:, by] for ref in (own0, own1)]
        results = products(lower, upper, 0, wd_ref[block(j, PAIR), :])
        for i in range(3):
            if j == 0:
                total[i] = results[i]
            else:
                total[i] += results[i]


def first_output(wd, hidden_own):
    return call(
        first_output_kernel,
        "first_output",
        1,
        1 << 12,
        out_shape=jax.ShapeDtypeStruct((3, CUT, FEAT), F32),
        in_specs=[vmem()] * 3,
        out_specs=vmem(),
    )(wd, *hidden_own)


def last_output_kernel(rows_ref, offs, cnts, early_ref, wd_ref, come0, come1, near_ref, away_ref):
    totals = None
    for j in range(STEPS):
        by = slice(j * BLK, (j + 1) * BLK)
        lower = [ref[0, :CUT, by] for ref in (come0, come1)]
        upper = [ref[0, CUT:, by] for ref in (come0, come1)]
        results = products(lower, upper, 1, wd_ref[j * PAIR : (j + 1) * PAIR, :])
        totals = results if j == 0 else [a + b for a, b in zip(totals, results)]
    pieces = (early_ref[0], early_ref[1] + totals[2], early_ref[2] + totals[1], totals[0])
    mixed = jnp.concatenate([piece.astype(BF) for piece in pieces], axis=0)
    rows = rows_ref[0:1, :]
    slot = lax.broadcasted_iota(jnp.int32, (BLK, LIVE), 0)
    for k in range(8):
        pick = picked(rows, offs, cnts, k, slot)
        target = near_ref if k < 4 else away_ref
        target[k % 4] = jnp.dot(pick, mixed, preferred_element_type=F32).astype(BF)


def last_output(rows, offs, cnts, early, wd, hidden_come):
    return call(
        last_output_kernel,
        "last_output",
        1,
        1 << 12,
        grid=(1,),
        out_shape=(jax.ShapeDtypeStruct((4, BLK, FEAT), BF),) * 2,
        in_specs=[
            whole((1, LIVE)),
            whole((8, 8, BLK)),
            whole((8, 8, BLK)),
            whole((3, CUT, FEAT)),
            whole((UNITS, FEAT)),
        ]
        + [whole((1, 2 * CUT, HALF))] * 2,
        out_specs=(whole((4, BLK, FEAT)),) * 2,
    )(rows, offs, cnts, early, wd, *hidden_come)


def store(block_of, scratch, outs, sems):
    copies = []
    for j in range(STEPS):
        places = block_of(j, [ref.at[j] for ref in scratch])
        for i, (ref, out, place) in enumerate(zip(scratch, outs, places)):
            copy = pltpu.make_async_copy(ref.at[j], out.at[place], sems.at[i, j])
            copy.start()
            copies.append(copy)
    for copy in copies:
        copy.wait()


def down_kernel(dm, g_ref, own0, own1, come0, come1, out, scratch, sems):
    def block_of(j, targets):
        by = block(j, BLK)
        left = jnp.concatenate([own0[0, :, by], come0[0, :, by]], axis=0)
        right = jnp.concatenate(
            [ref[0, block(i, CUT), by] for i in range(2) for ref in (own1, come1)], axis=0
        )
        down = lax.dot_general(
            jnp.concatenate([left, right], axis=1),
            g_ref[...],
            (((0,), (0,)), ((), ())),
            preferred_element_type=F32,
        )
        for r in range(4):
            for b in range(2):
                at, to = block(r, BLK), block(b, BLK)
                targets[0][to, at] = kept(dm, 2 * j + b, r, down[to, at])
        return [(pl.ds(j * PAIR, PAIR), pl.ds(0, FEAT))]

    store(block_of, [scratch], [out], sems)


def down_gradient(dm, g, parts):
    return call(
        down_kernel,
        "down_gradient",
        1,
        1 << 12,
        out_shape=jax.ShapeDtypeStruct((UNITS, FEAT), F32),
        in_specs=[smem()] + [vmem()] * 5,
        out_specs=pl.BlockSpec(memory_space=pl.ANY),
        scratch_shapes=[
            pltpu.VMEM((STEPS, PAIR, FEAT), F32),
            pltpu.SemaphoreType.DMA((1, STEPS)),
        ],
    )(dm, g, *parts)


def plane_products(turns, parts, at, by):
    return [
        jnp.dot(
            turn[:, at : at + 2 * CUT],
            jnp.concatenate([part[0, :, by], part[1, :, by]], axis=1),
            preferred_element_type=F32,
        )
        for turn, part in zip(turns, parts)
    ]


def first_grad_kernel(xt0, xt1, own0, own1, gate_out, up_out):
    for j in range(STEPS):
        sums = plane_products((xt0, xt1), (own0, own1), 0, block(j, BLK))
        for q, both in enumerate(sums):
            to = block(2 * j + q, BLK)
            gate_out[:, to] = both[:, :BLK]
            up_out[:, to] = both[:, BLK:]


def first_grad(turns, derived_own):
    return call(
        first_grad_kernel,
        "first_grad",
        2 * LIVE * FEAT * UNITS,
        13 << 20,
        out_shape=(jax.ShapeDtypeStruct((FEAT, UNITS), F32),) * 2,
        in_specs=[vmem()] * 4,
        out_specs=(vmem(),) * 2,
    )(*turns, *derived_own)


def last_grad_kernel(
    gm, um, xt0, xt1, gate_in, up_in, come0, come1, gate_out, up_out, gate_part, up_part, sems
):
    def block_of(j, targets):
        sums = plane_products((xt0, xt1), (come0, come1), 2 * CUT, block(j, BLK))
        for q, both in enumerate(sums):
            of, to = block(2 * j + q, BLK), block(q, BLK)
            for r in range(4):
                at = block(r, BLK)
                targets[0][at, to] = kept(gm, r, 2 * j + q, gate_in[at, of] + both[at, :BLK])
                targets[1][at, to] = kept(um, r, 2 * j + q, up_in[at, of] + both[at, BLK:])
        return [(pl.ds(0, FEAT), pl.ds(j * PAIR, PAIR))] * 2

    store(block_of, [gate_part, up_part], [gate_out, up_out], sems)


def last_grad(gm, um, turns, begun, derived_come):
    return call(
        last_grad_kernel,
        "last_grad",
        2 * LIVE * FEAT * UNITS,
        13 << 20,
        out_shape=(jax.ShapeDtypeStruct((FEAT, UNITS), F32),) * 2,
        in_specs=[smem()] * 2 + [vmem()] * 6,
        out_specs=(pl.BlockSpec(memory_space=pl.ANY),) * 2,
        scratch_shapes=[pltpu.VMEM((STEPS, FEAT, PAIR), F32)] * 2
        + [pltpu.SemaphoreType.DMA((2, STEPS))],
    )(gm, um, *turns, *begun, *derived_come)


def split(value, axis):
    lower = lax.slice_in_dim(value, 0, 1, axis=axis)
    upper = lax.slice_in_dim(value, 1, 2, axis=axis)
    return lower, upper


def activate(total):
    gate, upward, back = total[0], total[1], total[2]
    sigma = jax.nn.sigmoid(gate)
    active = gate * sigma
    hidden = (active * upward).astype(BF)
    d_gate = (back * upward * sigma * (1.0 + gate * (1.0 - sigma))).astype(BF)
    d_up = (back * active).astype(BF)
    return jnp.stack([d_gate, d_up, hidden])


def exchange(values, number):
    return [
        lax.ppermute(values[q], ("col", "dp"), partners(ROUNDS[q][number][1])) for q in SIDES
    ]


def on_device(
    tokens, cotangent, gate_weight, up_weight, down_weight, gate_mask, up_mask, down_mask, counts
):
    live = (lax.iota(jnp.int32, tokens.shape[0]) < counts[0])[:, None]
    place = lax.axis_index("col")
    order = jnp.arange(8)
    shard = ((place // 2 + order % 4) % SIDE) * 2 + ((place % 2) ^ (order // 4))
    own = pack(tokens, cotangent, counts)
    column = [own] + [lax.ppermute(own, "col", shift(-dz, 0)) for dz in (1, 2, 3)]
    beside = [lax.ppermute(own, "col", shift(0, 1))]
    wx, wdt, wd = prepare(gate_mask, up_mask, down_mask, gate_weight, up_weight, down_weight)
    rows = logical_rows()
    column[1], column[3], wx, wdt, wd, rows_down, rows_along, shard = lax.optimization_barrier(
        (column[1], column[3], wx, wdt, wd, rows[:, None], rows[None, :], shard)
    )
    beside += [lax.ppermute(value, "col", shift(0, 1)) for value in column[1:]]
    x, g, offs, cnts = compact(shard, rows_down, column + beside)

    early = partials(FIRST, 1, x, g, wx, wdt)
    come_early = exchange(early, 0)
    x_rest, g_rest, *_ = lax.optimization_barrier((x, g, *early))
    late = partials(0, 3, x_rest, g_rest, wx, wdt)
    zero = [late[q] for q in SIDES]
    side = [[late[2 * (2 - ROUNDS[q][n][0]) + q] for q in SIDES] for n in range(2)]
    come_rest = exchange(side[0], 0)
    turns = turned(x_rest)
    *come_early, turn0, turn1 = lax.optimization_barrier((*come_early, *turns))
    second = [
        (side[1][q].astype(F32) + come_early[q].astype(F32)).astype(BF) for q in SIDES
    ]
    come_second = exchange(second, 1)
    *come_rest, last0, last1 = lax.optimization_barrier((*come_rest, *come_second))
    come_second = [last0, last1]
    keep, send = [None] * 2, [None] * 2
    for q in SIDES:
        total = (
            zero[q].astype(F32) + come_rest[q].astype(F32) + come_second[q].astype(F32)
        ).reshape(3, 2, 2, 48, HALF)
        keep[q], upper = split(total, ROUNDS[q][2][0] - 1)
        send[q] = upper.astype(BF)
    come = exchange(send, 2)
    keep = [(keep[q] + come[q].astype(F32)).astype(BF) for q in SIDES]
    come = exchange(keep, 3)
    held = []
    for q in SIDES:
        axis = ROUNDS[q][3][0] - 1
        lower, upper = split(come[q], axis)
        arrived = jnp.concatenate([upper, lower], axis=axis)
        held.append(activate(keep[q].astype(F32) + arrived.astype(F32)))
    come = exchange(held, 2)
    held = [
        jnp.concatenate([held[q], come[q]], axis=ROUNDS[q][2][0] - 1).reshape(3, CUT, HALF)
        for q in SIDES
    ]
    near = exchange(held, 1)
    hidden_own = [jnp.concatenate([held[q][2:], near[q][2:]], axis=1) for q in SIDES]
    derived_own = [jnp.concatenate([held[q][:2], near[q][:2]], axis=1) for q in SIDES]
    hidden_come = exchange(hidden_own, 0)
    derived_come = exchange(derived_own, 0)

    begun = first_output(wd, hidden_own)
    grads_begun = first_grad((turn0, turn1), derived_own)
    begun, *grads_begun = lax.optimization_barrier((begun, *grads_begun))
    mine, away = last_output(rows_along, offs, cnts, begun, wd, hidden_come)
    other = lax.ppermute(away, "col", shift(0, 1))
    down_grad = down_gradient(down_mask, g, hidden_own + hidden_come)
    other, down_grad = lax.optimization_barrier((other, down_grad))
    summed = mine.astype(F32) + other.astype(F32)
    terms = [summed[k].astype(BF) for k in range(4)]
    arrived = [lax.ppermute(terms[dz], "col", shift(dz, 0)) for dz in (1, 2, 3)]
    gate_grad, up_grad = last_grad(
        gate_mask, up_mask, (turn0, turn1), grads_begun, derived_come
    )
    *arrived, gate_grad, up_grad = lax.optimization_barrier((*arrived, gate_grad, up_grad))
    mixed = sum((term.astype(F32) for term in arrived), terms[0].astype(F32))
    output = jnp.where(live, mixed, jnp.zeros_like(mixed)).astype(BF)
    return (output, gate_grad, up_grad, down_grad)


def solution(mesh):
    in_specs = (
        P("col", "dp"),
        P("col", "dp"),
        P("dp", "col"),
        P("dp", "col"),
        P("col", "dp"),
        P("dp", "col"),
        P("dp", "col"),
        P("col", "dp"),
        P("col"),
    )
    out_specs = (P("col", "dp"), P("dp", "col"), P("dp", "col"), P("col", "dp"))
    return jax.shard_map(
        on_device, mesh=mesh, in_specs=in_specs, out_specs=out_specs, check_vma=False
    )
```

```python
import functools

import jax
import jax.numpy as jnp
from jax import lax
from jax.experimental import pallas as pl
from jax.experimental.pallas import tpu as pltpu
from jax.sharding import PartitionSpec as P

BF = jnp.bfloat16
F32 = jnp.float32
LIVE = 768
PAD = 144
SIDE = 4
BLK = 128
PAIR = 2 * BLK
UNITS = 1792
HALF = UNITS // 2
STEPS = UNITS // PAIR
FEAT = 512
SLOTS = 1024
CUT = 192
FIRST = 576
LAST = LIVE - FIRST
VMEM = 32 << 20

MASKS = {"xA": (1, 0), "xB": (3, 0), "yA": (0, 1), "yB": (0, 3)}
ROUNDS = (
    ((0, ("xA", "yA")), (1, ("xB", "yB")), (2, ("yA", "xA")), (3, ("yB", "xB"))),
    ((1, ("xB", "yB")), (0, ("xA", "yA")), (3, ("yB", "xB")), (2, ("yA", "xA"))),
)
SIDES = (0, 1)


def partners(names):
    pairs = []
    for col in range(2 * SIDE):
        dx, dy = MASKS[names[col % 2]]
        for x in range(SIDE):
            for y in range(SIDE):
                start = (col * SIDE + x) * SIDE + y
                pairs.append((start, (col * SIDE + (x ^ dx)) * SIDE + (y ^ dy)))
    return pairs


def shift(dz, dc):
    return [
        (z * 2 + c, ((z + dz) % SIDE) * 2 + (c + dc) % 2) for z in range(SIDE) for c in range(2)
    ]


def logical_rows():
    place = lax.axis_index("dp")
    x, y = place // SIDE, place % SIDE

    def sides(v):
        high = v // 2
        return (v % 2) ^ high, high

    xa, xb = sides(x)
    ya, yb = sides(y)
    first = xa * 8 + xb * 4 + ya * 2 + yb
    second = ya * 8 + yb * 4 + xa * 2 + xb
    mask = jnp.where(lax.axis_index("col") % 2 > 0, second, first)
    row = lax.iota(jnp.int32, LIVE)
    return ((row // 48) ^ mask) * 48 + row % 48


def kept(mask_ref, row, col, value):
    return jnp.where(mask_ref[row, col] > 0, value, jnp.zeros_like(value))


def smem():
    return pl.BlockSpec(memory_space=pltpu.SMEM)


def whole(shape):
    return pl.BlockSpec(shape, lambda j: (0,) * len(shape))


def vmem():
    return pl.BlockSpec(memory_space=pltpu.VMEM)


def block(j, size):
    return slice(j * size, (j + 1) * size)


def call(kernel, name, flops, moved, **rest):
    return pl.pallas_call(
        kernel,
        compiler_params=pltpu.CompilerParams(vmem_limit_bytes=VMEM),
        cost_estimate=pl.CostEstimate(flops=flops, bytes_accessed=moved, transcendentals=0),
        name=name,
        **rest,
    )


def pack_kernel(tok_ref, cot_ref, count_ref, out_ref, sems):
    copies = [
        pltpu.make_async_copy(
            ref, out_ref.at[pl.ds(0, BLK), pl.ds(i * FEAT, FEAT)], sems.at[i]
        )
        for i, ref in enumerate((tok_ref, cot_ref))
    ]
    for copy in copies:
        copy.start()
    count = jnp.full((PAD - BLK, 2 * FEAT), count_ref[0], jnp.int32)
    out_ref[BLK:, :] = count.astype(F32).astype(BF)
    for copy in copies:
        copy.wait()


def pack(tokens, cotangent, counts):
    return call(
        pack_kernel,
        "pack",
        0,
        1 << 19,
        out_shape=jax.ShapeDtypeStruct((PAD, 2 * FEAT), BF),
        in_specs=[pl.BlockSpec(memory_space=pl.ANY)] * 2 + [smem()],
        out_specs=pl.BlockSpec(memory_space=pltpu.VMEM),
        scratch_shapes=[pltpu.SemaphoreType.DMA((2,))],
    )(tokens, cotangent, counts)


def prepare_kernel(gm, um, dm, wg, wu, wd, wx_ref, wdt_ref, wd_ref):
    j = pl.program_id(0)
    for which, (mask, ref) in enumerate(((gm, wg), (um, wu))):
        for r in range(4):
            for b in range(2):
                at = slice(r * BLK, (r + 1) * BLK)
                wx_ref[0, at, which * PAIR + b * BLK : which * PAIR + (b + 1) * BLK] = kept(
                    mask, r, 2 * j + b, ref[at, b * BLK : (b + 1) * BLK]
                )
    down = jnp.concatenate(
        [
            jnp.concatenate(
                [
                    kept(dm, 2 * j + b, c, wd[b * BLK : (b + 1) * BLK, c * BLK : (c + 1) * BLK])
                    for c in range(4)
                ],
                axis=1,
            )
            for b in range(2)
        ],
        axis=0,
    )
    wd_ref[...] = down
    wdt_ref[0] = down.T


def prepare(gm, um, dm, wg, wu, wd):
    return call(
        prepare_kernel,
        "prepare",
        0,
        13 << 20,
        grid=(STEPS,),
        out_shape=(
            jax.ShapeDtypeStruct((STEPS, FEAT, 2 * PAIR), BF),
            jax.ShapeDtypeStruct((STEPS, FEAT, PAIR), BF),
            jax.ShapeDtypeStruct((UNITS, FEAT), BF),
        ),
        in_specs=[
            smem(),
            smem(),
            smem(),
            pl.BlockSpec((FEAT, PAIR), lambda j: (0, j)),
            pl.BlockSpec((FEAT, PAIR), lambda j: (0, j)),
            pl.BlockSpec((PAIR, FEAT), lambda j: (j, 0)),
        ],
        out_specs=(
            pl.BlockSpec((1, FEAT, 2 * PAIR), lambda j: (j, 0, 0)),
            pl.BlockSpec((1, FEAT, PAIR), lambda j: (j, 0, 0)),
            pl.BlockSpec((PAIR, FEAT), lambda j: (j, 0)),
        ),
    )(gm, um, dm, wg, wu, wd)


def compact_kernel(shard, rows_ref, *refs):
    sources, (x_ref, g_ref, offs_ref, cnts_ref) = refs[:8], refs[8:]
    rows = rows_ref[...]
    slot = lax.broadcasted_iota(jnp.int32, (LIVE, BLK), 1)
    cnts = [ref[BLK : BLK + 1, 0:1].astype(F32).astype(jnp.int32) for ref in sources]
    picks = []
    for k in range(8):
        offset = jnp.zeros((1, 1), jnp.int32)
        for other in range(8):
            if other != k:
                offset += jnp.where(shard[other] < shard[k], cnts[other], 0)
        offs_ref[k] = jnp.broadcast_to(offset, (8, BLK))
        cnts_ref[k] = jnp.broadcast_to(cnts[k], (8, BLK))
        hit = (rows - offset == slot) & (slot < cnts[k])
        picks.append(jnp.where(hit, 1.0, 0.0).astype(BF))
    source = jnp.concatenate([ref[:BLK, :] for ref in sources], axis=0)
    total = jnp.dot(jnp.concatenate(picks, axis=1), source, preferred_element_type=F32)
    x_ref[...] = total[:, :FEAT].astype(BF)
    g_ref[...] = total[:, FEAT:].astype(BF)


def compact(shard, rows, sources):
    vmem = pl.BlockSpec(memory_space=pltpu.VMEM)
    return call(
        compact_kernel,
        "compact",
        2 * LIVE * SLOTS * SLOTS,
        5 << 20,
        out_shape=(
            jax.ShapeDtypeStruct((LIVE, FEAT), BF),
            jax.ShapeDtypeStruct((LIVE, FEAT), BF),
            jax.ShapeDtypeStruct((8, 8, BLK), jnp.int32),
            jax.ShapeDtypeStruct((8, 8, BLK), jnp.int32),
        ),
        in_specs=[smem(), vmem] + [vmem] * 8,
        out_specs=(vmem,) * 4,
    )(shard, rows, *sources)


ORDERS = ((0, 1, 2, 3), (0, 2, 1, 3))


def turn_kernel(x_ref, *outs):
    for order, out in zip(ORDERS, outs):
        rows = [x_ref[p * CUT : (p + 1) * CUT, :] for p in order]
        out[...] = jnp.concatenate(rows, axis=0).astype(F32).T.astype(BF)


def turned(x):
    return call(
        turn_kernel,
        "turned",
        1,
        1 << 12,
        out_shape=(jax.ShapeDtypeStruct((FEAT, LIVE), BF),) * 2,
        in_specs=[vmem()],
        out_specs=(vmem(),) * 2,
    )(x)


def partial_kernel(start, pieces, x_ref, g_ref, wx_ref, wdt_ref, *outs):
    count = pieces * CUT
    x, g = x_ref[start : start + count, :], g_ref[start : start + count, :]
    for j in range(STEPS):
        both = jnp.dot(x, wx_ref[j], preferred_element_type=F32)
        back = jnp.dot(g, wdt_ref[j], preferred_element_type=F32)
        for which, result in enumerate((both[:, :PAIR], both[:, PAIR:], back)):
            for piece in range(pieces):
                for q in SIDES:
                    outs[piece * 2 + q][which, :, block(j, BLK)] = result[
                        block(piece, CUT), block(q, BLK)
                    ].astype(BF)


def partials(start, pieces, x, g, wx, wdt):
    count = pieces * CUT
    return call(
        functools.partial(partial_kernel, start, pieces),
        "partials",
        2 * count * FEAT * 3 * UNITS,
        7 << 20,
        out_shape=(jax.ShapeDtypeStruct((3, CUT, HALF), BF),) * (2 * pieces),
        in_specs=[vmem()] * 4,
        out_specs=(vmem(),) * (2 * pieces),
    )(x, g, wx, wdt)


def picked(rows, offs, cnts, k, slot):
    hit = (rows - offs[k, 0:1, 0:1] == slot) & (slot < cnts[k, 0:1, 0:1])
    return jnp.where(hit, 1.0, 0.0).astype(BF)


def products(lower, upper, shared, w_down):
    both, single = (lower, upper) if shared == 0 else (upper, lower)
    result = [
        jnp.dot(jnp.concatenate(both, axis=1), w_down, preferred_element_type=F32)
    ]
    for q in SIDES:
        result.append(
            jnp.dot(single[q], w_down[q * BLK : (q + 1) * BLK, :], preferred_element_type=F32)
        )
    return result


def first_output_kernel(wd_ref, own0, own1, total):
    for j in range(STEPS):
        by = block(j, BLK)
        lower = [ref[0, :CUT, by] for ref in (own0, own1)]
        upper = [ref[0, CUT:, by] for ref in (own0, own1)]
        results = products(lower, upper, 0, wd_ref[block(j, PAIR), :])
        for i in range(3):
            if j == 0:
                total[i] = results[i]
            else:
                total[i] += results[i]


def first_output(wd, hidden_own):
    return call(
        first_output_kernel,
        "first_output",
        1,
        1 << 12,
        out_shape=jax.ShapeDtypeStruct((3, CUT, FEAT), F32),
        in_specs=[vmem()] * 3,
        out_specs=vmem(),
    )(wd, *hidden_own)


def last_output_kernel(rows_ref, offs, cnts, early_ref, wd_ref, come0, come1, near_ref, away_ref):
    totals = None
    for j in range(STEPS):
        by = slice(j * BLK, (j + 1) * BLK)
        lower = [ref[0, :CUT, by] for ref in (come0, come1)]
        upper = [ref[0, CUT:, by] for ref in (come0, come1)]
        results = products(lower, upper, 1, wd_ref[j * PAIR : (j + 1) * PAIR, :])
        totals = results if j == 0 else [a + b for a, b in zip(totals, results)]
    pieces = (early_ref[0], early_ref[1] + totals[2], early_ref[2] + totals[1], totals[0])
    mixed = jnp.concatenate([piece.astype(BF) for piece in pieces], axis=0)
    rows = rows_ref[0:1, :]
    slot = lax.broadcasted_iota(jnp.int32, (BLK, LIVE), 0)
    for k in range(8):
        pick = picked(rows, offs, cnts, k, slot)
        target = near_ref if k < 4 else away_ref
        target[k % 4] = jnp.dot(pick, mixed, preferred_element_type=F32).astype(BF)


def last_output(rows, offs, cnts, early, wd, hidden_come):
    return call(
        last_output_kernel,
        "last_output",
        1,
        1 << 12,
        grid=(1,),
        out_shape=(jax.ShapeDtypeStruct((4, BLK, FEAT), BF),) * 2,
        in_specs=[
            whole((1, LIVE)),
            whole((8, 8, BLK)),
            whole((8, 8, BLK)),
            whole((3, CUT, FEAT)),
            whole((UNITS, FEAT)),
        ]
        + [whole((1, 2 * CUT, HALF))] * 2,
        out_specs=(whole((4, BLK, FEAT)),) * 2,
    )(rows, offs, cnts, early, wd, *hidden_come)


def store(block_of, scratch, outs, sems):
    copies = []
    for j in range(STEPS):
        places = block_of(j, [ref.at[j] for ref in scratch])
        for i, (ref, out, place) in enumerate(zip(scratch, outs, places)):
            copy = pltpu.make_async_copy(ref.at[j], out.at[place], sems.at[i, j])
            copy.start()
            copies.append(copy)
    for copy in copies:
        copy.wait()


def down_kernel(dm, g_ref, own0, own1, come0, come1, out, scratch, sems):
    def block_of(j, targets):
        by = block(j, BLK)
        left = jnp.concatenate([own0[0, :, by], come0[0, :, by]], axis=0)
        right = jnp.concatenate(
            [ref[0, block(i, CUT), by] for i in range(2) for ref in (own1, come1)], axis=0
        )
        down = lax.dot_general(
            jnp.concatenate([left, right], axis=1),
            g_ref[...],
            (((0,), (0,)), ((), ())),
            preferred_element_type=F32,
        )
        for r in range(4):
            for b in range(2):
                at, to = block(r, BLK), block(b, BLK)
                targets[0][to, at] = kept(dm, 2 * j + b, r, down[to, at])
        return [(pl.ds(j * PAIR, PAIR), pl.ds(0, FEAT))]

    store(block_of, [scratch], [out], sems)


def down_gradient(dm, g, parts):
    return call(
        down_kernel,
        "down_gradient",
        1,
        1 << 12,
        out_shape=jax.ShapeDtypeStruct((UNITS, FEAT), F32),
        in_specs=[smem()] + [vmem()] * 5,
        out_specs=pl.BlockSpec(memory_space=pl.ANY),
        scratch_shapes=[
            pltpu.VMEM((STEPS, PAIR, FEAT), F32),
            pltpu.SemaphoreType.DMA((1, STEPS)),
        ],
    )(dm, g, *parts)


def plane_products(turns, parts, at, by):
    return [
        jnp.dot(
            turn[:, at : at + 2 * CUT],
            jnp.concatenate([part[0, :, by], part[1, :, by]], axis=1),
            preferred_element_type=F32,
        )
        for turn, part in zip(turns, parts)
    ]


def first_grad_kernel(xt0, xt1, own0, own1, gate_out, up_out):
    for j in range(STEPS):
        sums = plane_products((xt0, xt1), (own0, own1), 0, block(j, BLK))
        for q, both in enumerate(sums):
            to = block(2 * j + q, BLK)
            gate_out[:, to] = both[:, :BLK]
            up_out[:, to] = both[:, BLK:]


def first_grad(turns, derived_own):
    return call(
        first_grad_kernel,
        "first_grad",
        2 * LIVE * FEAT * UNITS,
        13 << 20,
        out_shape=(jax.ShapeDtypeStruct((FEAT, UNITS), F32),) * 2,
        in_specs=[vmem()] * 4,
        out_specs=(vmem(),) * 2,
    )(*turns, *derived_own)


def last_grad_kernel(
    gm, um, xt0, xt1, gate_in, up_in, come0, come1, gate_out, up_out, gate_part, up_part, sems
):
    def block_of(j, targets):
        sums = plane_products((xt0, xt1), (come0, come1), 2 * CUT, block(j, BLK))
        for q, both in enumerate(sums):
            of, to = block(2 * j + q, BLK), block(q, BLK)
            for r in range(4):
                at = block(r, BLK)
                targets[0][at, to] = kept(gm, r, 2 * j + q, gate_in[at, of] + both[at, :BLK])
                targets[1][at, to] = kept(um, r, 2 * j + q, up_in[at, of] + both[at, BLK:])
        return [(pl.ds(0, FEAT), pl.ds(j * PAIR, PAIR))] * 2

    store(block_of, [gate_part, up_part], [gate_out, up_out], sems)


def last_grad(gm, um, turns, begun, derived_come):
    return call(
        last_grad_kernel,
        "last_grad",
        2 * LIVE * FEAT * UNITS,
        13 << 20,
        out_shape=(jax.ShapeDtypeStruct((FEAT, UNITS), F32),) * 2,
        in_specs=[smem()] * 2 + [vmem()] * 6,
        out_specs=(pl.BlockSpec(memory_space=pl.ANY),) * 2,
        scratch_shapes=[pltpu.VMEM((STEPS, FEAT, PAIR), F32)] * 2
        + [pltpu.SemaphoreType.DMA((2, STEPS))],
    )(gm, um, *turns, *begun, *derived_come)


def split(value, axis):
    lower = lax.slice_in_dim(value, 0, 1, axis=axis)
    upper = lax.slice_in_dim(value, 1, 2, axis=axis)
    return lower, upper


def activate(total):
    gate, upward, back = total[0], total[1], total[2]
    sigma = jax.nn.sigmoid(gate)
    active = gate * sigma
    hidden = (active * upward).astype(BF)
    d_gate = (back * upward * sigma * (1.0 + gate * (1.0 - sigma))).astype(BF)
    d_up = (back * active).astype(BF)
    return jnp.stack([d_gate, d_up, hidden])


def exchange(values, number):
    return [
        lax.ppermute(values[q], ("col", "dp"), partners(ROUNDS[q][number][1])) for q in SIDES
    ]


def on_device(
    tokens, cotangent, gate_weight, up_weight, down_weight, gate_mask, up_mask, down_mask, counts
):
    live = (lax.iota(jnp.int32, tokens.shape[0]) < counts[0])[:, None]
    place = lax.axis_index("col")
    order = jnp.arange(8)
    shard = ((place // 2 + order % 4) % SIDE) * 2 + ((place % 2) ^ (order // 4))
    own = pack(tokens, cotangent, counts)
    column = [own] + [lax.ppermute(own, "col", shift(-dz, 0)) for dz in (1, 2, 3)]
    beside = [lax.ppermute(own, "col", shift(0, 1))]
    wx, wdt, wd = prepare(gate_mask, up_mask, down_mask, gate_weight, up_weight, down_weight)
    rows = logical_rows()
    column[1], column[3], wx, wdt, wd, rows_down, rows_along, shard = lax.optimization_barrier(
        (column[1], column[3], wx, wdt, wd, rows[:, None], rows[None, :], shard)
    )
    beside += [lax.ppermute(value, "col", shift(0, 1)) for value in column[1:]]
    x, g, offs, cnts = compact(shard, rows_down, column + beside)

    early = partials(FIRST, 1, x, g, wx, wdt)
    come_early = exchange(early, 0)
    x_rest, g_rest, *_ = lax.optimization_barrier((x, g, *early))
    late = partials(0, 3, x_rest, g_rest, wx, wdt)
    zero = [late[q] for q in SIDES]
    side = [[late[2 * (2 - ROUNDS[q][n][0]) + q] for q in SIDES] for n in range(2)]
    come_rest = exchange(side[0], 0)
    turns = turned(x_rest)
    *come_early, turn0, turn1 = lax.optimization_barrier((*come_early, *turns))
    second = [
        (side[1][q].astype(F32) + come_early[q].astype(F32)).astype(BF) for q in SIDES
    ]
    come_second = exchange(second, 1)
    *come_rest, last0, last1 = lax.optimization_barrier((*come_rest, *come_second))
    come_second = [last0, last1]
    keep, send = [None] * 2, [None] * 2
    for q in SIDES:
        total = (
            zero[q].astype(F32) + come_rest[q].astype(F32) + come_second[q].astype(F32)
        ).reshape(3, 2, 2, 48, HALF)
        keep[q], upper = split(total, ROUNDS[q][2][0] - 1)
        send[q] = upper.astype(BF)
    come = exchange(send, 2)
    keep = [(keep[q] + come[q].astype(F32)).astype(BF) for q in SIDES]
    come = exchange(keep, 3)
    held = []
    for q in SIDES:
        axis = ROUNDS[q][3][0] - 1
        lower, upper = split(come[q], axis)
        arrived = jnp.concatenate([upper, lower], axis=axis)
        held.append(activate(keep[q].astype(F32) + arrived.astype(F32)))
    come = exchange(held, 2)
    held = [
        jnp.concatenate([held[q], come[q]], axis=ROUNDS[q][2][0] - 1).reshape(3, CUT, HALF)
        for q in SIDES
    ]
    near = exchange(held, 1)
    hidden_own = [jnp.concatenate([held[q][2:], near[q][2:]], axis=1) for q in SIDES]
    derived_own = [jnp.concatenate([held[q][:2], near[q][:2]], axis=1) for q in SIDES]
    hidden_come = exchange(hidden_own, 0)
    derived_come = exchange(derived_own, 0)

    begun = first_output(wd, hidden_own)
    grads_begun = first_grad((turn0, turn1), derived_own)
    begun, *grads_begun = lax.optimization_barrier((begun, *grads_begun))
    mine, away = last_output(rows_along, offs, cnts, begun, wd, hidden_come)
    other = lax.ppermute(away, "col", shift(0, 1))
    down_grad = down_gradient(down_mask, g, hidden_own + hidden_come)
    other, down_grad = lax.optimization_barrier((other, down_grad))
    summed = mine.astype(F32) + other.astype(F32)
    terms = [summed[k].astype(BF) for k in range(4)]
    arrived = [lax.ppermute(terms[dz], "col", shift(dz, 0)) for dz in (1, 2, 3)]
    gate_grad, up_grad = last_grad(
        gate_mask, up_mask, (turn0, turn1), grads_begun, derived_come
    )
    *arrived, gate_grad, up_grad = lax.optimization_barrier((*arrived, gate_grad, up_grad))
    mixed = sum((term.astype(F32) for term in arrived), terms[0].astype(F32))
    output = jnp.where(live, mixed, jnp.zeros_like(mixed)).astype(BF)
    return (output, gate_grad, up_grad, down_grad)


def solution(mesh):
    in_specs = (
        P("col", "dp"),
        P("col", "dp"),
        P("dp", "col"),
        P("dp", "col"),
        P("col", "dp"),
        P("dp", "col"),
        P("dp", "col"),
        P("col", "dp"),
        P("col"),
    )
    out_specs = (P("col", "dp"), P("dp", "col"), P("dp", "col"), P("col", "dp"))
    return jax.shard_map(
        on_device, mesh=mesh, in_specs=in_specs, out_specs=out_specs, check_vma=False
    )
```
